512 devices in a mesh: dp: 32 (over y, z_lo), mp: 16 (over x, z_hi, core).
Axes of the slice: x: 4, y: 4, z: 16 (z_hi: 2, z_lo: 8; z = z_hi * 8 + z_lo), core: 2. Of those that a mesh axis runs over, the one named last changes fastest.
Arguments:
- tokens: bfloat16 [4096, 6144], P('dp', 'mp'), as said below
- norm_gain: bfloat16 [6144], P('mp'), may hold values from 0.099609375 to 1.8984375
- attn_weights: bfloat16 [4, 6144, 4096], P(None, 'dp', 'mp'), as said below
- stored_grads: bfloat16 [4, 6144, 4096], P(None, 'dp', 'mp'), as said below
- cotangent: bfloat16 [4096, 6144], P('dp'), may hold values from -12 to 12
Outputs:
- input_grad: bfloat16 [4096, 6144], P('dp', 'mp')
The draws below stay inside these ranges and needn't reach their ends.
Inputs may be any that keep to these rules, and one draw needn't show every extreme that they name: `tokens`: Real-valued. `attn_weights`: Real-valued. `stored_grads`: Real-valued.
All inputs are finite; a program needn't handle non-finite values.
Results may differ from the reference program's by a relative error of at most 0.024.
Values may be sent and summed in bfloat16 or wider, within the bound.
A program may use at most 128 MiB of HBM per device.

```python
import math
import jax
import jax.numpy as jnp
from jax import lax

D = 6144
HD = 128
HEAD_DEV = 2
PATCHES = 128
HEADS = 32
TOKENS = 4096
N_DP = 32
N_MP = 16


def rise_norm(rise):
    if rise == 1.0:
        return 1.0
    return math.sqrt((rise * rise - 1.0) / (2.0 * math.log(rise)))


def spread_field(key, rows, cols, row_rise, col_rise):
    first_key, second_key, third_key = jax.random.split(key, 3)
    lift = math.log(10.0)
    row_place = jnp.arange(rows, dtype=jnp.float32) / max(rows - 1, 1)
    col_place = jnp.arange(cols, dtype=jnp.float32) / max(cols - 1, 1)
    row_scale = jnp.exp(jax.random.uniform(first_key, (rows, 1)) * lift) * jnp.power(row_rise, row_place)[:, None]
    col_scale = jnp.exp(jax.random.uniform(second_key, (1, cols)) * lift) * jnp.power(col_rise, col_place)[None, :]
    base = jax.random.truncated_normal(third_key, -4.0, 4.0, (rows, cols))
    whole = 21.5 * rise_norm(row_rise) * rise_norm(col_rise)
    return base * row_scale * col_scale / whole


def block_field(key, rows, cols):
    lift = math.log(10.0)
    field = spread_field(jax.random.fold_in(key, 0), rows, cols, 1.0 / 3.0, 1.0 / 3.0)
    row_blocks = jnp.exp(jax.random.uniform(jax.random.fold_in(key, 1), (N_DP,)) * lift)
    row_factor = jnp.repeat(row_blocks, rows // N_DP, total_repeat_length=rows)[:, None]
    head_blocks = jnp.exp(jax.random.uniform(jax.random.fold_in(key, 2), (HEADS,)) * lift)
    head_factor = jnp.repeat(head_blocks, HD, total_repeat_length=cols)[None, :]
    return field * row_factor * head_factor / 21.5


def draw_tokens(key, part):
    key = jax.random.fold_in(key, 1)
    field = spread_field(key, TOKENS, D, 3.0, 3.0)
    offset = jax.random.truncated_normal(jax.random.fold_in(key, 5), -4.0, 4.0, (TOKENS, 1)) * 0.5
    return (field + offset).astype(jnp.bfloat16)


def draw_attn_weights(key, part):
    key = jax.random.fold_in(key, 2)
    blocks = []
    for index in range(4):
        factor = D ** (-0.5) if index < 3 else (HEADS * HD) ** (-0.5)
        blocks.append(spread_field(jax.random.fold_in(key, 10 + index), D, HEADS * HD, 3.0, 3.0) * factor)
    return jnp.stack(blocks).astype(jnp.bfloat16)


def draw_stored_grads(key, part):
    key = jax.random.fold_in(key, 3)
    factor = 1.0
    blocks = []
    for index in range(4):
        blocks.append(block_field(jax.random.fold_in(key, 30 + index), D, HEADS * HD) * factor)
    return jnp.stack(blocks).astype(jnp.bfloat16)


def block_levels(rng, extent, pieces, smallest, largest):
    level = 1.0
    for position, parts in pieces:
        draws = jax.random.uniform(jax.random.fold_in(jax.random.fold_in(rng, 6), position), (parts,), jnp.float32, smallest / len(pieces), largest / len(pieces))
        level = level * jnp.repeat(jnp.exp(draws), extent[position] // parts).reshape((-1,) + (1,) * (len(extent) - 1 - position))
    return level


def scatter_about(rng, shape, spread, limit, shards=(), kind=jnp.bfloat16):
    drawn = spread * jax.random.normal(rng, shape, jnp.float32)
    if shards:
        drawn = drawn * block_levels(rng, shape, shards, -0.22, 0.18)
    return jnp.clip(drawn, -limit, limit).astype(kind)


def setup_inputs(seed: int = 0) -> dict:
    seeds = jax.random.split(jax.random.key(seed), 6)
    tokens = draw_tokens(jax.random.fold_in(seeds[5], 71), 0)
    norm_gain = jnp.clip(1.0 + 0.18 * jax.random.normal(seeds[1], (D,), jnp.float32), 0.099609375, 1.8984375).astype(jnp.bfloat16)
    attn_weights = draw_attn_weights(jax.random.fold_in(seeds[5], 71), 0)
    stored_grads = draw_stored_grads(jax.random.fold_in(seeds[5], 71), 0)
    cotangent = scatter_about(seeds[4], (TOKENS, D), 2.0, 12.0, ((0, 32),))
    return {"tokens": tokens, "norm_gain": norm_gain, "attn_weights": attn_weights, "stored_grads": stored_grads, "cotangent": cotangent}


ascent_radius = 0.15

def row_norm(matrix):
    center = matrix - lax.optimization_barrier(jnp.mean(matrix, axis=-1, keepdims=True))
    inverse = lax.rsqrt(lax.optimization_barrier(jnp.mean(center * center, axis=-1, keepdims=True)) + 1e-06)
    return (center * inverse, inverse)

def row_norm_back(upstream, normed, inverse):
    first_mean = lax.optimization_barrier(jnp.mean(upstream, axis=-1, keepdims=True))
    second_mean = lax.optimization_barrier(jnp.mean(upstream * normed, axis=-1, keepdims=True))
    return (upstream - first_mean - normed * second_mean) * inverse

def head_group(normed_in, cotangent, group_cols, images):
    tokens_here = normed_in.shape[0]
    width = group_cols.shape[2]
    head_count = width // HD
    head_shape = (images, PATCHES, head_count, HD)
    score_scale = HD ** (-0.5)
    projected = jnp.einsum('td,mde->mte', normed_in.astype(jnp.float32), group_cols[:3].astype(jnp.float32))
    q_hat, q_inv = row_norm(projected[0].reshape(head_shape))
    k_hat, k_inv = row_norm(projected[1].reshape(head_shape))
    queries = q_hat.astype(jnp.bfloat16)
    key_rows = k_hat.astype(jnp.bfloat16)
    value_rows = projected[2].reshape(head_shape).astype(jnp.bfloat16)
    scores = jnp.einsum('bqhe,bkhe->bhqk', queries.astype(jnp.float32), key_rows.astype(jnp.float32)) * score_scale
    exps = jnp.exp(scores)
    probabilities = exps / lax.optimization_barrier(jnp.sum(exps, axis=-1, keepdims=True))
    grad_attn = jnp.dot(cotangent, group_cols[3], preferred_element_type=jnp.float32).astype(jnp.bfloat16)
    grad_attn = grad_attn.reshape(head_shape)
    probs_low = probabilities.astype(jnp.bfloat16)
    grad_values = jnp.einsum('bhqk,bqhe->bkhe', probs_low.astype(jnp.float32), grad_attn.astype(jnp.float32))
    grad_probs = jnp.einsum('bqhe,bkhe->bhqk', grad_attn.astype(jnp.float32), value_rows.astype(jnp.float32))
    inner = lax.optimization_barrier(jnp.sum(probabilities * grad_probs, axis=-1, keepdims=True))
    grad_scores = (probabilities * (grad_probs - inner) * score_scale).astype(jnp.bfloat16)
    grad_query = jnp.einsum('bhqk,bkhe->bqhe', grad_scores.astype(jnp.float32), key_rows.astype(jnp.float32))
    grad_keys = jnp.einsum('bhqk,bqhe->bkhe', grad_scores.astype(jnp.float32), queries.astype(jnp.float32))
    grad_q = row_norm_back(grad_query, q_hat, q_inv).astype(jnp.bfloat16).reshape(tokens_here, width)
    grad_k = row_norm_back(grad_keys, k_hat, k_inv).astype(jnp.bfloat16).reshape(tokens_here, width)
    grad_v = grad_values.astype(jnp.bfloat16).reshape(tokens_here, width)
    stacked = jnp.stack([grad_q, grad_k, grad_v])
    term = jnp.einsum('mte,mde->td', stacked.astype(jnp.float32), group_cols[:3].astype(jnp.float32))
    return term.astype(jnp.bfloat16)

def reference(tokens, norm_gain, attn_weights, stored_grads, cotangent):
    normed, inverse = row_norm(tokens.astype(jnp.float32))
    gain_row = norm_gain.astype(jnp.float32)[None, :]
    normed_in = (normed * gain_row).astype(jnp.bfloat16)
    weight_squares = lax.optimization_barrier(jnp.sum(jnp.square(attn_weights.astype(jnp.float32)), axis=(1, 2)))
    grad_squares = lax.optimization_barrier(jnp.sum(jnp.square(stored_grads.astype(jnp.float32)), axis=(1, 2)))
    ascent_ratio = ascent_radius * jnp.sqrt(weight_squares) / (jnp.sqrt(grad_squares) + 1e-12)
    shifted = (attn_weights.astype(jnp.float32) + ascent_ratio[:, None, None] * stored_grads.astype(jnp.float32)).astype(jnp.bfloat16)
    images = TOKENS // PATCHES
    width = HEAD_DEV * HD

    def accumulate(running, group_index):
        group_cols = lax.dynamic_slice_in_dim(shifted, group_index * width, width, 2)
        return (running + head_group(normed_in, cotangent, group_cols, images).astype(jnp.float32), None)
    running, _ = lax.scan(accumulate, jnp.zeros((TOKENS, D), jnp.float32), jnp.arange(N_MP, dtype=jnp.int32))
    upstream = running * gain_row
    return row_norm_back(upstream, normed, inverse).astype(jnp.bfloat16)
```

```python
import jax
import jax.numpy as jnp
from jax import lax
from jax.experimental import pallas as pl
from jax.experimental.pallas import tpu as pltpu
from jax.sharding import PartitionSpec as P

MESH = pl.DeviceIdType.MESH
F32, BF16 = jnp.float32, jnp.bfloat16
HD = 128
NX, NY, ZH, ZL, NC = 4, 4, 2, 8, 2
ascent_radius = 0.15


def mm(a, b):
    return lax.dot_general(a, b, (((1,), (0,)), ((), ())), preferred_element_type=F32)


def mm_nt(a, b):
    return lax.dot_general(a, b, (((1,), (1,)), ((), ())), preferred_element_type=F32)


def mm_tn(a, b):
    return lax.dot_general(a, b, (((0,), (0,)), ((), ())), preferred_element_type=F32)


def row_norm(matrix):
    center = matrix - jnp.mean(matrix, axis=-1, keepdims=True)
    inverse = lax.rsqrt(jnp.mean(center * center, axis=-1, keepdims=True) + 1e-06)
    return center * inverse, inverse


def row_norm_back(upstream, normed, inverse):
    first_mean = jnp.mean(upstream, axis=-1, keepdims=True)
    second_mean = jnp.mean(upstream * normed, axis=-1, keepdims=True)
    return (upstream - first_mean - normed * second_mean) * inverse


def columns_to_rows(first, second):
    lane = lax.broadcasted_iota(jnp.int32, (HD, HD), 1)
    both = jnp.where(lane == 0, first, jnp.where(lane == 1, second, 0.0))
    return both.T[0:8]


def rows_to_columns(first, second):
    sub = lax.broadcasted_iota(jnp.int32, (HD, HD), 0)
    both = jnp.where(sub == 0, first, jnp.where(sub == 1, second, 0.0))
    turned = both.T
    return turned[:, 0:1], turned[:, 1:2]


def kernel(
    tok, gain, w, g, cot, out,
    st_z, st_xc, st_y, rs, fin, nin, normed, invc, xc, wall, pf, pown, psend, precv, dbuf, tbuf, tr, sbuf, sr, ubuf, ur,
    st_s, st_r, xs, xr, cs, n3s, ws, wr, ps, pr, ds_, dr, tcs, tcr, ss, srs, us, urs,
):
    n_mp = NX * ZH * NC
    n_z = ZH * ZL
    width = tok.shape[1]
    band = ZH * NC * width
    n_feat = n_mp * width
    rows = w.shape[1]
    dp = lax.axis_index("dp")
    mp = lax.axis_index("mp")
    y, p = lax.div(dp, ZL), lax.rem(dp, ZL)
    x, c = lax.div(mp, ZH * NC), lax.rem(mp, NC)
    zh = lax.rem(lax.div(mp, NC), ZH)
    z = zh * ZL + p
    xcore = x * NC + c

    def dev(x_, y_, zh_, p_, c_):
        return (y_ * ZL + p_, (x_ * ZH + zh_) * NC + c_)

    def dev_z(k):
        return dev(x, y, lax.div(k, ZL), lax.rem(k, ZL), c)

    def dev_xc(k):
        return dev(lax.div(k, NC), y, zh, p, lax.rem(k, NC))

    def dev_y(k):
        return dev(x, k, zh, p, c)

    def dev_mp(k):
        return (dp, k)

    def remote(src, dst, ssem, rsem, device):
        return pltpu.make_async_remote_copy(
            src_ref=src, dst_ref=dst, send_sem=ssem, recv_sem=rsem, device_id=device, device_id_type=MESH
        )

    def others(n, mine, fn):
        def step(i, carry):
            fn(lax.rem(mine + i, n), i)
            return carry

        lax.fori_loop(1, n, step, 0)

    def share(buf, n, mine, dev_of, ssem, rsem):
        others(n, mine, lambda k, i: remote(buf.at[mine], buf.at[mine], ssem, rsem, dev_of(k)).start())

    def arrived(buf, n, sem):
        part = buf.at[pl.ds(0, n - 1)]
        pltpu.make_async_copy(part, part, sem).wait()

    barrier = pltpu.get_barrier_semaphore()

    def greet(device):
        pl.semaphore_signal(barrier, inc=1, device_id=device, device_id_type=MESH)

    others(n_mp, mp, lambda k, i: greet(dev_mp(k)))
    others(NY, y, lambda k, i: greet(dev_y(k)))

    def greet_z(k, i):
        @pl.when(lax.rem(k, ZL) != p)
        def _():
            greet(dev_z(k))

    others(n_z, z, greet_z)

    @pl.when(x != y)
    def _():
        for k in range(ZH):
            greet(dev(y, x, k, p, c))

    st_z[z] = jnp.zeros((16, HD), F32)
    for m in range(4):
        for base, ref in ((0, w), (8, g)):
            values = ref[m].astype(F32)
            sums = jnp.sum(values * values, axis=0, keepdims=True)
            st_z[z, base + m : base + m + 1] = sums[:, :HD] + sums[:, HD:]
    part = tok[...].astype(F32)
    part_mean = jnp.sum(part, axis=-1, keepdims=True) * (1.0 / width)
    part_square = jnp.sum(jnp.square(part - part_mean), axis=-1, keepdims=True)
    rs[mp] = columns_to_rows(part_mean, part_square)

    pl.semaphore_wait(barrier, (n_mp - 1) + (NY - 1) + (n_z - ZH) + jnp.where(x != y, ZH, 0))

    share(st_z, n_z, z, dev_z, st_s.at[0], st_r.at[0])
    share(rs, n_mp, mp, dev_mp, st_s.at[1], st_r.at[1])
    arrived(st_z, n_z, st_r.at[0])
    st_xc[xcore] = jnp.sum(st_z[...], axis=0)
    share(st_xc, NX * NC, xcore, dev_xc, st_s.at[2], st_r.at[2])

    arrived(rs, n_mp, st_r.at[1])
    means = rs[:, 0:1, :]
    mean = jnp.sum(means, axis=0) * (1.0 / n_mp)
    square = jnp.sum(rs[:, 1:2, :], axis=0) + width * jnp.sum(jnp.square(means - mean[None]), axis=0)
    inverse = lax.rsqrt(square * (1.0 / n_feat) + 1e-06)
    mean_col, inv_col = rows_to_columns(mean, inverse)
    normed[...] = (tok[...].astype(F32) - mean_col) * inv_col
    invc[...] = jnp.broadcast_to(inv_col, (HD, HD))
    nin[...] = (normed[...] * gain[...].astype(F32)).astype(BF16)

    for k in range(ZH):
        here = (x == y) & (zh == k)
        dst = xc.at[0, zh * NC + c, y]
        landed = xr.at[0, zh * NC + c, y]

        @pl.when(here)
        def _():
            pltpu.make_async_copy(nin, dst, landed).start()

        @pl.when(jnp.logical_not(here))
        def _():
            remote(nin, dst, xs.at[k], landed, dev(y, x, k, p, c)).start()

    arrived(st_xc, NX * NC, st_r.at[2])
    st_y[y] = jnp.sum(st_xc[...], axis=0)
    share(st_y, NY, y, dev_y, st_s.at[3], st_r.at[3])
    arrived(st_y, NY, st_r.at[3])
    total = jnp.sum(jnp.sum(st_y[...], axis=0), axis=-1, keepdims=True)
    ratio = ascent_radius * jnp.sqrt(total[0:8]) / (jnp.sqrt(total[8:16]) + 1e-12)
    for m in range(4):
        wall[m, p] = (w[m].astype(F32) + ratio[m : m + 1] * g[m].astype(F32)).astype(BF16)

    def weight_copy(way, m, s):
        return remote(
            wall.at[m, s], wall.at[m, s], ws.at[way, m, s], wr.at[m, s], dev(x, y, zh, p + 1 - 2 * way, c)
        )

    def send_weight(way, m, s):
        @pl.when(p < ZL - 1 if way == 0 else p > 0)
        def _():
            weight_copy(way, m, s).start()

    def send_own(ph):
        m = lax.rem(ph + 3, 4)
        send_weight(0, m, p)
        send_weight(1, m, p)

    send_own(0)

    for j in range(ZH * NC):
        pltpu.make_async_copy(
            cot.at[:, pl.ds(pl.multiple_of(y * band + j * width, HD), width)], xc.at[1, j, y], xr.at[1, j, y]
        ).start()

    def send_cot(k, i):
        for j in range(ZH * NC):
            remote(
                cot.at[:, pl.ds(pl.multiple_of(k * band + j * width, HD), width)],
                xc.at[1, j, y],
                cs.at[i, j],
                xr.at[1, j, y],
                dev_y(k),
            ).start()

    others(NY, y, send_cot)

    def wait_block(ref, sem):
        pltpu.make_async_copy(ref, ref, sem).wait()

    def send_tokens():
        for k in range(ZH):
            j = k * NC + c
            wait_block(xc.at[0, j, x], xr.at[0, j, x])
            others(
                NX * NC,
                xcore,
                lambda q, i: remote(
                    xc.at[0, j, x], xc.at[0, j, x], n3s.at[k, i], xr.at[0, j, x], dev_xc(q)
                ).start(),
            )

    def multiply(ph):
        m = lax.rem(ph + 3, 4)
        sel = jnp.where(ph == 0, 1, 0)

        @pl.when(ph < 2)
        def _():
            def wait_one(i, carry):
                j, tb = lax.div(i, NY), lax.rem(i, NY)

                @pl.when((ph == 0) | (lax.rem(j, NC) != c) | (tb != x))
                def _():
                    wait_block(xc.at[sel, j, tb], xr.at[sel, j, tb])

                return carry

            lax.fori_loop(0, ZH * NC * NY, wait_one, 0)

        columns = wall.shape[3]
        weights = wall[m].reshape(ZL * rows, columns)
        acc = None
        for j in range(ZH * NC):
            left = xc[sel, j].reshape(NY * HD, width)
            term = mm(left, weights[j * width : (j + 1) * width])
            acc = term if acc is None else acc + term
        pf[...] = acc.reshape(NY, HD, columns)
        pown[m] = pf[y]
        psend[m] = pf[...].astype(BF16)
        others(
            NY, y, lambda k, i: remote(psend.at[m, k], precv.at[m, y], ps.at[m, i], pr.at[m, y], dev_y(k)).start()
        )

    def phase(ph, carry):
        @pl.when(ph < 4)
        def _():
            m = lax.rem(ph + 3, 4)

            def hop(t, carry):
                from_low = p - t

                @pl.when(from_low >= 0)
                def _():
                    wait_block(wall.at[m, from_low], wr.at[m, from_low])
                    send_weight(0, m, from_low)

                from_high = p + t

                @pl.when(from_high < ZL)
                def _():
                    wait_block(wall.at[m, from_high], wr.at[m, from_high])
                    send_weight(1, m, from_high)

                @pl.when((t == max(ZL - 3, 1)) & (ph < 3))
                def _():
                    send_own(ph + 1)

                return carry

            lax.fori_loop(1, ZL, hop, 0)

        @pl.when(ph == 0)
        def _():
            send_tokens()

        @pl.when(ph > 0)
        def _():
            multiply(ph - 1)

        return carry

    lax.fori_loop(0, 5, phase, 0)

    def projected(m):
        value = pown[m]
        for i in range(1, NY):
            k = lax.rem(y + i, NY)
            wait_block(precv.at[m, k], pr.at[m, k])
            value = value + precv[m, k].astype(F32)
        return value

    grad_attn_all = projected(3).astype(BF16)
    query_all = projected(0)
    key_all = projected(1)
    value_all = projected(2).astype(BF16)
    score_scale = HD ** (-0.5)
    for h in range(wall.shape[3] // HD):
        cols = slice(h * HD, (h + 1) * HD)
        q_hat, q_inv = row_norm(query_all[:, cols])
        k_hat, k_inv = row_norm(key_all[:, cols])
        queries, key_rows = q_hat.astype(BF16), k_hat.astype(BF16)
        value_rows, grad_attn = value_all[:, cols], grad_attn_all[:, cols]
        exps = jnp.exp(mm_nt(queries, key_rows) * score_scale)
        probs = exps / jnp.sum(exps, axis=-1, keepdims=True)
        grad_values = mm_tn(probs.astype(BF16), grad_attn)
        grad_probs = mm_nt(grad_attn, value_rows)
        inner = jnp.sum(probs * grad_probs, axis=-1, keepdims=True)
        grad_scores = (probs * (grad_probs - inner) * score_scale).astype(BF16)
        grad_query = mm(grad_scores, key_rows)
        grad_keys = mm_tn(grad_scores, queries)
        dbuf[y, 0, :, cols] = row_norm_back(grad_query, q_hat, q_inv).astype(BF16)
        dbuf[y, 1, :, cols] = row_norm_back(grad_keys, k_hat, k_inv).astype(BF16)
        dbuf[y, 2, :, cols] = grad_values.astype(BF16)
    others(NY, y, lambda k, i: remote(dbuf.at[y], dbuf.at[y], ds_.at[i], dr.at[y], dev_y(k)).start())

    def terms(i, carry):
        tb = lax.rem(y + i, NY)

        @pl.when(i > 0)
        def _():
            wait_block(dbuf.at[tb], dr.at[tb])

        for j in range(ZH * NC):
            acc = None
            for m in range(3):
                weights = wall[m].reshape(ZL * rows, wall.shape[3])[j * width : (j + 1) * width]
                term = mm_nt(dbuf[tb, m], weights)
                acc = term if acc is None else acc + term
            tbuf[j % NC, tb, j // NC] = acc.astype(BF16)
        remote(tbuf.at[1 - c, tb], tr.at[tb], tcs.at[tb], tcr.at[tb], dev(x, y, zh, p, 1 - c)).start()
        return carry

    lax.fori_loop(0, NY, terms, 0)

    def add_cores(i, carry):
        tb = lax.rem(y + i, NY)
        wait_block(tr.at[tb], tcr.at[tb])
        sbuf[tb] = (tbuf[c, tb].astype(F32) + tr[tb].astype(F32)).astype(BF16)

        @pl.when(tb != x)
        def _():
            remote(sbuf.at[tb], sr.at[x], ss.at[tb], srs.at[x], dev(tb, y, zh, p, c)).start()

        return carry

    lax.fori_loop(0, NY, add_cores, 0)
    value = sbuf[x].astype(F32)
    for i in range(1, NX):
        k = lax.rem(x + i, NX)
        wait_block(sr.at[k], srs.at[k])
        value = value + sr[k].astype(F32)
    ubuf[...] = value.astype(BF16)
    for k in range(ZH):
        here = (x == y) & (zh == k)

        @pl.when(here)
        def _():
            pltpu.make_async_copy(ubuf.at[k], ur.at[zh], urs.at[zh]).start()

        @pl.when(jnp.logical_not(here))
        def _():
            remote(ubuf.at[k], ur.at[zh], us.at[k], urs.at[zh], dev(y, x, k, p, c)).start()

    for k in range(ZH):
        wait_block(ur.at[k], urs.at[k])
    upstream = (ur[0].astype(F32) + ur[1].astype(F32)) * gain[...].astype(F32)
    fin[mp] = columns_to_rows(
        jnp.sum(upstream, axis=-1, keepdims=True), jnp.sum(upstream * normed[...], axis=-1, keepdims=True)
    )
    share(fin, n_mp, mp, dev_mp, st_s.at[4], st_r.at[4])
    arrived(fin, n_mp, st_r.at[4])
    sums = jnp.sum(fin[...], axis=0) * (1.0 / n_feat)
    first, second = rows_to_columns(sums[0:1], sums[1:2])
    out[...] = ((upstream - first - normed[...] * second) * invc[:, 0:1]).astype(BF16)

    arrived(st_z, n_z, st_s.at[0])
    arrived(rs, n_mp, st_s.at[1])
    arrived(st_xc, NX * NC, st_s.at[2])
    arrived(st_y, NY, st_s.at[3])
    arrived(fin, n_mp, st_s.at[4])
    for k in range(ZH):
        here = (x == y) & (zh == k)

        @pl.when(jnp.logical_not(here))
        def _():
            wait_block(nin, xs.at[k])
            wait_block(ubuf.at[k], us.at[k])

    def left_y(i, carry):
        for j in range(ZH * NC):
            wait_block(xc.at[1, j, 0], cs.at[i, j])
        for m in range(4):
            wait_block(psend.at[m, 0], ps.at[m, i])
        wait_block(dbuf.at[0], ds_.at[i])
        return carry

    lax.fori_loop(1, NY, left_y, 0)

    def left_xc(i, carry):
        for k in range(ZH):
            wait_block(xc.at[0, 0, 0], n3s.at[k, i])
        return carry

    lax.fori_loop(1, NX * NC, left_xc, 0)

    def left_blocks(tb, carry):
        wait_block(tr.at[tb], tcs.at[tb])

        @pl.when(tb != x)
        def _():
            wait_block(sbuf.at[tb], ss.at[tb])

        return carry

    lax.fori_loop(0, NY, left_blocks, 0)

    def left_weights(i, carry):
        m, s = lax.div(i, ZL), lax.rem(i, ZL)

        @pl.when((p < ZL - 1) & (s <= p))
        def _():
            wait_block(wall.at[m, s], ws.at[0, m, s])

        @pl.when((p > 0) & (s >= p))
        def _():
            wait_block(wall.at[m, s], ws.at[1, m, s])

        return carry

    lax.fori_loop(0, 4 * ZL, left_weights, 0)


def per_device(tokens, norm_gain, attn_weights, stored_grads, cotangent):
    width = tokens.shape[1]
    _, rows, columns = attn_weights.shape
    n_mp = NX * ZH * NC
    nj = ZH * NC
    dma = pltpu.SemaphoreType.DMA
    vmem = pl.BlockSpec(memory_space=pltpu.VMEM)
    return pl.pallas_call(
        kernel,
        out_shape=jax.ShapeDtypeStruct((HD, width), BF16),
        in_specs=[vmem, vmem, vmem, vmem, pl.BlockSpec(memory_space=pl.ANY)],
        out_specs=vmem,
        scratch_shapes=[
            pltpu.VMEM((ZH * ZL, 16, HD), F32),
            pltpu.VMEM((NX * NC, 16, HD), F32),
            pltpu.VMEM((NY, 16, HD), F32),
            pltpu.VMEM((n_mp, 8, HD), F32),
            pltpu.VMEM((n_mp, 8, HD), F32),
            pltpu.VMEM((HD, width), BF16),
            pltpu.VMEM((HD, width), F32),
            pltpu.VMEM((HD, HD), F32),
            pltpu.VMEM((2, nj, NY, HD, width), BF16),
            pltpu.VMEM((4, ZL, rows, columns), BF16),
            pltpu.VMEM((NY, HD, columns), F32),
            pltpu.VMEM((4, HD, columns), F32),
            pltpu.VMEM((4, NY, HD, columns), BF16),
            pltpu.VMEM((4, NY, HD, columns), BF16),
            pltpu.VMEM((NY, 3, HD, columns), BF16),
            pltpu.VMEM((NC, NY, ZH, HD, width), BF16),
            pltpu.VMEM((NY, ZH, HD, width), BF16),
            pltpu.VMEM((NY, ZH, HD, width), BF16),
            pltpu.VMEM((NX, ZH, HD, width), BF16),
            pltpu.VMEM((ZH, HD, width), BF16),
            pltpu.VMEM((ZH, HD, width), BF16),
            dma((5,)),
            dma((5,)),
            dma((ZH,)),
            dma((2, nj, NY)),
            dma((NY, nj)),
            dma((ZH, NX * NC)),
            dma((2, 4, ZL)),
            dma((4, ZL)),
            dma((4, NY)),
            dma((4, NY)),
            dma((NY,)),
            dma((NY,)),
            dma((NY,)),
            dma((NY,)),
            dma((NY,)),
            dma((NX,)),
            dma((ZH,)),
            dma((ZH,)),
        ],
        compiler_params=pltpu.CompilerParams(
            collective_id=0, has_side_effects=True, vmem_limit_bytes=48 * 1024 * 1024
        ),
    )(tokens, norm_gain.reshape(1, -1), attn_weights, stored_grads, cotangent)


def solution(mesh):
    return jax.shard_map(
        per_device,
        mesh=mesh,
        in_specs=(P("dp", "mp"), P("mp"), P(None, "dp", "mp"), P(None, "dp", "mp"), P("dp", None)),
        out_specs=P("dp", "mp"),
        check_vma=False,
    )
```

```python
import jax
import jax.numpy as jnp
from jax import lax
from jax.experimental import pallas as pl
from jax.experimental.pallas import tpu as pltpu
from jax.sharding import PartitionSpec as P

MESH = pl.DeviceIdType.MESH
F32, BF16 = jnp.float32, jnp.bfloat16
HD = 128
NX, NY, ZH, ZL, NC = 4, 4, 2, 8, 2
NH = 2
NR = 2
ascent_radius = 0.15


def mm(a, b):
    return lax.dot_general(a, b, (((1,), (0,)), ((), ())), preferred_element_type=F32)


def mm_nt(a, b):
    return lax.dot_general(a, b, (((1,), (1,)), ((), ())), preferred_element_type=F32)


def mm_tn(a, b):
    return lax.dot_general(a, b, (((0,), (0,)), ((), ())), preferred_element_type=F32)


def row_norm(matrix):
    center = matrix - jnp.mean(matrix, axis=-1, keepdims=True)
    inverse = lax.rsqrt(jnp.mean(center * center, axis=-1, keepdims=True) + 1e-06)
    return center * inverse, inverse


def row_norm_back(upstream, normed, inverse):
    first_mean = jnp.mean(upstream, axis=-1, keepdims=True)
    second_mean = jnp.mean(upstream * normed, axis=-1, keepdims=True)
    return (upstream - first_mean - normed * second_mean) * inverse


def columns_to_rows(first, second):
    lane = lax.broadcasted_iota(jnp.int32, (HD, HD), 1)
    both = jnp.where(lane == 0, first, jnp.where(lane == 1, second, 0.0))
    return both.T[0:8]


def rows_to_columns(first, second):
    sub = lax.broadcasted_iota(jnp.int32, (HD, HD), 0)
    both = jnp.where(sub == 0, first, jnp.where(sub == 1, second, 0.0))
    turned = both.T
    return turned[:, 0:1], turned[:, 1:2]


def kernel(
    tok, gain, w, g, cot, out,
    st_z, st_xyc, rs, gx, fa, fb, nin, normed, invc, xc, wall, pf, pown, psend, precv, dbuf, tbuf, tr, sbuf, sr, ubuf, ur,
    st_s, st_r, gs, gr, fs, xs, xr, cs, n3s, ws, wr, ps, pr, ds_, dr, tcs, tcr, ss, srs, us, urs,
):
    n_mp = NX * ZH * NC
    n_z = ZH * ZL
    width = tok.shape[1]
    band = ZH * NC * width
    n_feat = n_mp * width
    rows = w.shape[1]
    dp = lax.axis_index("dp")
    mp = lax.axis_index("mp")
    y, p = lax.div(dp, ZL), lax.rem(dp, ZL)
    x, c = lax.div(mp, ZH * NC), lax.rem(mp, NC)
    zh = lax.rem(lax.div(mp, NC), ZH)
    z = zh * ZL + p
    xcore = x * NC + c
    xyc = y * NX * NC + xcore
    half = HD // NR
    n_xyc = NX * NY * NC

    def dev(x_, y_, zh_, p_, c_):
        return (y_ * ZL + p_, (x_ * ZH + zh_) * NC + c_)

    def dev_z(k):
        return dev(x, y, lax.div(k, ZL), lax.rem(k, ZL), c)

    def dev_xc(k):
        return dev(lax.div(k, NC), y, zh, p, lax.rem(k, NC))

    def dev_xyc(k):
        return dev(lax.rem(lax.div(k, NC), NX), lax.div(k, NX * NC), zh, p, lax.rem(k, NC))

    def dev_y(k):
        return dev(x, k, zh, p, c)

    def dev_mp(k):
        return (dp, k)

    def remote(src, dst, ssem, rsem, device):
        return pltpu.make_async_remote_copy(
            src_ref=src, dst_ref=dst, send_sem=ssem, recv_sem=rsem, device_id=device, device_id_type=MESH
        )

    def others(n, mine, fn):
        def step(i, carry):
            fn(lax.rem(mine + i, n), i)
            return carry

        lax.fori_loop(1, n, step, 0)

    def share(buf, n, mine, dev_of, ssem, rsem):
        others(n, mine, lambda k, i: remote(buf.at[mine], buf.at[mine], ssem, rsem, dev_of(k)).start())

    def arrived(buf, n, sem):
        part = buf.at[pl.ds(0, n - 1)]
        pltpu.make_async_copy(part, part, sem).wait()

    barrier = pltpu.get_barrier_semaphore()

    def greet(device):
        pl.semaphore_signal(barrier, inc=1, device_id=device, device_id_type=MESH)

    others(n_z, z, lambda k, i: greet(dev_z(k)))
    others(n_xyc, xyc, lambda k, i: greet(dev_xyc(k)))

    def greet_mp(k, i):
        far = lax.rem(lax.div(k, NC), ZH) != zh

        @pl.when(far & ((lax.div(k, ZH * NC) != x) | (lax.rem(k, NC) != c)))
        def _():
            greet(dev_mp(k))

    others(n_mp, mp, greet_mp)

    def greet_turned(k, i):
        @pl.when(x != y)
        def _():
            greet(dev(y, x, k, p, c))

    others(ZH, zh, greet_turned)

    lane = lax.broadcasted_iota(jnp.int32, (1, HD), 1)
    row = jnp.zeros((1, HD), F32)
    for m in range(4):
        for base, ref in ((0, w), (4, g)):
            values = ref[m].astype(F32)
            sums = jnp.sum(values * values, axis=0, keepdims=True)
            row = jnp.where(lane == base + m, jnp.sum(sums, axis=1, keepdims=True), row)
    st_z[z] = row
    part = tok[...].astype(F32)
    part_mean = jnp.sum(part, axis=-1, keepdims=True) * (1.0 / width)
    part_square = jnp.sum(jnp.square(part - part_mean), axis=-1, keepdims=True)
    rs[mp] = columns_to_rows(part_mean, part_square)[0:2]
    gx_row = jnp.broadcast_to(gain[...].astype(F32), (8, width))
    gx[ZH] = gx_row

    pl.semaphore_wait(
        barrier, (n_z - 1) + (n_xyc - 1) + (ZH - 1) * (NX * NC - 1) + jnp.where(x != y, ZH - 1, 0)
    )

    share(st_z, n_z, z, dev_z, st_s.at[0], st_r.at[0])
    share(rs, n_mp, mp, dev_mp, st_s.at[1], st_r.at[1])
    arrived(st_z, n_z, st_r.at[0])
    st_xyc[xyc] = jnp.sum(st_z[...], axis=0)
    share(st_xyc, n_xyc, xyc, dev_xyc, st_s.at[2], st_r.at[2])

    arrived(rs, n_mp, st_r.at[1])
    means = rs[:, 0:1, :]
    mean = jnp.sum(means, axis=0) * (1.0 / n_mp)
    square = jnp.sum(rs[:, 1:2, :], axis=0) + width * jnp.sum(jnp.square(means - mean[None]), axis=0)
    inverse = lax.rsqrt(square * (1.0 / n_feat) + 1e-06)
    mean_col, inv_col = rows_to_columns(mean, inverse)
    normed[...] = (tok[...].astype(F32) - mean_col) * inv_col
    invc[...] = jnp.broadcast_to(inv_col, (HD, HD))
    nin[...] = (normed[...] * gain[...].astype(F32)).astype(BF16)

    for k in range(ZH):
        here = (x == y) & (zh == k)
        dst = xc.at[0, zh * NC + c, y]
        landed = xr.at[0, zh * NC + c, y]

        @pl.when(here)
        def _():
            pltpu.make_async_copy(nin, dst, landed).start()
            pltpu.make_async_copy(gx.at[ZH], gx.at[zh], gr.at[zh]).start()

        @pl.when(jnp.logical_not(here))
        def _():
            remote(nin, dst, xs.at[k], landed, dev(y, x, k, p, c)).start()
            remote(gx.at[ZH], gx.at[zh], gs.at[k], gr.at[zh], dev(y, x, k, p, c)).start()

    arrived(st_xyc, n_xyc, st_r.at[2])
    total = jnp.sum(st_xyc[...], axis=0)
    piece = rows // NH
    for m in range(4):
        ratio = (
            ascent_radius * jnp.sqrt(total[:, m : m + 1]) / (jnp.sqrt(total[:, 4 + m : 5 + m]) + 1e-12)
        )
        shifted = (w[m].astype(F32) + ratio * g[m].astype(F32)).astype(BF16)
        for h in range(NH):
            wall[m, p, h] = shifted[h * piece : (h + 1) * piece]

    def send_weight(way, m, s, h):
        @pl.when(p < ZL - 1 if way == 0 else p > 0)
        def _():
            block = wall.at[m, s, h]
            remote(
                block, block, ws.at[way, m, s, h], wr.at[m, s, h], dev(x, y, zh, p + 1 - 2 * way, c)
            ).start()

    def send_own(ph):
        m = lax.rem(ph + 3, 4)
        for h in range(NH):
            send_weight(0, m, p, h)
            send_weight(1, m, p, h)

    send_own(0)

    for j in range(ZH * NC):
        pltpu.make_async_copy(
            cot.at[:, pl.ds(pl.multiple_of(y * band + j * width, HD), width)], xc.at[1, j, y], xr.at[1, j, y]
        ).start()

    def send_cot(k, i):
        for j in range(ZH * NC):
            remote(
                cot.at[:, pl.ds(pl.multiple_of(k * band + j * width, HD), width)],
                xc.at[1, j, y],
                cs.at[i, j],
                xr.at[1, j, y],
                dev_y(k),
            ).start()

    others(NY, y, send_cot)

    def wait_block(ref, sem):
        pltpu.make_async_copy(ref, ref, sem).wait()

    def send_tokens():
        for k in range(ZH):
            j = k * NC + c
            wait_block(xc.at[0, j, x], xr.at[0, j, x])
            others(
                NX * NC,
                xcore,
                lambda q, i: remote(
                    xc.at[0, j, x], xc.at[0, j, x], n3s.at[k, i], xr.at[0, j, x], dev_xc(q)
                ).start(),
            )

    def multiply(ph):
        m = lax.rem(ph + 3, 4)
        sel = jnp.where(ph == 0, 1, 0)

        @pl.when(ph < 2)
        def _():
            def wait_one(i, carry):
                j, tb = lax.div(i, NY), lax.rem(i, NY)

                @pl.when((ph == 0) | (lax.rem(j, NC) != c) | (tb != x))
                def _():
                    wait_block(xc.at[sel, j, tb], xr.at[sel, j, tb])

                return carry

            lax.fori_loop(0, ZH * NC * NY, wait_one, 0)

        columns = wall.shape[4]
        weights = wall[m].reshape(ZL * rows, columns)
        acc = None
        for j in range(ZH * NC):
            left = xc[sel, j].reshape(NY * HD, width)
            term = mm(left, weights[j * width : (j + 1) * width])
            acc = term if acc is None else acc + term
        pf[...] = acc.reshape(NY, HD, columns)
        pown[m] = pf[y]
        psend[m] = pf[...].astype(BF16)
        others(
            NY, y, lambda k, i: remote(psend.at[m, k], precv.at[m, y], ps.at[m, i], pr.at[m, y], dev_y(k)).start()
        )

    def phase(ph, carry):
        m = lax.rem(ph + 3, 4)

        def hop(t, carry):
            from_low = p - t
            from_high = p + t
            for h in range(NH):

                @pl.when(from_low >= 0)
                def _():
                    wait_block(wall.at[m, from_low, h], wr.at[m, from_low, h])
                    send_weight(0, m, from_low, h)

                @pl.when(from_high < ZL)
                def _():
                    wait_block(wall.at[m, from_high, h], wr.at[m, from_high, h])
                    send_weight(1, m, from_high, h)

            @pl.when((t == max(ZL - 2, 1)) & (ph < 3))
            def _():
                send_own(ph + 1)

            @pl.when((t == min(6, ZL - 1)) & (ph == 0))
            def _():
                send_tokens()

            @pl.when((t == min(4, ZL - 1)) & (ph > 0))
            def _():
                multiply(ph - 1)

            return carry

        lax.fori_loop(1, ZL, hop, 0)
        return carry

    lax.fori_loop(0, 4, phase, 0)
    multiply(3)

    def projected(m):
        value = pown[m]
        for i in range(1, NY):
            k = lax.rem(y + i, NY)
            wait_block(precv.at[m, k], pr.at[m, k])
            value = value + precv[m, k].astype(F32)
        return value

    grad_attn_all = projected(3).astype(BF16)
    query_all = projected(0)
    key_all = projected(1)
    value_all = projected(2).astype(BF16)
    score_scale = HD ** (-0.5)
    for h in range(wall.shape[4] // HD):
        cols = slice(h * HD, (h + 1) * HD)
        q_hat, q_inv = row_norm(query_all[:, cols])
        k_hat, k_inv = row_norm(key_all[:, cols])
        queries, key_rows = q_hat.astype(BF16), k_hat.astype(BF16)
        value_rows, grad_attn = value_all[:, cols], grad_attn_all[:, cols]
        exps = jnp.exp(mm_nt(queries, key_rows) * score_scale)
        probs = exps / jnp.sum(exps, axis=-1, keepdims=True)
        grad_values = mm_tn(probs.astype(BF16), grad_attn)
        grad_probs = mm_nt(grad_attn, value_rows)
        inner = jnp.sum(probs * grad_probs, axis=-1, keepdims=True)
        grad_scores = (probs * (grad_probs - inner) * score_scale).astype(BF16)
        grad_query = mm(grad_scores, key_rows)
        grad_keys = mm_tn(grad_scores, queries)
        grads = (
            row_norm_back(grad_query, q_hat, q_inv).astype(BF16),
            row_norm_back(grad_keys, k_hat, k_inv).astype(BF16),
            grad_values.astype(BF16),
        )
        for m in range(3):
            for r in range(NR):
                dbuf[r, y, m, :, cols] = grads[m][r * half : (r + 1) * half]
    for r in range(NR):
        others(
            NY, y, lambda k, i: remote(dbuf.at[r, y], dbuf.at[r, y], ds_.at[r, i], dr.at[r, y], dev_y(k)).start()
        )

    def term_block(r, tb, own):
        if not own:
            wait_block(dbuf.at[r, tb], dr.at[r, tb])
        for j in range(ZH * NC):
            acc = None
            for m in range(3):
                weights = wall[m].reshape(ZL * rows, wall.shape[4])[j * width : (j + 1) * width]
                term = mm_nt(dbuf[r, tb, m], weights)
                acc = term if acc is None else acc + term
            tbuf[j % NC, r, tb, j // NC] = acc.astype(BF16)
        remote(
            tbuf.at[1 - c, r, tb], tr.at[r, tb], tcs.at[r, tb], tcr.at[r, tb], dev(x, y, zh, p, 1 - c)
        ).start()

    def add_cores(r, tb):
        wait_block(tr.at[r, tb], tcr.at[r, tb])
        sbuf[r, tb] = (tbuf[c, r, tb].astype(F32) + tr[r, tb].astype(F32)).astype(BF16)

        @pl.when(tb != x)
        def _():
            remote(sbuf.at[r, tb], sr.at[r, x], ss.at[r, tb], srs.at[r, x], dev(tb, y, zh, p, c)).start()

    order = [0, 1, 3, 2] if NY == 4 else list(range(NY))
    for r in range(NR):
        before = None
        for i in order:
            tb = lax.rem(y + i, NY)
            term_block(r, tb, i == 0)
            if before is not None:
                add_cores(r, before)
            before = tb
        add_cores(r, before)

    for k in range(ZH):
        wait_block(gx.at[k], gr.at[k])
    firsts, seconds = [], []
    for r in range(NR):
        value = sbuf[r, x].astype(F32)
        for i in range(1, NX):
            k = lax.rem(x + i, NX)
            wait_block(sr.at[r, k], srs.at[r, k])
            value = value + sr[r, k].astype(F32)
        ubuf[r] = value.astype(BF16)
        for k in range(ZH):
            here = (x == y) & (zh == k)

            @pl.when(here)
            def _():
                pltpu.make_async_copy(ubuf.at[r, k], ur.at[r, zh], urs.at[r, zh]).start()

            @pl.when(jnp.logical_not(here))
            def _():
                remote(ubuf.at[r, k], ur.at[r, zh], us.at[r, k], urs.at[r, zh], dev(y, x, k, p, c)).start()

        first, second = 0.0, 0.0
        for k in range(ZH):
            tokens_in = xc[0, k * NC + c, x, r * half : (r + 1) * half].astype(F32)
            first = first + jnp.sum(value[k] * gx[k, 0:1], axis=-1, keepdims=True)
            second = second + jnp.sum(value[k] * tokens_in, axis=-1, keepdims=True)
        firsts.append(first)
        seconds.append(second)
    fa[zh] = columns_to_rows(jnp.concatenate(firsts, axis=0), jnp.concatenate(seconds, axis=0))[0:2]
    share(fa, ZH, zh, lambda k: dev(x, y, k, p, c), st_s.at[3], st_r.at[3])
    arrived(fa, ZH, st_r.at[3])
    fb[NY * NC] = jnp.sum(fa[...], axis=0)
    yc = y * NC + c

    def send_sums(i, carry):
        device = dev(lax.div(i, NC), x, zh, p, lax.rem(i, NC))
        here = (x == y) & (i == xcore)

        @pl.when(here)
        def _():
            pltpu.make_async_copy(fb.at[NY * NC], fb.at[yc], st_r.at[4]).start()

        @pl.when(jnp.logical_not(here))
        def _():
            remote(fb.at[NY * NC], fb.at[yc], fs.at[i], st_r.at[4], device).start()

        return carry

    lax.fori_loop(0, NX * NC, send_sums, 0)
    for r in range(NR):
        for k in range(ZH):
            wait_block(ur.at[r, k], urs.at[r, k])
    arrived(fb, NY * NC + 1, st_r.at[4])
    sums = jnp.sum(fb[0 : NY * NC], axis=0) * (1.0 / n_feat)
    first, second = rows_to_columns(sums[0:1], sums[1:2])
    for r in range(NR):
        part = slice(r * half, (r + 1) * half)
        share_sum = ur[r, 0].astype(F32)
        for k in range(1, ZH):
            share_sum = share_sum + ur[r, k].astype(F32)
        upstream = share_sum * gain[...].astype(F32)
        out[part] = ((upstream - first[part] - normed[part] * second[part]) * invc[part, 0:1]).astype(BF16)

    arrived(st_z, n_z, st_s.at[0])
    arrived(rs, n_mp, st_s.at[1])
    arrived(st_xyc, n_xyc, st_s.at[2])
    arrived(fa, ZH, st_s.at[3])
    for k in range(ZH):
        here = (x == y) & (zh == k)

        @pl.when(jnp.logical_not(here))
        def _():
            wait_block(nin, xs.at[k])
            wait_block(gx.at[ZH], gs.at[k])
            for r in range(NR):
                wait_block(ubuf.at[r, k], us.at[r, k])

    def left_y(i, carry):
        for j in range(ZH * NC):
            wait_block(xc.at[1, j, 0], cs.at[i, j])
        for m in range(4):
            wait_block(psend.at[m, 0], ps.at[m, i])
        for r in range(NR):
            wait_block(dbuf.at[r, 0], ds_.at[r, i])
        return carry

    lax.fori_loop(1, NY, left_y, 0)

    def left_xc(i, carry):
        @pl.when(i > 0)
        def _():
            for k in range(ZH):
                wait_block(xc.at[0, 0, 0], n3s.at[k, i])

        @pl.when((x != y) | (i != xcore))
        def _():
            wait_block(fb.at[0], fs.at[i])

        return carry

    lax.fori_loop(0, NX * NC, left_xc, 0)

    def left_blocks(tb, carry):
        for r in range(NR):
            wait_block(tr.at[r, tb], tcs.at[r, tb])

        @pl.when(tb != x)
        def _():
            for r in range(NR):
                wait_block(sbuf.at[r, tb], ss.at[r, tb])

        return carry

    lax.fori_loop(0, NY, left_blocks, 0)

    def left_weights(i, carry):
        m, s = lax.div(i, ZL), lax.rem(i, ZL)
        for h in range(NH):

            @pl.when((p < ZL - 1) & (s <= p))
            def _():
                wait_block(wall.at[m, s, h], ws.at[0, m, s, h])

            @pl.when((p > 0) & (s >= p))
            def _():
                wait_block(wall.at[m, s, h], ws.at[1, m, s, h])

        return carry

    lax.fori_loop(0, 4 * ZL, left_weights, 0)


def per_device(tokens, norm_gain, attn_weights, stored_grads, cotangent):
    width = tokens.shape[1]
    _, rows, columns = attn_weights.shape
    n_mp = NX * ZH * NC
    nj = ZH * NC
    dma = pltpu.SemaphoreType.DMA
    vmem = pl.BlockSpec(memory_space=pltpu.VMEM)
    return pl.pallas_call(
        kernel,
        out_shape=jax.ShapeDtypeStruct((HD, width), BF16),
        in_specs=[vmem, vmem, vmem, vmem, pl.BlockSpec(memory_space=pl.ANY)],
        out_specs=vmem,
        scratch_shapes=[
            pltpu.VMEM((ZH * ZL, 1, HD), F32),
            pltpu.VMEM((NX * NY * NC, 1, HD), F32),
            pltpu.VMEM((n_mp, 2, HD), F32),
            pltpu.VMEM((ZH + 1, 8, width), F32),
            pltpu.VMEM((ZH, 2, HD), F32),
            pltpu.VMEM((NY * NC + 1, 2, HD), F32),
            pltpu.VMEM((HD, width), BF16),
            pltpu.VMEM((HD, width), F32),
            pltpu.VMEM((HD, HD), F32),
            pltpu.VMEM((2, nj, NY, HD, width), BF16),
            pltpu.VMEM((4, ZL, NH, rows // NH, columns), BF16),
            pltpu.VMEM((NY, HD, columns), F32),
            pltpu.VMEM((4, HD, columns), F32),
            pltpu.VMEM((4, NY, HD, columns), BF16),
            pltpu.VMEM((4, NY, HD, columns), BF16),
            pltpu.VMEM((NR, NY, 3, HD // NR, columns), BF16),
            pltpu.VMEM((NC, NR, NY, ZH, HD // NR, width), BF16),
            pltpu.VMEM((NR, NY, ZH, HD // NR, width), BF16),
            pltpu.VMEM((NR, NY, ZH, HD // NR, width), BF16),
            pltpu.VMEM((NR, NX, ZH, HD // NR, width), BF16),
            pltpu.VMEM((NR, ZH, HD // NR, width), BF16),
            pltpu.VMEM((NR, ZH, HD // NR, width), BF16),
            dma((4,)),
            dma((5,)),
            dma((ZH,)),
            dma((ZH,)),
            dma((NX * NC,)),
            dma((ZH,)),
            dma((2, nj, NY)),
            dma((NY, nj)),
            dma((ZH, NX * NC)),
            dma((2, 4, ZL, NH)),
            dma((4, ZL, NH)),
            dma((4, NY)),
            dma((4, NY)),
            dma((NR, NY)),
            dma((NR, NY)),
            dma((NR, NY)),
            dma((NR, NY)),
            dma((NR, NY)),
            dma((NR, NX)),
            dma((NR, ZH)),
            dma((NR, ZH)),
        ],
        compiler_params=pltpu.CompilerParams(
            collective_id=0, has_side_effects=True, vmem_limit_bytes=48 * 1024 * 1024
        ),
    )(tokens, norm_gain.reshape(1, -1), attn_weights, stored_grads, cotangent)


def solution(mesh):
    return jax.shard_map(
        per_device,
        mesh=mesh,
        in_specs=(P("dp", "mp"), P("mp"), P(None, "dp", "mp"), P(None, "dp", "mp"), P("dp", None)),
        out_specs=P("dp", "mp"),
        check_vma=False,
    )
```

```python
import jax
import jax.numpy as jnp
from jax import lax
from jax.experimental import pallas as pl
from jax.experimental.pallas import tpu as pltpu
from jax.sharding import PartitionSpec as P

MESH = pl.DeviceIdType.MESH
F32, BF16 = jnp.float32, jnp.bfloat16
HD = 128
NX, NY, ZH, ZL, NC = 4, 4, 2, 8, 2
NH = 2
NR = 2
ascent_radius = 0.15


def mm(a, b):
    return lax.dot_general(a, b, (((1,), (0,)), ((), ())), preferred_element_type=F32)


def mm_nt(a, b):
    return lax.dot_general(a, b, (((1,), (1,)), ((), ())), preferred_element_type=F32)


def mm_tn(a, b):
    return lax.dot_general(a, b, (((0,), (0,)), ((), ())), preferred_element_type=F32)


def row_norm(matrix):
    center = matrix - jnp.mean(matrix, axis=-1, keepdims=True)
    inverse = lax.rsqrt(jnp.mean(center * center, axis=-1, keepdims=True) + 1e-06)
    return center * inverse, inverse


def row_norm_back(upstream, normed, inverse):
    first_mean = jnp.mean(upstream, axis=-1, keepdims=True)
    second_mean = jnp.mean(upstream * normed, axis=-1, keepdims=True)
    return (upstream - first_mean - normed * second_mean) * inverse


def columns_to_rows(first, second):
    lane = lax.broadcasted_iota(jnp.int32, (HD, HD), 1)
    both = jnp.where(lane == 0, first, jnp.where(lane == 1, second, 0.0))
    return both.T[0:8]


def rows_to_columns(first, second):
    sub = lax.broadcasted_iota(jnp.int32, (HD, HD), 0)
    both = jnp.where(sub == 0, first, jnp.where(sub == 1, second, 0.0))
    turned = both.T
    return turned[:, 0:1], turned[:, 1:2]


def kernel(
    tok_hbm, gain_hbm, w_hbm, g_hbm, cot, out,
    tok, gain, w, g,
    st_z, st_xyc, rs, gx, fa, fb, nin, normed, invc, xc, wall, pf, pown, psend, precv, dbuf, tbuf, tr, sbuf, sr, ubuf, ur,
    ins, st_s, st_r, gs, gr, fs, xs, xr, cs, n3s, ws, wr, ps, pr, ds_, dr, tcs, tcr, ss, srs, us, urs,
):
    n_mp = NX * ZH * NC
    n_z = ZH * ZL
    width = tok.shape[1]
    band = ZH * NC * width
    n_feat = n_mp * width
    rows = w.shape[1]
    dp = lax.axis_index("dp")
    mp = lax.axis_index("mp")
    y, p = lax.div(dp, ZL), lax.rem(dp, ZL)
    x, c = lax.div(mp, ZH * NC), lax.rem(mp, NC)
    zh = lax.rem(lax.div(mp, NC), ZH)
    z = zh * ZL + p
    xcore = x * NC + c
    xyc = y * NX * NC + xcore
    half = HD // NR
    n_xyc = NX * NY * NC

    def dev(x_, y_, zh_, p_, c_):
        return (y_ * ZL + p_, (x_ * ZH + zh_) * NC + c_)

    def dev_z(k):
        return dev(x, y, lax.div(k, ZL), lax.rem(k, ZL), c)

    def dev_y(k):
        return dev(x, k, zh, p, c)

    def remote(src, dst, ssem, rsem, device):
        return pltpu.make_async_remote_copy(
            src_ref=src, dst_ref=dst, send_sem=ssem, recv_sem=rsem, device_id=device, device_id_type=MESH
        )

    def share(buf, mine, peers, ssem, rsem):
        for device in peers:
            remote(buf.at[mine], buf.at[mine], ssem, rsem, device).start()

    def arrived(buf, n, sem):
        part = buf.at[pl.ds(0, n - 1)]
        pltpu.make_async_copy(part, part, sem).wait()

    loads = [
        pltpu.make_async_copy(src, dst, ins.at[i])
        for i, (src, dst) in enumerate(((w_hbm, w), (g_hbm, g), (tok_hbm, tok), (gain_hbm, gain)))
    ]
    for load in loads:
        load.start()

    barrier = pltpu.get_barrier_semaphore()

    def greet(device):
        pl.semaphore_signal(barrier, inc=1, device_id=device, device_id_type=MESH)

    z_peers = []
    for i in range(1, n_z):
        k = lax.rem(z + i, n_z)
        z_peers.append((k, dev_z(k)))
    at_x = [lax.rem(x + i, NX) for i in range(NX)]
    at_y = [lax.rem(y + i, NY) for i in range(NY)]
    at_c = [c, 1 - c]
    at_z = [zh, 1 - zh]
    plane_peers = [
        dev(at_x[i], at_y[j], zh, p, at_c[q]) for j in range(NY) for i in range(NX) for q in range(NC) if i + j + q
    ]
    near_peers = [dev(at_x[i], y, zh, p, at_c[q]) for i in range(NX) for q in range(NC) if i + q]
    far_peers = [dev(at_x[i], y, 1 - zh, p, at_c[q]) for i in range(NX) for q in range(NC) if i + q]
    partner = dev(x, y, 1 - zh, p, c)
    y_peers = [(at_y[i], dev_y(at_y[i])) for i in range(1, NY)]
    for _, device in z_peers:
        greet(device)
    for device in far_peers + plane_peers:
        greet(device)

    @pl.when(x != y)
    def _():
        greet(dev(y, x, 1 - zh, p, c))

    loads[0].wait()
    loads[1].wait()
    lane = lax.broadcasted_iota(jnp.int32, (1, HD), 1)
    row = jnp.zeros((1, HD), F32)
    for m in range(4):
        for base, ref in ((0, w), (4, g)):
            values = ref[m].astype(F32)
            sums = jnp.sum(values * values, axis=0, keepdims=True)
            row = jnp.where(lane == base + m, jnp.sum(sums, axis=1, keepdims=True), row)
    st_z[z] = row
    loads[2].wait()
    loads[3].wait()
    part = tok[...].astype(F32)
    part_mean = jnp.sum(part, axis=-1, keepdims=True) * (1.0 / width)
    part_square = jnp.sum(jnp.square(part - part_mean), axis=-1, keepdims=True)
    rs[mp] = columns_to_rows(part_mean, part_square)[0:2]
    gx_row = jnp.broadcast_to(gain[...].astype(F32).reshape(1, -1), (8, width))
    gx[ZH] = gx_row

    pl.semaphore_wait(
        barrier, (n_z - 1) + (n_xyc - 1) + (ZH - 1) * (NX * NC - 1) + jnp.where(x != y, ZH - 1, 0)
    )

    share(st_z, z, [d for _, d in z_peers], st_s.at[0], st_r.at[0])
    share(rs, mp, near_peers + [partner] + far_peers, st_s.at[1], st_r.at[1])
    arrived(st_z, n_z, st_r.at[0])
    st_xyc[xyc] = jnp.sum(st_z[...], axis=0)
    share(st_xyc, xyc, plane_peers, st_s.at[2], st_r.at[2])

    arrived(rs, n_mp, st_r.at[1])
    means = rs[:, 0:1, :]
    mean = jnp.sum(means, axis=0) * (1.0 / n_mp)
    square = jnp.sum(rs[:, 1:2, :], axis=0) + width * jnp.sum(jnp.square(means - mean[None]), axis=0)
    inverse = lax.rsqrt(square * (1.0 / n_feat) + 1e-06)
    mean_col, inv_col = rows_to_columns(mean, inverse)
    normed[...] = (tok[...].astype(F32) - mean_col) * inv_col
    invc[...] = jnp.broadcast_to(inv_col, (HD, HD))
    nin[...] = (normed[...] * gain[...].astype(F32).reshape(1, -1)).astype(BF16)

    for k in range(ZH):
        here = (x == y) & (zh == k)
        dst = xc.at[0, zh * NC + c, y]
        landed = xr.at[0, zh * NC + c, y]

        @pl.when(here)
        def _():
            pltpu.make_async_copy(nin, dst, landed).start()
            pltpu.make_async_copy(gx.at[ZH], gx.at[zh], gr.at[zh]).start()

        @pl.when(jnp.logical_not(here))
        def _():
            remote(nin, dst, xs.at[k], landed, dev(y, x, k, p, c)).start()
            remote(gx.at[ZH], gx.at[zh], gs.at[k], gr.at[zh], dev(y, x, k, p, c)).start()

    arrived(st_xyc, n_xyc, st_r.at[2])
    total = jnp.sum(st_xyc[...], axis=0)
    piece = rows // NH
    for m in range(4):
        ratio = (
            ascent_radius * jnp.sqrt(total[:, m : m + 1]) / (jnp.sqrt(total[:, 4 + m : 5 + m]) + 1e-12)
        )
        shifted = (w[m].astype(F32) + ratio * g[m].astype(F32)).astype(BF16)
        for h in range(NH):
            wall[m, p, h] = shifted[h * piece : (h + 1) * piece]

    pairs = ((3, 0), (1, 2))

    def send_weight(way, m, s, h):
        @pl.when(p < ZL - 1 if way == 0 else p > 0)
        def _():
            block = wall.at[m, s, h]
            remote(
                block, block, ws.at[way, m, s, h], wr.at[m, s, h], dev(x, y, zh, p + 1 - 2 * way, c)
            ).start()

    def send_own(ph):
        for m in pairs[ph]:
            for h in range(NH):
                send_weight(0, m, p, h)
                send_weight(1, m, p, h)

    send_own(0)

    for j in range(ZH * NC):
        pltpu.make_async_copy(
            cot.at[:, pl.ds(pl.multiple_of(y * band + j * width, HD), width)], xc.at[1, j, y], xr.at[1, j, y]
        ).start()

    for i, (k, device) in enumerate(y_peers):
        for j in range(ZH * NC):
            remote(
                cot.at[:, pl.ds(pl.multiple_of(k * band + j * width, HD), width)],
                xc.at[1, j, y],
                cs.at[i, j],
                xr.at[1, j, y],
                device,
            ).start()

    def wait_block(ref, sem):
        pltpu.make_async_copy(ref, ref, sem).wait()

    def send_tokens():
        for k in range(ZH):
            j = k * NC + c
            block = xc.at[0, j, x]
            wait_block(block, xr.at[0, j, x])
            for i, device in enumerate(near_peers):
                remote(block, block, n3s.at[k, i], xr.at[0, j, x], device).start()

    def multiply(m, sel, fresh):
        if fresh:

            def wait_one(i, carry):
                j, tb = lax.div(i, NY), lax.rem(i, NY)

                @pl.when((sel == 1) | (lax.rem(j, NC) != c) | (tb != x))
                def _():
                    wait_block(xc.at[sel, j, tb], xr.at[sel, j, tb])

                return carry

            lax.fori_loop(0, ZH * NC * NY, wait_one, 0)

        columns = wall.shape[4]
        weights = wall[m].reshape(ZL * rows, columns)
        acc = None
        for j in range(ZH * NC):
            left = xc[sel, j].reshape(NY * HD, width)
            term = mm(left, weights[j * width : (j + 1) * width])
            acc = term if acc is None else acc + term
        pf[...] = acc.reshape(NY, HD, columns)
        pown[m] = pf[y]
        psend[m] = pf[...].astype(BF16)
        for i, (k, device) in enumerate(y_peers):
            remote(psend.at[m, k], precv.at[m, y], ps.at[m, i], pr.at[m, y], device).start()

    def phase(ph, middle):
        def hop(t, carry):
            from_low = p - t
            from_high = p + t
            for m in pairs[ph]:
                for h in range(NH):

                    @pl.when(from_low >= 0)
                    def _():
                        wait_block(wall.at[m, from_low, h], wr.at[m, from_low, h])
                        send_weight(0, m, from_low, h)

                    @pl.when(from_high < ZL)
                    def _():
                        wait_block(wall.at[m, from_high, h], wr.at[m, from_high, h])
                        send_weight(1, m, from_high, h)

            return carry

        cut = max(ZL - 2, 2)
        lax.fori_loop(1, cut, hop, 0)
        middle()
        lax.fori_loop(cut, ZL, hop, 0)

    def middle_first():
        send_own(1)
        send_tokens()

    def middle_second():
        multiply(3, 1, True)
        multiply(0, 0, True)

    phase(0, middle_first)
    phase(1, middle_second)
    multiply(1, 0, False)
    multiply(2, 0, False)

    def projected(m):
        value = pown[m]
        for i in range(1, NY):
            k = lax.rem(y + i, NY)
            wait_block(precv.at[m, k], pr.at[m, k])
            value = value + precv[m, k].astype(F32)
        return value

    grad_attn_all = projected(3).astype(BF16)
    query_all = projected(0)
    key_all = projected(1)
    value_all = projected(2).astype(BF16)
    score_scale = HD ** (-0.5)
    for h in range(wall.shape[4] // HD):
        cols = slice(h * HD, (h + 1) * HD)
        q_hat, q_inv = row_norm(query_all[:, cols])
        k_hat, k_inv = row_norm(key_all[:, cols])
        queries, key_rows = q_hat.astype(BF16), k_hat.astype(BF16)
        value_rows, grad_attn = value_all[:, cols], grad_attn_all[:, cols]
        exps = jnp.exp(mm_nt(queries, key_rows) * score_scale)
        probs = exps / jnp.sum(exps, axis=-1, keepdims=True)
        grad_values = mm_tn(probs.astype(BF16), grad_attn)
        grad_probs = mm_nt(grad_attn, value_rows)
        inner = jnp.sum(probs * grad_probs, axis=-1, keepdims=True)
        grad_scores = (probs * (grad_probs - inner) * score_scale).astype(BF16)
        grad_query = mm(grad_scores, key_rows)
        grad_keys = mm_tn(grad_scores, queries)
        grads = (
            row_norm_back(grad_query, q_hat, q_inv).astype(BF16),
            row_norm_back(grad_keys, k_hat, k_inv).astype(BF16),
            grad_values.astype(BF16),
        )
        for m in range(3):
            for r in range(NR):
                dbuf[r, y, m, :, cols] = grads[m][r * half : (r + 1) * half]
    for r in range(NR):
        for i, (_, device) in enumerate(y_peers):
            remote(dbuf.at[r, y], dbuf.at[r, y], ds_.at[r, i], dr.at[r, y], device).start()

    def term_block(r, tb, own):
        if not own:
            wait_block(dbuf.at[r, tb], dr.at[r, tb])
        for j in range(ZH * NC):
            acc = None
            for m in range(3):
                weights = wall[m].reshape(ZL * rows, wall.shape[4])[j * width : (j + 1) * width]
                term = mm_nt(dbuf[r, tb, m], weights)
                acc = term if acc is None else acc + term
            tbuf[j % NC, r, tb, j // NC] = acc.astype(BF16)
        remote(
            tbuf.at[1 - c, r, tb], tr.at[r, tb], tcs.at[r, tb], tcr.at[r, tb], dev(x, y, zh, p, 1 - c)
        ).start()

    def add_cores(r, tb):
        wait_block(tr.at[r, tb], tcr.at[r, tb])
        sbuf[r, tb] = (tbuf[c, r, tb].astype(F32) + tr[r, tb].astype(F32)).astype(BF16)

        @pl.when(tb != x)
        def _():
            remote(sbuf.at[r, tb], sr.at[r, x], ss.at[r, tb], srs.at[r, x], dev(tb, y, zh, p, c)).start()

    order = [0, 1, 3, 2] if NY == 4 else list(range(NY))
    for r in range(NR):
        before = None
        for i in order:
            tb = lax.rem(y + i, NY)
            term_block(r, tb, i == 0)
            if before is not None:
                add_cores(r, before)
            before = tb
        add_cores(r, before)

    for k in range(ZH):
        wait_block(gx.at[k], gr.at[k])
    firsts, seconds = [], []
    for r in range(NR):
        value = sbuf[r, x].astype(F32)
        for i in range(1, NX):
            k = lax.rem(x + i, NX)
            wait_block(sr.at[r, k], srs.at[r, k])
            value = value + sr[r, k].astype(F32)
        ubuf[r] = value.astype(BF16)
        for k in range(ZH):
            here = (x == y) & (zh == k)

            @pl.when(here)
            def _():
                pltpu.make_async_copy(ubuf.at[r, k], ur.at[r, zh], urs.at[r, zh]).start()

            @pl.when(jnp.logical_not(here))
            def _():
                remote(ubuf.at[r, k], ur.at[r, zh], us.at[r, k], urs.at[r, zh], dev(y, x, k, p, c)).start()

        first, second = 0.0, 0.0
        for k in range(ZH):
            tokens_in = xc[0, k * NC + c, x, r * half : (r + 1) * half].astype(F32)
            first = first + jnp.sum(value[k] * gx[k, 0:1], axis=-1, keepdims=True)
            second = second + jnp.sum(value[k] * tokens_in, axis=-1, keepdims=True)
        firsts.append(first)
        seconds.append(second)
    fa[zh] = columns_to_rows(jnp.concatenate(firsts, axis=0), jnp.concatenate(seconds, axis=0))[0:2]
    share(fa, zh, [partner], st_s.at[3], st_r.at[3])
    arrived(fa, ZH, st_r.at[3])
    fb[NY * NC] = jnp.sum(fa[...], axis=0)
    yc = y * NC + c

    def send_sums(i, carry):
        device = dev(lax.div(i, NC), x, zh, p, lax.rem(i, NC))
        here = (x == y) & (i == xcore)

        @pl.when(here)
        def _():
            pltpu.make_async_copy(fb.at[NY * NC], fb.at[yc], st_r.at[4]).start()

        @pl.when(jnp.logical_not(here))
        def _():
            remote(fb.at[NY * NC], fb.at[yc], fs.at[i], st_r.at[4], device).start()

        return carry

    lax.fori_loop(0, NX * NC, send_sums, 0)
    for r in range(NR):
        for k in range(ZH):
            wait_block(ur.at[r, k], urs.at[r, k])
    arrived(fb, NY * NC + 1, st_r.at[4])
    sums = jnp.sum(fb[0 : NY * NC], axis=0) * (1.0 / n_feat)
    first, second = rows_to_columns(sums[0:1], sums[1:2])
    for r in range(NR):
        part = slice(r * half, (r + 1) * half)
        share_sum = ur[r, 0].astype(F32)
        for k in range(1, ZH):
            share_sum = share_sum + ur[r, k].astype(F32)
        upstream = share_sum * gain[...].astype(F32).reshape(1, -1)
        out[part] = ((upstream - first[part] - normed[part] * second[part]) * invc[part, 0:1]).astype(BF16)

    arrived(st_z, n_z, st_s.at[0])
    arrived(rs, n_mp, st_s.at[1])
    arrived(st_xyc, n_xyc, st_s.at[2])
    arrived(fa, ZH, st_s.at[3])
    for k in range(ZH):
        here = (x == y) & (zh == k)

        @pl.when(jnp.logical_not(here))
        def _():
            wait_block(nin, xs.at[k])
            wait_block(gx.at[ZH], gs.at[k])
            for r in range(NR):
                wait_block(ubuf.at[r, k], us.at[r, k])

    def left_y(i, carry):
        for j in range(ZH * NC):
            wait_block(xc.at[1, j, 0], cs.at[i, j])
        for m in range(4):
            wait_block(psend.at[m, 0], ps.at[m, i])
        for r in range(NR):
            wait_block(dbuf.at[r, 0], ds_.at[r, i])
        return carry

    lax.fori_loop(0, NY - 1, left_y, 0)

    def left_xc(i, carry):
        @pl.when(i > 0)
        def _():
            for k in range(ZH):
                wait_block(xc.at[0, 0, 0], n3s.at[k, i - 1])

        @pl.when((x != y) | (i != xcore))
        def _():
            wait_block(fb.at[0], fs.at[i])

        return carry

    lax.fori_loop(0, NX * NC, left_xc, 0)

    def left_blocks(tb, carry):
        for r in range(NR):
            wait_block(tr.at[r, tb], tcs.at[r, tb])

        @pl.when(tb != x)
        def _():
            for r in range(NR):
                wait_block(sbuf.at[r, tb], ss.at[r, tb])

        return carry

    lax.fori_loop(0, NY, left_blocks, 0)

    def left_weights(i, carry):
        m, s = lax.div(i, ZL), lax.rem(i, ZL)
        for h in range(NH):

            @pl.when((p < ZL - 1) & (s <= p))
            def _():
                wait_block(wall.at[m, s, h], ws.at[0, m, s, h])

            @pl.when((p > 0) & (s >= p))
            def _():
                wait_block(wall.at[m, s, h], ws.at[1, m, s, h])

        return carry

    lax.fori_loop(0, 4 * ZL, left_weights, 0)


def per_device(tokens, norm_gain, attn_weights, stored_grads, cotangent):
    width = tokens.shape[1]
    _, rows, columns = attn_weights.shape
    n_mp = NX * ZH * NC
    nj = ZH * NC
    dma = pltpu.SemaphoreType.DMA
    vmem = pl.BlockSpec(memory_space=pltpu.VMEM)
    return pl.pallas_call(
        kernel,
        out_shape=jax.ShapeDtypeStruct((HD, width), BF16),
        in_specs=[pl.BlockSpec(memory_space=pltpu.HBM)] * 5,
        out_specs=vmem,
        scratch_shapes=[
            pltpu.VMEM(tokens.shape, BF16),
            pltpu.VMEM((width,), BF16),
            pltpu.VMEM(attn_weights.shape, BF16),
            pltpu.VMEM(attn_weights.shape, BF16),
            pltpu.VMEM((ZH * ZL, 1, HD), F32),
            pltpu.VMEM((NX * NY * NC, 1, HD), F32),
            pltpu.VMEM((n_mp, 2, HD), F32),
            pltpu.VMEM((ZH + 1, 8, width), F32),
            pltpu.VMEM((ZH, 2, HD), F32),
            pltpu.VMEM((NY * NC + 1, 2, HD), F32),
            pltpu.VMEM((HD, width), BF16),
            pltpu.VMEM((HD, width), F32),
            pltpu.VMEM((HD, HD), F32),
            pltpu.VMEM((2, nj, NY, HD, width), BF16),
            pltpu.VMEM((4, ZL, NH, rows // NH, columns), BF16),
            pltpu.VMEM((NY, HD, columns), F32),
            pltpu.VMEM((4, HD, columns), F32),
            pltpu.VMEM((4, NY, HD, columns), BF16),
            pltpu.VMEM((4, NY, HD, columns), BF16),
            pltpu.VMEM((NR, NY, 3, HD // NR, columns), BF16),
            pltpu.VMEM((NC, NR, NY, ZH, HD // NR, width), BF16),
            pltpu.VMEM((NR, NY, ZH, HD // NR, width), BF16),
            pltpu.VMEM((NR, NY, ZH, HD // NR, width), BF16),
            pltpu.VMEM((NR, NX, ZH, HD // NR, width), BF16),
            pltpu.VMEM((NR, ZH, HD // NR, width), BF16),
            pltpu.VMEM((NR, ZH, HD // NR, width), BF16),
            dma((4,)),
            dma((4,)),
            dma((5,)),
            dma((ZH,)),
            dma((ZH,)),
            dma((NX * NC,)),
            dma((ZH,)),
            dma((2, nj, NY)),
            dma((NY, nj)),
            dma((ZH, NX * NC)),
            dma((2, 4, ZL, NH)),
            dma((4, ZL, NH)),
            dma((4, NY)),
            dma((4, NY)),
            dma((NR, NY)),
            dma((NR, NY)),
            dma((NR, NY)),
            dma((NR, NY)),
            dma((NR, NY)),
            dma((NR, NX)),
            dma((NR, ZH)),
            dma((NR, ZH)),
        ],
        compiler_params=pltpu.CompilerParams(
            collective_id=0, has_side_effects=True, vmem_limit_bytes=60 * 1024 * 1024
        ),
    )(tokens, norm_gain, attn_weights, stored_grads, cotangent)


def solution(mesh):
    return jax.shard_map(
        per_device,
        mesh=mesh,
        in_specs=(P("dp", "mp"), P("mp"), P(None, "dp", "mp"), P(None, "dp", "mp"), P("dp", None)),
        out_specs=P("dp", "mp"),
        check_vma=False,
    )
```

```python
import jax
import jax.numpy as jnp
from jax import lax
from jax.experimental import pallas as pl
from jax.experimental.pallas import tpu as pltpu
from jax.sharding import PartitionSpec as P

MESH = pl.DeviceIdType.MESH
F32, BF16 = jnp.float32, jnp.bfloat16
HD = 128
NX, NY, ZH, ZL, NC = 4, 4, 2, 8, 2
NH = 2
NR = 2
ascent_radius = 0.15


def mm(a, b):
    return lax.dot_general(a, b, (((1,), (0,)), ((), ())), preferred_element_type=F32)


def mm_nt(a, b):
    return lax.dot_general(a, b, (((1,), (1,)), ((), ())), preferred_element_type=F32)


def mm_tn(a, b):
    return lax.dot_general(a, b, (((0,), (0,)), ((), ())), preferred_element_type=F32)


def row_norm(matrix):
    center = matrix - jnp.mean(matrix, axis=-1, keepdims=True)
    inverse = lax.rsqrt(jnp.mean(center * center, axis=-1, keepdims=True) + 1e-06)
    return center * inverse, inverse


def row_norm_back(upstream, normed, inverse):
    first_mean = jnp.mean(upstream, axis=-1, keepdims=True)
    second_mean = jnp.mean(upstream * normed, axis=-1, keepdims=True)
    return (upstream - first_mean - normed * second_mean) * inverse


def columns_to_rows(first, second):
    lane = lax.broadcasted_iota(jnp.int32, (HD, HD), 1)
    both = jnp.where(lane == 0, first, jnp.where(lane == 1, second, 0.0))
    return both.T[0:8]


def rows_to_columns(first, second):
    sub = lax.broadcasted_iota(jnp.int32, (HD, HD), 0)
    both = jnp.where(sub == 0, first, jnp.where(sub == 1, second, 0.0))
    turned = both.T
    return turned[:, 0:1], turned[:, 1:2]


def kernel(
    tok_hbm, gain_hbm, w_hbm, g_hbm, cot, out,
    tok, gain, w, g,
    st_z, st_xyc, rs, gx, fb, mi, xraw, normed, invc, xc, wall, pf, pown, psend, precv, dbuf, tbuf, tr, sbuf, sr, ubuf, ur,
    ins, st_s, st_r, gs, gr, fs, ms, xs, xw, xr, cs, n3s, ws, wr, ps, pr, ds_, dr, tcs, tcr, ss, srs, us, urs,
):
    n_mp = NX * ZH * NC
    n_z = ZH * ZL
    width = tok.shape[1]
    band = ZH * NC * width
    n_feat = n_mp * width
    rows = w.shape[1]
    dp = lax.axis_index("dp")
    mp = lax.axis_index("mp")
    y, p = lax.div(dp, ZL), lax.rem(dp, ZL)
    x, c = lax.div(mp, ZH * NC), lax.rem(mp, NC)
    zh = lax.rem(lax.div(mp, NC), ZH)
    z = zh * ZL + p
    xcore = x * NC + c
    xyc = y * NX * NC + xcore
    half = HD // NR
    n_xyc = NX * NY * NC

    def dev(x_, y_, zh_, p_, c_):
        return (y_ * ZL + p_, (x_ * ZH + zh_) * NC + c_)

    def dev_z(k):
        return dev(x, y, lax.div(k, ZL), lax.rem(k, ZL), c)

    def dev_y(k):
        return dev(x, k, zh, p, c)

    def remote(src, dst, ssem, rsem, device):
        return pltpu.make_async_remote_copy(
            src_ref=src, dst_ref=dst, send_sem=ssem, recv_sem=rsem, device_id=device, device_id_type=MESH
        )

    def share(buf, mine, peers, ssem, rsem):
        for device in peers:
            remote(buf.at[mine], buf.at[mine], ssem, rsem, device).start()

    def arrived(buf, n, sem):
        part = buf.at[pl.ds(0, n - 1)]
        pltpu.make_async_copy(part, part, sem).wait()

    loads = [
        pltpu.make_async_copy(src, dst, ins.at[i])
        for i, (src, dst) in enumerate(((w_hbm, w), (g_hbm, g), (tok_hbm, tok), (gain_hbm, gain)))
    ]
    for load in loads:
        load.start()

    barrier = pltpu.get_barrier_semaphore()

    def greet(device):
        pl.semaphore_signal(barrier, inc=1, device_id=device, device_id_type=MESH)

    z_peers = []
    for i in range(1, n_z):
        k = lax.rem(z + i, n_z)
        z_peers.append((k, dev_z(k)))
    at_x = [lax.rem(x + i, NX) for i in range(NX)]
    at_y = [lax.rem(y + i, NY) for i in range(NY)]
    at_c = [c, 1 - c]
    at_z = [zh, 1 - zh]
    plane_peers = [
        dev(at_x[i], at_y[j], zh, p, at_c[q]) for j in range(NY) for i in range(NX) for q in range(NC) if i + j + q
    ]
    near_peers = [dev(at_x[i], y, zh, p, at_c[q]) for i in range(NX) for q in range(NC) if i + q]
    far_peers = [dev(at_x[i], y, 1 - zh, p, at_c[q]) for i in range(NX) for q in range(NC) if i + q]
    partner = dev(x, y, 1 - zh, p, c)
    y_peers = [(at_y[i], dev_y(at_y[i])) for i in range(1, NY)]
    for _, device in z_peers:
        greet(device)
    for device in far_peers + plane_peers:
        greet(device)
    for j in range(1, NY):
        for i in range(NX):

            @pl.when((at_y[j] == x) | (at_x[i] == y))
            def _():
                for q in range(NC):
                    greet(dev(at_x[i], at_y[j], 1 - zh, p, at_c[q]))

    loads[0].wait()
    loads[1].wait()
    lane = lax.broadcasted_iota(jnp.int32, (1, HD), 1)
    row = jnp.zeros((1, HD), F32)
    for m in range(4):
        for base, ref in ((0, w), (4, g)):
            values = ref[m].astype(F32)
            sums = jnp.sum(values * values, axis=0, keepdims=True)
            row = jnp.where(lane == base + m, jnp.sum(sums, axis=1, keepdims=True), row)
    st_z[z] = row
    loads[2].wait()
    loads[3].wait()
    part = tok[...].astype(F32)
    part_mean = jnp.sum(part, axis=-1, keepdims=True) * (1.0 / width)
    part_square = jnp.sum(jnp.square(part - part_mean), axis=-1, keepdims=True)
    rs[mp] = columns_to_rows(part_mean, part_square)[0:2]
    gx_row = jnp.broadcast_to(gain[...].astype(F32).reshape(1, -1), (8, width))
    gx[ZH] = gx_row

    far_places = jnp.where(x == y, 2 * NX - 1, 3 * NX - 2)
    pl.semaphore_wait(barrier, (n_z - 1) + (n_xyc - 1) + NC * far_places - 1)

    share(st_z, z, [d for _, d in z_peers], st_s.at[0], st_r.at[0])
    share(rs, mp, near_peers + [partner] + far_peers, st_s.at[1], st_r.at[1])
    for k in at_z[::-1]:
        here = (x == y) & (zh == k)

        @pl.when(here)
        def _():
            pltpu.make_async_copy(tok, xraw.at[zh], xw.at[zh]).start()
            pltpu.make_async_copy(gx.at[ZH], gx.at[zh], gr.at[zh]).start()

        @pl.when(jnp.logical_not(here))
        def _():
            remote(tok, xraw.at[zh], xs.at[k], xw.at[zh], dev(y, x, k, p, c)).start()
            remote(gx.at[ZH], gx.at[zh], gs.at[k], gr.at[zh], dev(y, x, k, p, c)).start()

    arrived(st_z, n_z, st_r.at[0])
    st_xyc[xyc] = jnp.sum(st_z[...], axis=0)
    share(st_xyc, xyc, plane_peers, st_s.at[2], st_r.at[2])

    arrived(rs, n_mp, st_r.at[1])
    means = rs[:, 0:1, :]
    mean = jnp.sum(means, axis=0) * (1.0 / n_mp)
    square = jnp.sum(rs[:, 1:2, :], axis=0) + width * jnp.sum(jnp.square(means - mean[None]), axis=0)
    inverse = lax.rsqrt(square * (1.0 / n_feat) + 1e-06)
    mean_col, inv_col = rows_to_columns(mean, inverse)
    normed[...] = (tok[...].astype(F32) - mean_col) * inv_col
    invc[...] = jnp.broadcast_to(inv_col, (HD, HD))
    mi[0] = jnp.concatenate([mean, inverse], axis=0)

    @pl.when(x == y)
    def _():
        pltpu.make_async_copy(mi.at[0], mi.at[1], ms.at[0]).start()

    @pl.when(x != y)
    def _():
        remote(mi.at[0], mi.at[1], ms.at[1], ms.at[0], dev(y, x, zh, p, c)).start()

    arrived(st_xyc, n_xyc, st_r.at[2])
    total = jnp.sum(st_xyc[...], axis=0)
    piece = rows // NH
    for m in range(4):
        ratio = (
            ascent_radius * jnp.sqrt(total[:, m : m + 1]) / (jnp.sqrt(total[:, 4 + m : 5 + m]) + 1e-12)
        )
        shifted = (w[m].astype(F32) + ratio * g[m].astype(F32)).astype(BF16)
        for h in range(NH):
            wall[m, p, h] = shifted[h * piece : (h + 1) * piece]

    pairs = ((3, 0), (1, 2))

    def send_weight(way, m, s, h):
        @pl.when(p < ZL - 1 if way == 0 else p > 0)
        def _():
            block = wall.at[m, s, h]
            remote(
                block, block, ws.at[way, m, s, h], wr.at[m, s, h], dev(x, y, zh, p + 1 - 2 * way, c)
            ).start()

    def send_own(ph):
        for m in pairs[ph]:
            for h in range(NH):
                send_weight(0, m, p, h)
                send_weight(1, m, p, h)

    send_own(0)

    for j in range(ZH * NC):
        pltpu.make_async_copy(
            cot.at[:, pl.ds(pl.multiple_of(y * band + j * width, HD), width)], xc.at[1, j, y], xr.at[1, j, y]
        ).start()

    for i, (k, device) in enumerate(y_peers):
        for j in range(ZH * NC):
            remote(
                cot.at[:, pl.ds(pl.multiple_of(k * band + j * width, HD), width)],
                xc.at[1, j, y],
                cs.at[i, j],
                xr.at[1, j, y],
                device,
            ).start()

    def wait_block(ref, sem):
        pltpu.make_async_copy(ref, ref, sem).wait()

    def send_tokens():
        wait_block(mi.at[1], ms.at[0])
        mean_there, inv_there = rows_to_columns(mi[1, 0:1], mi[1, 1:2])
        for k in range(ZH):
            j = k * NC + c
            block = xc.at[0, j, x]
            wait_block(xraw.at[k], xw.at[k])
            wait_block(gx.at[k], gr.at[k])
            hat = (xraw[k].astype(F32) - mean_there) * inv_there
            xc[0, j, x] = (hat * gx[k, 0:1]).astype(BF16)
            for i, device in enumerate(near_peers):
                remote(block, block, n3s.at[k, i], xr.at[0, j, x], device).start()

    def multiply(m, sel, fresh):
        if fresh:

            def wait_one(i, carry):
                j, tb = lax.div(i, NY), lax.rem(i, NY)

                @pl.when((sel == 1) | (lax.rem(j, NC) != c) | (tb != x))
                def _():
                    wait_block(xc.at[sel, j, tb], xr.at[sel, j, tb])

                return carry

            lax.fori_loop(0, ZH * NC * NY, wait_one, 0)

        columns = wall.shape[4]
        weights = wall[m].reshape(ZL * rows, columns)
        acc = None
        for j in range(ZH * NC):
            left = xc[sel, j].reshape(NY * HD, width)
            term = mm(left, weights[j * width : (j + 1) * width])
            acc = term if acc is None else acc + term
        pf[...] = acc.reshape(NY, HD, columns)
        pown[m] = pf[y]
        psend[m] = pf[...].astype(BF16)
        for i, (k, device) in enumerate(y_peers):
            remote(psend.at[m, k], precv.at[m, y], ps.at[m, i], pr.at[m, y], device).start()

    def phase(ph, middle):
        def hop(t, carry):
            from_low = p - t
            from_high = p + t
            for m in pairs[ph]:
                for h in range(NH):

                    @pl.when(from_low >= 0)
                    def _():
                        wait_block(wall.at[m, from_low, h], wr.at[m, from_low, h])
                        send_weight(0, m, from_low, h)

                    @pl.when(from_high < ZL)
                    def _():
                        wait_block(wall.at[m, from_high, h], wr.at[m, from_high, h])
                        send_weight(1, m, from_high, h)

            return carry

        cut = max(ZL - 2, 2)
        lax.fori_loop(1, cut, hop, 0)
        middle()
        lax.fori_loop(cut, ZL, hop, 0)

    def middle_first():
        send_own(1)
        send_tokens()

    def middle_second():
        multiply(3, 1, True)
        multiply(0, 0, True)

    phase(0, middle_first)
    phase(1, middle_second)
    multiply(1, 0, False)
    multiply(2, 0, False)

    def projected(m):
        value = pown[m]
        for i in range(1, NY):
            k = lax.rem(y + i, NY)
            wait_block(precv.at[m, k], pr.at[m, k])
            value = value + precv[m, k].astype(F32)
        return value

    grad_attn_all = projected(3).astype(BF16)
    query_all = projected(0)
    key_all = projected(1)
    value_all = projected(2).astype(BF16)
    score_scale = HD ** (-0.5)
    for h in range(wall.shape[4] // HD):
        cols = slice(h * HD, (h + 1) * HD)
        q_hat, q_inv = row_norm(query_all[:, cols])
        k_hat, k_inv = row_norm(key_all[:, cols])
        queries, key_rows = q_hat.astype(BF16), k_hat.astype(BF16)
        value_rows, grad_attn = value_all[:, cols], grad_attn_all[:, cols]
        exps = jnp.exp(mm_nt(queries, key_rows) * score_scale)
        probs = exps / jnp.sum(exps, axis=-1, keepdims=True)
        grad_values = mm_tn(probs.astype(BF16), grad_attn)
        grad_probs = mm_nt(grad_attn, value_rows)
        inner = jnp.sum(probs * grad_probs, axis=-1, keepdims=True)
        grad_scores = (probs * (grad_probs - inner) * score_scale).astype(BF16)
        grad_query = mm(grad_scores, key_rows)
        grad_keys = mm_tn(grad_scores, queries)
        grads = (
            row_norm_back(grad_query, q_hat, q_inv).astype(BF16),
            row_norm_back(grad_keys, k_hat, k_inv).astype(BF16),
            grad_values.astype(BF16),
        )
        for m in range(3):
            for r in range(NR):
                dbuf[r, y, m, :, cols] = grads[m][r * half : (r + 1) * half]
    for r in range(NR):
        for i, (_, device) in enumerate(y_peers):
            remote(dbuf.at[r, y], dbuf.at[r, y], ds_.at[r, i], dr.at[r, y], device).start()

    goal = [1 - zh, zh]
    apart = width // rows

    def term_block(side, r, tb, wait):
        if wait:
            wait_block(dbuf.at[r, tb], dr.at[r, tb])
        for half_c in range(NC):
            j = goal[side] * NC + half_c
            acc = None
            for m in range(3):
                weights = wall[m, pl.ds(j * apart, apart)].reshape(width, wall.shape[4])
                term = mm_nt(dbuf[r, tb, m], weights)
                acc = term if acc is None else acc + term
            tbuf[half_c, side, r, tb] = acc.astype(BF16)
        remote(
            tbuf.at[1 - c, side, r, tb], tr.at[side, r, tb], tcs.at[side, r, tb], tcr.at[side, r, tb], other_core
        ).start()

    def add_cores(side, r, tb):
        wait_block(tr.at[side, r, tb], tcr.at[side, r, tb])
        sbuf[side, r, tb] = (tbuf[c, side, r, tb].astype(F32) + tr[side, r, tb].astype(F32)).astype(BF16)

        @pl.when(tb != x)
        def _():
            remote(
                sbuf.at[side, r, tb], sr.at[side, r, x], ss.at[side, r, tb], srs.at[side, r, x], dev(tb, y, zh, p, c)
            ).start()

    other_core = dev(x, y, zh, p, 1 - c)
    order = [0, 1, 3, 2] if NY == 4 else list(range(NY))

    def blocks(side, r):
        before = None
        for i in order:
            tb = at_y[i]
            term_block(side, r, tb, side == 0 and i > 0)
            if before is not None:
                add_cores(side, r, before)
            before = tb
        add_cores(side, r, before)

    firsts, seconds = [0.0] * NR, [0.0] * NR

    def gather_x(side, r):
        k = goal[side]
        value = sbuf[side, r, x].astype(F32)
        for i in range(1, NX):
            wait_block(sr.at[side, r, at_x[i]], srs.at[side, r, at_x[i]])
            value = value + sr[side, r, at_x[i]].astype(F32)
        ubuf[side, r] = value.astype(BF16)
        if side == 0:
            remote(ubuf.at[0, r], ur.at[r, zh], us.at[0, r], urs.at[r, zh], dev(y, x, k, p, c)).start()
        else:

            @pl.when(x == y)
            def _():
                pltpu.make_async_copy(ubuf.at[1, r], ur.at[r, zh], urs.at[r, zh]).start()

            @pl.when(x != y)
            def _():
                remote(ubuf.at[1, r], ur.at[r, zh], us.at[1, r], urs.at[r, zh], dev(y, x, k, p, c)).start()

        tokens_in = xc[0, k * NC + c, x, r * half : (r + 1) * half].astype(F32)
        firsts[r] = firsts[r] + jnp.sum(value * gx[k, 0:1], axis=-1, keepdims=True)
        seconds[r] = seconds[r] + jnp.sum(value * tokens_in, axis=-1, keepdims=True)

    for r in range(NR):
        blocks(0, r)
    for r in range(NR):
        gather_x(0, r)
        blocks(1, r)
    for r in range(NR):
        gather_x(1, r)
    n_sums = NY * ZH * NC
    fb[n_sums] = columns_to_rows(jnp.concatenate(firsts, axis=0), jnp.concatenate(seconds, axis=0))[0:2]
    slot = (y * ZH + zh) * NC + c
    for far in (1, 0):
        for i in range(NX):
            for q in range(NC):
                device = dev(at_x[i], x, at_z[far], p, at_c[q])

                @pl.when((x == y) & (far + i + q == 0))
                def _():
                    pltpu.make_async_copy(fb.at[n_sums], fb.at[slot], st_r.at[4]).start()

                @pl.when((x != y) | (far + i + q > 0))
                def _():
                    remote(
                        fb.at[n_sums], fb.at[slot], fs.at[(far * NX + i) * NC + q], st_r.at[4], device
                    ).start()

    arrived(fb, n_sums + 1, st_r.at[4])
    sums = jnp.sum(fb[0:n_sums], axis=0) * (1.0 / n_feat)
    first, second = rows_to_columns(sums[0:1], sums[1:2])
    for r in range(NR):
        part = slice(r * half, (r + 1) * half)
        share_sum = 0.0
        for k in range(ZH):
            wait_block(ur.at[r, k], urs.at[r, k])
            share_sum = share_sum + ur[r, k].astype(F32)
        upstream = share_sum * gain[...].astype(F32).reshape(1, -1)
        out[part] = ((upstream - first[part] - normed[part] * second[part]) * invc[part, 0:1]).astype(BF16)

    arrived(st_z, n_z, st_s.at[0])
    arrived(rs, n_mp, st_s.at[1])
    arrived(st_xyc, n_xyc, st_s.at[2])
    for k in range(ZH):
        here = (x == y) & (zh == k)

        @pl.when(jnp.logical_not(here))
        def _():
            wait_block(xraw.at[0], xs.at[k])
            wait_block(gx.at[ZH], gs.at[k])

    @pl.when(x != y)
    def _():
        wait_block(mi.at[0], ms.at[1])
        for r in range(NR):
            wait_block(ubuf.at[1, r], us.at[1, r])

    for r in range(NR):
        wait_block(ubuf.at[0, r], us.at[0, r])

    def left_y(i, carry):
        for j in range(ZH * NC):
            wait_block(xc.at[1, j, 0], cs.at[i, j])
        for m in range(4):
            wait_block(psend.at[m, 0], ps.at[m, i])
        for r in range(NR):
            wait_block(dbuf.at[r, 0], ds_.at[r, i])
        return carry

    lax.fori_loop(0, NY - 1, left_y, 0)

    def left_near(i, carry):
        for k in range(ZH):
            wait_block(xc.at[0, 0, 0], n3s.at[k, i])
        return carry

    lax.fori_loop(0, NX * NC - 1, left_near, 0)

    def left_sums(i, carry):
        @pl.when((x != y) | (i > 0))
        def _():
            wait_block(fb.at[0], fs.at[i])

        return carry

    lax.fori_loop(0, ZH * NX * NC, left_sums, 0)

    def left_blocks(tb, carry):
        for side in range(2):
            for r in range(NR):
                wait_block(tr.at[side, r, tb], tcs.at[side, r, tb])

        @pl.when(tb != x)
        def _():
            for side in range(2):
                for r in range(NR):
                    wait_block(sbuf.at[side, r, tb], ss.at[side, r, tb])

        return carry

    lax.fori_loop(0, NY, left_blocks, 0)

    def left_weights(i, carry):
        m, s = lax.div(i, ZL), lax.rem(i, ZL)
        for h in range(NH):

            @pl.when((p < ZL - 1) & (s <= p))
            def _():
                wait_block(wall.at[m, s, h], ws.at[0, m, s, h])

            @pl.when((p > 0) & (s >= p))
            def _():
                wait_block(wall.at[m, s, h], ws.at[1, m, s, h])

        return carry

    lax.fori_loop(0, 4 * ZL, left_weights, 0)


def per_device(tokens, norm_gain, attn_weights, stored_grads, cotangent):
    width = tokens.shape[1]
    _, rows, columns = attn_weights.shape
    n_mp = NX * ZH * NC
    nj = ZH * NC
    dma = pltpu.SemaphoreType.DMA
    vmem = pl.BlockSpec(memory_space=pltpu.VMEM)
    return pl.pallas_call(
        kernel,
        out_shape=jax.ShapeDtypeStruct((HD, width), BF16),
        in_specs=[pl.BlockSpec(memory_space=pltpu.HBM)] * 5,
        out_specs=vmem,
        scratch_shapes=[
            pltpu.VMEM(tokens.shape, BF16),
            pltpu.VMEM((width,), BF16),
            pltpu.VMEM(attn_weights.shape, BF16),
            pltpu.VMEM(attn_weights.shape, BF16),
            pltpu.VMEM((ZH * ZL, 1, HD), F32),
            pltpu.VMEM((NX * NY * NC, 1, HD), F32),
            pltpu.VMEM((n_mp, 2, HD), F32),
            pltpu.VMEM((ZH + 1, 8, width), F32),
            pltpu.VMEM((NY * ZH * NC + 1, 2, HD), F32),
            pltpu.VMEM((2, 2, HD), F32),
            pltpu.VMEM((ZH, HD, width), BF16),
            pltpu.VMEM((HD, width), F32),
            pltpu.VMEM((HD, HD), F32),
            pltpu.VMEM((2, nj, NY, HD, width), BF16),
            pltpu.VMEM((4, ZL, NH, rows // NH, columns), BF16),
            pltpu.VMEM((NY, HD, columns), F32),
            pltpu.VMEM((4, HD, columns), F32),
            pltpu.VMEM((4, NY, HD, columns), BF16),
            pltpu.VMEM((4, NY, HD, columns), BF16),
            pltpu.VMEM((NR, NY, 3, HD // NR, columns), BF16),
            pltpu.VMEM((NC, 2, NR, NY, HD // NR, width), BF16),
            pltpu.VMEM((2, NR, NY, HD // NR, width), BF16),
            pltpu.VMEM((2, NR, NY, HD // NR, width), BF16),
            pltpu.VMEM((2, NR, NX, HD // NR, width), BF16),
            pltpu.VMEM((2, NR, HD // NR, width), BF16),
            pltpu.VMEM((NR, ZH, HD // NR, width), BF16),
            dma((4,)),
            dma((4,)),
            dma((5,)),
            dma((ZH,)),
            dma((ZH,)),
            dma((ZH * NX * NC,)),
            dma((2,)),
            dma((ZH,)),
            dma((ZH,)),
            dma((2, nj, NY)),
            dma((NY, nj)),
            dma((ZH, NX * NC)),
            dma((2, 4, ZL, NH)),
            dma((4, ZL, NH)),
            dma((4, NY)),
            dma((4, NY)),
            dma((NR, NY)),
            dma((NR, NY)),
            dma((2, NR, NY)),
            dma((2, NR, NY)),
            dma((2, NR, NY)),
            dma((2, NR, NX)),
            dma((2, NR)),
            dma((NR, ZH)),
        ],
        compiler_params=pltpu.CompilerParams(
            collective_id=0, has_side_effects=True, vmem_limit_bytes=60 * 1024 * 1024
        ),
    )(tokens, norm_gain, attn_weights, stored_grads, cotangent)


def solution(mesh):
    return jax.shard_map(
        per_device,
        mesh=mesh,
        in_specs=(P("dp", "mp"), P("mp"), P(None, "dp", "mp"), P(None, "dp", "mp"), P("dp", None)),
        out_specs=P("dp", "mp"),
        check_vma=False,
    )
```

```python
import jax
import jax.numpy as jnp
from jax import lax
from jax.experimental import pallas as pl
from jax.experimental.pallas import tpu as pltpu
from jax.sharding import PartitionSpec as P

MESH = pl.DeviceIdType.MESH
F32, BF16 = jnp.float32, jnp.bfloat16
HD = 128
NX, NY, ZH, ZL, NC = 4, 4, 2, 8, 2
NH = 2
EXTRA = 16
NR = 2
ascent_radius = 0.15


def mm(a, b):
    return lax.dot_general(a, b, (((1,), (0,)), ((), ())), preferred_element_type=F32)


def mm_nt(a, b):
    return lax.dot_general(a, b, (((1,), (1,)), ((), ())), preferred_element_type=F32)


def mm_tn(a, b):
    return lax.dot_general(a, b, (((0,), (0,)), ((), ())), preferred_element_type=F32)


def row_norm(matrix):
    center = matrix - jnp.mean(matrix, axis=-1, keepdims=True)
    inverse = lax.rsqrt(jnp.mean(center * center, axis=-1, keepdims=True) + 1e-06)
    return center * inverse, inverse


def row_norm_back(upstream, normed, inverse):
    first_mean = jnp.mean(upstream, axis=-1, keepdims=True)
    second_mean = jnp.mean(upstream * normed, axis=-1, keepdims=True)
    return (upstream - first_mean - normed * second_mean) * inverse


def columns_to_rows(first, second):
    lane = lax.broadcasted_iota(jnp.int32, (HD, HD), 1)
    both = jnp.where(lane == 0, first, jnp.where(lane == 1, second, 0.0))
    return both.T[0:8]


def rows_to_columns(first, second):
    sub = lax.broadcasted_iota(jnp.int32, (HD, HD), 0)
    both = jnp.where(sub == 0, first, jnp.where(sub == 1, second, 0.0))
    turned = both.T
    return turned[:, 0:1], turned[:, 1:2]


def kernel(
    tok_hbm, gain_hbm, w_hbm, g_hbm, cot, out,
    tok, gain, w, g,
    st_z, st_xyc, rs, gx, fin, mi, xraw, normed, invc, xc, wall, pf, pown, psend, precv, dbuf, tbuf, tr, sbuf, sr, ubuf, ur,
    ins, st_s, st_r, gs, gr, ms, xs, xw, xr, cs, n3s, ws, wr, ps, pr, ds_, dr, tcs, tcr, ss, srs, us, urs,
):
    n_mp = NX * ZH * NC
    n_z = ZH * ZL
    width = tok.shape[1]
    band = ZH * NC * width
    n_feat = n_mp * width
    rows = w.shape[1]
    dp = lax.axis_index("dp")
    mp = lax.axis_index("mp")
    y, p = lax.div(dp, ZL), lax.rem(dp, ZL)
    x, c = lax.div(mp, ZH * NC), lax.rem(mp, NC)
    zh = lax.rem(lax.div(mp, NC), ZH)
    z = zh * ZL + p
    xcore = x * NC + c
    xyc = y * NX * NC + xcore
    half = HD // NR
    n_xyc = NX * NY * NC

    def dev(x_, y_, zh_, p_, c_):
        return (y_ * ZL + p_, (x_ * ZH + zh_) * NC + c_)

    def dev_z(k):
        return dev(x, y, lax.div(k, ZL), lax.rem(k, ZL), c)

    def dev_y(k):
        return dev(x, k, zh, p, c)

    def remote(src, dst, ssem, rsem, device):
        return pltpu.make_async_remote_copy(
            src_ref=src, dst_ref=dst, send_sem=ssem, recv_sem=rsem, device_id=device, device_id_type=MESH
        )

    def token_rows(sel, j, tb):
        return xc.at[sel, j, pl.ds(pl.multiple_of(tb * HD, HD), HD)]

    def share(buf, mine, peers, ssem, rsem):
        for device in peers:
            remote(buf.at[mine], buf.at[mine], ssem, rsem, device).start()

    def arrived(buf, n, sem):
        part = buf.at[pl.ds(0, n - 1)]
        pltpu.make_async_copy(part, part, sem).wait()

    loads = [
        pltpu.make_async_copy(src, dst, ins.at[i])
        for i, (src, dst) in enumerate(((w_hbm, w), (g_hbm, g), (tok_hbm, tok), (gain_hbm, gain)))
    ]
    for load in loads:
        load.start()

    barrier = pltpu.get_barrier_semaphore()

    def greet(device):
        pl.semaphore_signal(barrier, inc=1, device_id=device, device_id_type=MESH)

    z_peers = []
    for i in range(1, n_z):
        k = lax.rem(z + i, n_z)
        z_peers.append((k, dev_z(k)))
    at_x = [lax.rem(x + i, NX) for i in range(NX)]
    at_y = [lax.rem(y + i, NY) for i in range(NY)]
    at_c = [c, 1 - c]
    at_z = [zh, 1 - zh]
    plane_peers = [
        dev(at_x[i], at_y[j], zh, p, at_c[q]) for j in range(NY) for i in range(NX) for q in range(NC) if i + j + q
    ]
    near_peers = [dev(at_x[i], y, zh, p, at_c[q]) for i in range(NX) for q in range(NC) if i + q]
    far_peers = [dev(at_x[i], y, 1 - zh, p, at_c[q]) for i in range(NX) for q in range(NC) if i + q]
    partner = dev(x, y, 1 - zh, p, c)
    y_peers = [(at_y[i], dev_y(at_y[i])) for i in range(1, NY)]
    for _, device in z_peers:
        greet(device)
    for device in far_peers + plane_peers:
        greet(device)

    @pl.when(x != y)
    def _():
        greet(dev(y, x, 1 - zh, p, c))

    loads[0].wait()
    loads[1].wait()
    lane = lax.broadcasted_iota(jnp.int32, (1, HD), 1)
    row = jnp.zeros((1, HD), F32)
    for m in range(4):
        for base, ref in ((0, w), (4, g)):
            values = ref[m].astype(F32)
            sums = jnp.sum(values * values, axis=0, keepdims=True)
            row = jnp.where(lane == base + m, jnp.sum(sums, axis=1, keepdims=True), row)
    st_z[z] = row
    loads[2].wait()
    loads[3].wait()
    part = tok[...].astype(F32)
    part_mean = jnp.sum(part, axis=-1, keepdims=True) * (1.0 / width)
    part_square = jnp.sum(jnp.square(part - part_mean), axis=-1, keepdims=True)
    rs[mp] = columns_to_rows(part_mean, part_square)[0:2]
    gx[ZH * NC] = gain[...].astype(F32).reshape(1, -1)
    for j in range(ZH * NC):
        xc[1, j, NY * HD :] = jnp.zeros((EXTRA, width), BF16)

    pl.semaphore_wait(
        barrier, (n_z - 1) + (n_xyc - 1) + (ZH - 1) * (NX * NC - 1) + jnp.where(x != y, ZH - 1, 0)
    )

    share(st_z, z, [d for _, d in z_peers], st_s.at[0], st_r.at[0])
    share(rs, mp, near_peers + [partner] + far_peers, st_s.at[1], st_r.at[1])
    arrived(st_z, n_z, st_r.at[0])
    st_xyc[xyc] = jnp.sum(st_z[...], axis=0)
    share(st_xyc, xyc, plane_peers, st_s.at[2], st_r.at[2])

    for k in at_z[::-1]:
        here = (x == y) & (zh == k)

        @pl.when(here)
        def _():
            pltpu.make_async_copy(tok, xraw.at[zh], xw.at[zh]).start()

        @pl.when(jnp.logical_not(here))
        def _():
            remote(tok, xraw.at[zh], xs.at[k], xw.at[zh], dev(y, x, k, p, c)).start()

    arrived(rs, n_mp, st_r.at[1])
    means = rs[:, 0:1, :]
    mean = jnp.sum(means, axis=0) * (1.0 / n_mp)
    square = jnp.sum(rs[:, 1:2, :], axis=0) + width * jnp.sum(jnp.square(means - mean[None]), axis=0)
    inverse = lax.rsqrt(square * (1.0 / n_feat) + 1e-06)
    mean_col, inv_col = rows_to_columns(mean, inverse)
    normed[...] = (tok[...].astype(F32) - mean_col) * inv_col
    invc[...] = jnp.broadcast_to(inv_col, (HD, HD))
    mi[0] = jnp.concatenate([mean, inverse], axis=0)

    @pl.when(x == y)
    def _():
        pltpu.make_async_copy(mi.at[0], mi.at[1], ms.at[0]).start()

    @pl.when(x != y)
    def _():
        remote(mi.at[0], mi.at[1], ms.at[1], ms.at[0], dev(y, x, zh, p, c)).start()

    arrived(st_xyc, n_xyc, st_r.at[2])
    total = jnp.sum(st_xyc[...], axis=0)
    piece = rows // NH
    for m in range(4):
        ratio = (
            ascent_radius * jnp.sqrt(total[:, m : m + 1]) / (jnp.sqrt(total[:, 4 + m : 5 + m]) + 1e-12)
        )
        shifted = (w[m].astype(F32) + ratio * g[m].astype(F32)).astype(BF16)
        for h in range(NH):
            wall[m, p, h] = shifted[h * piece : (h + 1) * piece]

    pairs = ((3, 0), (1, 2))

    def send_weight(way, m, s, h):
        @pl.when(p < ZL - 1 if way == 0 else p > 0)
        def _():
            block = wall.at[m, s, h]
            remote(
                block, block, ws.at[way, m, s, h], wr.at[m, s, h], dev(x, y, zh, p + 1 - 2 * way, c)
            ).start()

    def send_own(ph):
        for m in pairs[ph]:
            for h in range(NH):
                send_weight(0, m, p, h)
                send_weight(1, m, p, h)

    send_own(0)

    mp_peers = near_peers + [partner] + far_peers

    @pl.when(x == y)
    def _():
        slot = zh * NC + c
        pltpu.make_async_copy(gx.at[ZH * NC], gx.at[slot], gr.at[0]).start()
        for i, device in enumerate(mp_peers):
            remote(gx.at[ZH * NC], gx.at[slot], gs.at[i], gr.at[0], device).start()

    for j in range(ZH * NC):
        pltpu.make_async_copy(
            cot.at[:, pl.ds(pl.multiple_of(y * band + j * width, HD), width)], token_rows(1, j, y), xr.at[1, j, y]
        ).start()

    for i, (k, device) in enumerate(y_peers):
        for j in range(ZH * NC):
            remote(
                cot.at[:, pl.ds(pl.multiple_of(k * band + j * width, HD), width)],
                token_rows(1, j, y),
                cs.at[i, j],
                xr.at[1, j, y],
                device,
            ).start()

    def wait_block(ref, sem):
        pltpu.make_async_copy(ref, ref, sem).wait()

    def send_tokens():
        wait_block(mi.at[1], ms.at[0])
        arrived(gx, ZH * NC + 1, gr.at[0])
        for j in range(ZH * NC):
            xc[0, j, NY * HD :] = jnp.broadcast_to(gx[j], (EXTRA, width)).astype(BF16)
        mean_there, inv_there = rows_to_columns(mi[1, 0:1], mi[1, 1:2])
        for k in range(ZH):
            j = k * NC + c
            block = token_rows(0, j, x)
            wait_block(xraw.at[k], xw.at[k])
            hat = (xraw[k].astype(F32) - mean_there) * inv_there
            block[...] = (hat * gx[j]).astype(BF16)
            for i, device in enumerate(near_peers):
                remote(block, block, n3s.at[k, i], xr.at[0, j, x], device).start()

    def multiply(m, sel, fresh):
        if fresh:

            def wait_one(i, carry):
                j, tb = lax.div(i, NY), lax.rem(i, NY)

                @pl.when((sel == 1) | (lax.rem(j, NC) != c) | (tb != x))
                def _():
                    wait_block(token_rows(sel, j, tb), xr.at[sel, j, tb])

                return carry

            lax.fori_loop(0, ZH * NC * NY, wait_one, 0)

        columns = wall.shape[4]
        weights = wall[m].reshape(ZL * rows, columns)
        acc = None
        for j in range(ZH * NC):
            term = mm(xc[sel, j], weights[j * width : (j + 1) * width])
            acc = term if acc is None else acc + term
        for k in range(NY):
            pf[k, 0:HD] = acc[k * HD : (k + 1) * HD]
            pf[k, HD:] = acc[NY * HD :]
        pown[m] = pf[y]
        psend[m] = pf[...].astype(BF16)
        for i, (k, device) in enumerate(y_peers):
            remote(psend.at[m, k], precv.at[m, y], ps.at[m, i], pr.at[m, y], device).start()

    def phase(ph, middle):
        def hop(t, carry):
            from_low = p - t
            from_high = p + t
            for m in pairs[ph]:
                for h in range(NH):

                    @pl.when(from_low >= 0)
                    def _():
                        wait_block(wall.at[m, from_low, h], wr.at[m, from_low, h])
                        send_weight(0, m, from_low, h)

                    @pl.when(from_high < ZL)
                    def _():
                        wait_block(wall.at[m, from_high, h], wr.at[m, from_high, h])
                        send_weight(1, m, from_high, h)

            return carry

        cut = max(ZL - 2, 2)
        lax.fori_loop(1, cut, hop, 0)
        middle()
        lax.fori_loop(cut, ZL, hop, 0)

    def middle_first():
        send_own(1)
        send_tokens()

    def middle_second():
        multiply(3, 1, True)
        multiply(0, 0, True)

    phase(0, middle_first)
    phase(1, middle_second)
    multiply(1, 0, False)
    multiply(2, 0, False)

    def projected(m):
        value = pown[m]
        for i in range(1, NY):
            k = lax.rem(y + i, NY)
            wait_block(precv.at[m, k], pr.at[m, k])
            value = value + precv[m, k].astype(F32)
        return value

    grad_attn_all = projected(3)[0:HD].astype(BF16)
    whole = [projected(m) for m in range(3)]
    query_all, key_all = whole[0][0:HD], whole[1][0:HD]
    value_all = whole[2][0:HD].astype(BF16)
    first_col, second_col = 0.0, 0.0
    score_scale = HD ** (-0.5)
    for h in range(wall.shape[4] // HD):
        cols = slice(h * HD, (h + 1) * HD)
        q_hat, q_inv = row_norm(query_all[:, cols])
        k_hat, k_inv = row_norm(key_all[:, cols])
        queries, key_rows = q_hat.astype(BF16), k_hat.astype(BF16)
        value_rows, grad_attn = value_all[:, cols], grad_attn_all[:, cols]
        exps = jnp.exp(mm_nt(queries, key_rows) * score_scale)
        probs = exps / jnp.sum(exps, axis=-1, keepdims=True)
        grad_values = mm_tn(probs.astype(BF16), grad_attn)
        grad_probs = mm_nt(grad_attn, value_rows)
        inner = jnp.sum(probs * grad_probs, axis=-1, keepdims=True)
        grad_scores = (probs * (grad_probs - inner) * score_scale).astype(BF16)
        grad_query = mm(grad_scores, key_rows)
        grad_keys = mm_tn(grad_scores, queries)
        grads = (
            row_norm_back(grad_query, q_hat, q_inv).astype(BF16),
            row_norm_back(grad_keys, k_hat, k_inv).astype(BF16),
            grad_values.astype(BF16),
        )
        for m in range(3):
            grad = grads[m].astype(F32)
            first_col = first_col + jnp.sum(grad * whole[m][HD : HD + 1, cols], axis=-1, keepdims=True)
            second_col = second_col + jnp.sum(grad * whole[m][0:HD, cols], axis=-1, keepdims=True)
        for m in range(3):
            for r in range(NR):
                dbuf[r, y, m, :, cols] = grads[m][r * half : (r + 1) * half]
    for r in range(NR):
        for i, (_, device) in enumerate(y_peers):
            remote(dbuf.at[r, y], dbuf.at[r, y], ds_.at[r, i], dr.at[r, y], device).start()

    fin[mp] = columns_to_rows(first_col, second_col)[0:2]
    share(fin, mp, near_peers + [partner] + far_peers, st_s.at[3], st_r.at[3])

    goal = [1 - zh, zh]
    apart = width // rows

    def term_block(side, r, tb, wait):
        if wait:
            wait_block(dbuf.at[r, tb], dr.at[r, tb])
        for half_c in range(NC):
            j = goal[side] * NC + half_c
            acc = None
            for m in range(3):
                weights = wall[m, pl.ds(j * apart, apart)].reshape(width, wall.shape[4])
                term = mm_nt(dbuf[r, tb, m], weights)
                acc = term if acc is None else acc + term
            tbuf[half_c, side, r, tb] = acc.astype(BF16)
        remote(
            tbuf.at[1 - c, side, r, tb], tr.at[side, r, tb], tcs.at[side, r, tb], tcr.at[side, r, tb], other_core
        ).start()

    def add_cores(side, r, tb):
        wait_block(tr.at[side, r, tb], tcr.at[side, r, tb])
        sbuf[side, r, tb] = (tbuf[c, side, r, tb].astype(F32) + tr[side, r, tb].astype(F32)).astype(BF16)

        @pl.when(tb != x)
        def _():
            remote(
                sbuf.at[side, r, tb], sr.at[side, r, x], ss.at[side, r, tb], srs.at[side, r, x], dev(tb, y, zh, p, c)
            ).start()

    other_core = dev(x, y, zh, p, 1 - c)
    order = [0, 1, 3, 2] if NY == 4 else list(range(NY))

    def blocks(side, r):
        before = None
        for i in order:
            tb = at_y[i]
            term_block(side, r, tb, side == 0 and i > 0)
            if before is not None:
                add_cores(side, r, before)
            before = tb
        add_cores(side, r, before)

    def gather_x(side, r):
        k = goal[side]
        value = sbuf[side, r, x].astype(F32)
        for i in range(1, NX):
            wait_block(sr.at[side, r, at_x[i]], srs.at[side, r, at_x[i]])
            value = value + sr[side, r, at_x[i]].astype(F32)
        ubuf[side, r] = value.astype(BF16)
        if side == 0:
            remote(ubuf.at[0, r], ur.at[r, zh], us.at[0, r], urs.at[r, zh], dev(y, x, k, p, c)).start()
        else:

            @pl.when(x == y)
            def _():
                pltpu.make_async_copy(ubuf.at[1, r], ur.at[r, zh], urs.at[r, zh]).start()

            @pl.when(x != y)
            def _():
                remote(ubuf.at[1, r], ur.at[r, zh], us.at[1, r], urs.at[r, zh], dev(y, x, k, p, c)).start()

    for r in range(NR):
        blocks(0, r)
    for r in range(NR):
        gather_x(0, r)
        blocks(1, r)
    for r in range(NR):
        gather_x(1, r)
    arrived(fin, n_mp, st_r.at[3])
    sums = jnp.sum(fin[...], axis=0) * (1.0 / n_feat)
    first, second = rows_to_columns(sums[0:1], sums[1:2])
    for r in range(NR):
        part = slice(r * half, (r + 1) * half)
        share_sum = 0.0
        for k in range(ZH):
            wait_block(ur.at[r, k], urs.at[r, k])
            share_sum = share_sum + ur[r, k].astype(F32)
        upstream = share_sum * gain[...].astype(F32).reshape(1, -1)
        out[part] = ((upstream - first[part] - normed[part] * second[part]) * invc[part, 0:1]).astype(BF16)

    arrived(st_z, n_z, st_s.at[0])
    arrived(rs, n_mp, st_s.at[1])
    arrived(st_xyc, n_xyc, st_s.at[2])
    arrived(fin, n_mp, st_s.at[3])
    for k in range(ZH):
        here = (x == y) & (zh == k)

        @pl.when(jnp.logical_not(here))
        def _():
            wait_block(xraw.at[0], xs.at[k])

    @pl.when(x != y)
    def _():
        wait_block(mi.at[0], ms.at[1])
        for r in range(NR):
            wait_block(ubuf.at[1, r], us.at[1, r])

    for r in range(NR):
        wait_block(ubuf.at[0, r], us.at[0, r])

    def left_y(i, carry):
        for j in range(ZH * NC):
            wait_block(token_rows(1, j, 0), cs.at[i, j])
        for m in range(4):
            wait_block(psend.at[m, 0], ps.at[m, i])
        for r in range(NR):
            wait_block(dbuf.at[r, 0], ds_.at[r, i])
        return carry

    lax.fori_loop(0, NY - 1, left_y, 0)

    def left_near(i, carry):
        for k in range(ZH):
            wait_block(token_rows(0, 0, 0), n3s.at[k, i])
        return carry

    lax.fori_loop(0, NX * NC - 1, left_near, 0)

    @pl.when(x == y)
    def _():
        for i in range(n_mp - 1):
            wait_block(gx.at[0], gs.at[i])

    def left_blocks(tb, carry):
        for side in range(2):
            for r in range(NR):
                wait_block(tr.at[side, r, tb], tcs.at[side, r, tb])

        @pl.when(tb != x)
        def _():
            for side in range(2):
                for r in range(NR):
                    wait_block(sbuf.at[side, r, tb], ss.at[side, r, tb])

        return carry

    lax.fori_loop(0, NY, left_blocks, 0)

    def left_weights(i, carry):
        m, s = lax.div(i, ZL), lax.rem(i, ZL)
        for h in range(NH):

            @pl.when((p < ZL - 1) & (s <= p))
            def _():
                wait_block(wall.at[m, s, h], ws.at[0, m, s, h])

            @pl.when((p > 0) & (s >= p))
            def _():
                wait_block(wall.at[m, s, h], ws.at[1, m, s, h])

        return carry

    lax.fori_loop(0, 4 * ZL, left_weights, 0)


def per_device(tokens, norm_gain, attn_weights, stored_grads, cotangent):
    width = tokens.shape[1]
    _, rows, columns = attn_weights.shape
    n_mp = NX * ZH * NC
    nj = ZH * NC
    dma = pltpu.SemaphoreType.DMA
    vmem = pl.BlockSpec(memory_space=pltpu.VMEM)
    return pl.pallas_call(
        kernel,
        out_shape=jax.ShapeDtypeStruct((HD, width), BF16),
        in_specs=[pl.BlockSpec(memory_space=pltpu.HBM)] * 5,
        out_specs=vmem,
        scratch_shapes=[
            pltpu.VMEM(tokens.shape, BF16),
            pltpu.VMEM((width,), BF16),
            pltpu.VMEM(attn_weights.shape, BF16),
            pltpu.VMEM(attn_weights.shape, BF16),
            pltpu.VMEM((ZH * ZL, 1, HD), F32),
            pltpu.VMEM((NX * NY * NC, 1, HD), F32),
            pltpu.VMEM((n_mp, 2, HD), F32),
            pltpu.VMEM((ZH * NC + 1, 1, width), F32),
            pltpu.VMEM((n_mp, 2, HD), F32),
            pltpu.VMEM((2, 2, HD), F32),
            pltpu.VMEM((ZH, HD, width), BF16),
            pltpu.VMEM((HD, width), F32),
            pltpu.VMEM((HD, HD), F32),
            pltpu.VMEM((2, nj, NY * HD + EXTRA, width), BF16),
            pltpu.VMEM((4, ZL, NH, rows // NH, columns), BF16),
            pltpu.VMEM((NY, HD + EXTRA, columns), F32),
            pltpu.VMEM((4, HD + EXTRA, columns), F32),
            pltpu.VMEM((4, NY, HD + EXTRA, columns), BF16),
            pltpu.VMEM((4, NY, HD + EXTRA, columns), BF16),
            pltpu.VMEM((NR, NY, 3, HD // NR, columns), BF16),
            pltpu.VMEM((NC, 2, NR, NY, HD // NR, width), BF16),
            pltpu.VMEM((2, NR, NY, HD // NR, width), BF16),
            pltpu.VMEM((2, NR, NY, HD // NR, width), BF16),
            pltpu.VMEM((2, NR, NX, HD // NR, width), BF16),
            pltpu.VMEM((2, NR, HD // NR, width), BF16),
            pltpu.VMEM((NR, ZH, HD // NR, width), BF16),
            dma((4,)),
            dma((4,)),
            dma((4,)),
            dma((n_mp - 1,)),
            dma((1,)),
            dma((2,)),
            dma((ZH,)),
            dma((ZH,)),
            dma((2, nj, NY)),
            dma((NY, nj)),
            dma((ZH, NX * NC)),
            dma((2, 4, ZL, NH)),
            dma((4, ZL, NH)),
            dma((4, NY)),
            dma((4, NY)),
            dma((NR, NY)),
            dma((NR, NY)),
            dma((2, NR, NY)),
            dma((2, NR, NY)),
            dma((2, NR, NY)),
            dma((2, NR, NX)),
            dma((2, NR)),
            dma((NR, ZH)),
        ],
        compiler_params=pltpu.CompilerParams(
            collective_id=0, has_side_effects=True, vmem_limit_bytes=60 * 1024 * 1024
        ),
    )(tokens, norm_gain, attn_weights, stored_grads, cotangent)


def solution(mesh):
    return jax.shard_map(
        per_device,
        mesh=mesh,
        in_specs=(P("dp", "mp"), P("mp"), P(None, "dp", "mp"), P(None, "dp", "mp"), P("dp", None)),
        out_specs=P("dp", "mp"),
        check_vma=False,
    )
```

```python
import jax
import jax.numpy as jnp
from jax import lax
from jax.experimental import pallas as pl
from jax.experimental.pallas import tpu as pltpu
from jax.sharding import PartitionSpec as P

MESH = pl.DeviceIdType.MESH
F32, BF16 = jnp.float32, jnp.bfloat16
HD = 128
NX, NY, ZH, ZL, NC = 4, 4, 2, 8, 2
NH = 2
EXTRA = 16
NR = 2
ascent_radius = 0.15


def mm(a, b):
    return lax.dot_general(a, b, (((1,), (0,)), ((), ())), preferred_element_type=F32)


def mm_nt(a, b):
    return lax.dot_general(a, b, (((1,), (1,)), ((), ())), preferred_element_type=F32)


def mm_tn(a, b):
    return lax.dot_general(a, b, (((0,), (0,)), ((), ())), preferred_element_type=F32)


def row_norm(matrix):
    center = matrix - jnp.mean(matrix, axis=-1, keepdims=True)
    inverse = lax.rsqrt(jnp.mean(center * center, axis=-1, keepdims=True) + 1e-06)
    return center * inverse, inverse


def row_norm_back(upstream, normed, inverse):
    first_mean = jnp.mean(upstream, axis=-1, keepdims=True)
    second_mean = jnp.mean(upstream * normed, axis=-1, keepdims=True)
    return (upstream - first_mean - normed * second_mean) * inverse


def columns_to_rows(first, second):
    lane = lax.broadcasted_iota(jnp.int32, (HD, HD), 1)
    both = jnp.where(lane == 0, first, jnp.where(lane == 1, second, 0.0))
    return both.T[0:8]


def rows_to_columns(first, second):
    sub = lax.broadcasted_iota(jnp.int32, (HD, HD), 0)
    both = jnp.where(sub == 0, first, jnp.where(sub == 1, second, 0.0))
    turned = both.T
    return turned[:, 0:1], turned[:, 1:2]


def kernel(
    tok_hbm, gain_hbm, w_hbm, g_hbm, cot, out,
    tok, gain, w, g,
    st_z, st_xyc, rs, gx, fin, mi, xraw, normed, invc, xc, wall, pf, pown, psend, precv, dbuf, tbuf, tr, sbuf, sr, ubuf, ur,
    ins, st_s, st_r, gs, gr, ms, xs, xw, xr, cs, n3s, ws, wr, ps, pr, ds_, dr, tcs, tcr, ss, srs, us, urs,
):
    n_mp = NX * ZH * NC
    n_z = ZH * ZL
    width = tok.shape[1]
    band = ZH * NC * width
    n_feat = n_mp * width
    rows = w.shape[1]
    dp = lax.axis_index("dp")
    mp = lax.axis_index("mp")
    y, p = lax.div(dp, ZL), lax.rem(dp, ZL)
    x, c = lax.div(mp, ZH * NC), lax.rem(mp, NC)
    zh = lax.rem(lax.div(mp, NC), ZH)
    z = zh * ZL + p
    xcore = x * NC + c
    xyc = y * NX * NC + xcore
    half = HD // NR
    n_xyc = NX * NY * NC

    def dev(x_, y_, zh_, p_, c_):
        return (y_ * ZL + p_, (x_ * ZH + zh_) * NC + c_)

    def dev_z(k):
        return dev(x, y, lax.div(k, ZL), lax.rem(k, ZL), c)

    def dev_y(k):
        return dev(x, k, zh, p, c)

    def remote(src, dst, ssem, rsem, device):
        return pltpu.make_async_remote_copy(
            src_ref=src, dst_ref=dst, send_sem=ssem, recv_sem=rsem, device_id=device, device_id_type=MESH
        )

    def token_rows(sel, j, tb):
        return xc.at[sel, j, pl.ds(pl.multiple_of(tb * HD, HD), HD)]

    def share(buf, mine, peers, ssem, rsem):
        for device in peers:
            remote(buf.at[mine], buf.at[mine], ssem, rsem, device).start()

    def arrived(buf, n, sem):
        part = buf.at[pl.ds(0, n - 1)]
        pltpu.make_async_copy(part, part, sem).wait()

    loads = [
        pltpu.make_async_copy(src, dst, ins.at[i])
        for i, (src, dst) in enumerate(((w_hbm, w), (g_hbm, g), (tok_hbm, tok), (gain_hbm, gain)))
    ]
    for load in loads:
        load.start()

    barrier = pltpu.get_barrier_semaphore()

    def greet(device):
        pl.semaphore_signal(barrier, inc=1, device_id=device, device_id_type=MESH)

    z_peers = []
    for i in range(1, n_z):
        k = lax.rem(z + i, n_z)
        z_peers.append((k, dev_z(k)))
    at_x = [lax.rem(x + i, NX) for i in range(NX)]
    at_y = [lax.rem(y + i, NY) for i in range(NY)]
    at_c = [c, 1 - c]
    at_z = [zh, 1 - zh]
    plane_peers = [
        dev(at_x[i], at_y[j], zh, p, at_c[q]) for j in range(NY) for i in range(NX) for q in range(NC) if i + j + q
    ]
    near_peers = [dev(at_x[i], y, zh, p, at_c[q]) for i in range(NX) for q in range(NC) if i + q]
    far_peers = [dev(at_x[i], y, 1 - zh, p, at_c[q]) for i in range(NX) for q in range(NC) if i + q]
    partner = dev(x, y, 1 - zh, p, c)
    y_peers = [(at_y[i], dev_y(at_y[i])) for i in range(1, NY)]
    for _, device in z_peers:
        greet(device)
    for device in far_peers + plane_peers:
        greet(device)

    @pl.when(x != y)
    def _():
        greet(dev(y, x, 1 - zh, p, c))

    loads[0].wait()
    loads[1].wait()
    lane = lax.broadcasted_iota(jnp.int32, (1, HD), 1)
    row = jnp.zeros((1, HD), F32)
    for m in range(4):
        for base, ref in ((0, w), (4, g)):
            values = ref[m].astype(F32)
            sums = jnp.sum(values * values, axis=0, keepdims=True)
            row = jnp.where(lane == base + m, jnp.sum(sums, axis=1, keepdims=True), row)
    st_z[z] = row
    loads[2].wait()
    loads[3].wait()
    part = tok[...].astype(F32)
    part_mean = jnp.sum(part, axis=-1, keepdims=True) * (1.0 / width)
    part_square = jnp.sum(jnp.square(part - part_mean), axis=-1, keepdims=True)
    rs[mp] = columns_to_rows(part_mean, part_square)[0:2]
    gx[ZH * NC] = gain[...].astype(F32).reshape(1, -1)
    for j in range(ZH * NC):
        xc[1, j, NY * HD :] = jnp.zeros((EXTRA, width), BF16)

    pl.semaphore_wait(
        barrier, (n_z - 1) + (n_xyc - 1) + (ZH - 1) * (NX * NC - 1) + jnp.where(x != y, ZH - 1, 0)
    )

    share(st_z, z, [d for _, d in z_peers], st_s.at[0], st_r.at[0])
    share(rs, mp, near_peers + [partner] + far_peers, st_s.at[1], st_r.at[1])
    arrived(st_z, n_z, st_r.at[0])
    st_xyc[xyc] = jnp.sum(st_z[...], axis=0)
    share(st_xyc, xyc, plane_peers, st_s.at[2], st_r.at[2])

    for k in at_z[::-1]:
        here = (x == y) & (zh == k)

        @pl.when(here)
        def _():
            pltpu.make_async_copy(tok, xraw.at[zh], xw.at[zh]).start()

        @pl.when(jnp.logical_not(here))
        def _():
            remote(tok, xraw.at[zh], xs.at[k], xw.at[zh], dev(y, x, k, p, c)).start()

    arrived(rs, n_mp, st_r.at[1])
    means = rs[:, 0:1, :]
    mean = jnp.sum(means, axis=0) * (1.0 / n_mp)
    square = jnp.sum(rs[:, 1:2, :], axis=0) + width * jnp.sum(jnp.square(means - mean[None]), axis=0)
    inverse = lax.rsqrt(square * (1.0 / n_feat) + 1e-06)
    mean_col, inv_col = rows_to_columns(mean, inverse)
    normed[...] = (tok[...].astype(F32) - mean_col) * inv_col
    invc[...] = jnp.broadcast_to(inv_col, (HD, HD))
    mi[0] = jnp.concatenate([mean, inverse], axis=0)

    @pl.when(x == y)
    def _():
        pltpu.make_async_copy(mi.at[0], mi.at[1], ms.at[0]).start()

    @pl.when(x != y)
    def _():
        remote(mi.at[0], mi.at[1], ms.at[1], ms.at[0], dev(y, x, zh, p, c)).start()

    arrived(st_xyc, n_xyc, st_r.at[2])
    total = jnp.sum(st_xyc[...], axis=0)
    piece = rows // NH
    for m in range(4):
        ratio = (
            ascent_radius * jnp.sqrt(total[:, m : m + 1]) / (jnp.sqrt(total[:, 4 + m : 5 + m]) + 1e-12)
        )
        shifted = (w[m].astype(F32) + ratio * g[m].astype(F32)).astype(BF16)
        for h in range(NH):
            wall[m, p, h] = shifted[h * piece : (h + 1) * piece]

    pairs = ((3, 0), (1, 2))

    def send_weight(way, m, s, h):
        @pl.when(p < ZL - 1 if way == 0 else p > 0)
        def _():
            block = wall.at[m, s, h]
            remote(
                block, block, ws.at[way, m, s, h], wr.at[m, s, h], dev(x, y, zh, p + 1 - 2 * way, c)
            ).start()

    def send_own(ph):
        for m in pairs[ph]:
            for h in range(NH):
                send_weight(0, m, p, h)
                send_weight(1, m, p, h)

    send_own(0)

    mp_peers = near_peers + [partner] + far_peers

    @pl.when(x == y)
    def _():
        slot = zh * NC + c
        pltpu.make_async_copy(gx.at[ZH * NC], gx.at[slot], gr.at[0]).start()
        for i, device in enumerate(mp_peers):
            remote(gx.at[ZH * NC], gx.at[slot], gs.at[i], gr.at[0], device).start()

    for j in range(ZH * NC):
        pltpu.make_async_copy(
            cot.at[:, pl.ds(pl.multiple_of(y * band + j * width, HD), width)], token_rows(1, j, y), xr.at[1, j, y]
        ).start()

    for i, (k, device) in enumerate(y_peers):
        for j in range(ZH * NC):
            remote(
                cot.at[:, pl.ds(pl.multiple_of(k * band + j * width, HD), width)],
                token_rows(1, j, y),
                cs.at[i, j],
                xr.at[1, j, y],
                device,
            ).start()

    def wait_block(ref, sem):
        pltpu.make_async_copy(ref, ref, sem).wait()

    def send_tokens():
        wait_block(mi.at[1], ms.at[0])
        arrived(gx, ZH * NC + 1, gr.at[0])
        for j in range(ZH * NC):
            xc[0, j, NY * HD :] = jnp.broadcast_to(gx[j], (EXTRA, width)).astype(BF16)
        mean_there, inv_there = rows_to_columns(mi[1, 0:1], mi[1, 1:2])
        for k in range(ZH):
            j = k * NC + c
            block = token_rows(0, j, x)
            wait_block(xraw.at[k], xw.at[k])
            hat = (xraw[k].astype(F32) - mean_there) * inv_there
            block[...] = (hat * gx[j]).astype(BF16)
            for i, device in enumerate(near_peers):
                remote(block, block, n3s.at[k, i], xr.at[0, j, x], device).start()

    def multiply(m, sel, fresh):
        if fresh:

            def wait_one(i, carry):
                j, tb = lax.div(i, NY), lax.rem(i, NY)

                @pl.when((sel == 1) | (lax.rem(j, NC) != c) | (tb != x))
                def _():
                    wait_block(token_rows(sel, j, tb), xr.at[sel, j, tb])

                return carry

            lax.fori_loop(0, ZH * NC * NY, wait_one, 0)

        columns = wall.shape[4]
        weights = wall[m].reshape(ZL * rows, columns)
        acc = None
        for j in range(ZH * NC):
            term = mm(xc[sel, j], weights[j * width : (j + 1) * width])
            acc = term if acc is None else acc + term
        for k in range(NY):
            pf[k, 0:HD] = acc[k * HD : (k + 1) * HD]
            pf[k, HD:] = acc[NY * HD :]
        pown[m] = pf[y]
        psend[m] = pf[...].astype(BF16)
        for i, (k, device) in enumerate(y_peers):
            remote(psend.at[m, k], precv.at[m, y], ps.at[m, i], pr.at[m, y], device).start()

    def phase(ph, middle):
        def hop(t, carry):
            from_low = p - t
            from_high = p + t
            for m in pairs[ph]:
                for h in range(NH):

                    @pl.when(from_low >= 0)
                    def _():
                        wait_block(wall.at[m, from_low, h], wr.at[m, from_low, h])
                        send_weight(0, m, from_low, h)

                    @pl.when(from_high < ZL)
                    def _():
                        wait_block(wall.at[m, from_high, h], wr.at[m, from_high, h])
                        send_weight(1, m, from_high, h)

            return carry

        cut = max(ZL - 2, 2)
        lax.fori_loop(1, cut, hop, 0)
        middle()
        lax.fori_loop(cut, ZL, hop, 0)

    def middle_first():
        send_own(1)
        send_tokens()

    def middle_second():
        multiply(3, 1, True)
        multiply(0, 0, True)

    phase(0, middle_first)
    phase(1, middle_second)
    multiply(1, 0, False)
    multiply(2, 0, False)

    def projected(m):
        value = pown[m]
        for i in range(1, NY):
            k = lax.rem(y + i, NY)
            wait_block(precv.at[m, k], pr.at[m, k])
            value = value + precv[m, k].astype(F32)
        return value

    grad_attn_all = projected(3)[0:HD].astype(BF16)
    whole = [projected(m) for m in range(3)]
    query_all, key_all = whole[0][0:HD], whole[1][0:HD]
    value_all = whole[2][0:HD].astype(BF16)
    score_scale = HD ** (-0.5)
    for h in range(wall.shape[4] // HD):
        cols = slice(h * HD, (h + 1) * HD)
        q_hat, q_inv = row_norm(query_all[:, cols])
        k_hat, k_inv = row_norm(key_all[:, cols])
        queries, key_rows = q_hat.astype(BF16), k_hat.astype(BF16)
        value_rows, grad_attn = value_all[:, cols], grad_attn_all[:, cols]
        exps = jnp.exp(mm_nt(queries, key_rows) * score_scale)
        probs = exps / jnp.sum(exps, axis=-1, keepdims=True)
        grad_values = mm_tn(probs.astype(BF16), grad_attn)
        grad_probs = mm_nt(grad_attn, value_rows)
        inner = jnp.sum(probs * grad_probs, axis=-1, keepdims=True)
        grad_scores = (probs * (grad_probs - inner) * score_scale).astype(BF16)
        grad_query = mm(grad_scores, key_rows)
        grad_keys = mm_tn(grad_scores, queries)
        grads = (
            row_norm_back(grad_query, q_hat, q_inv).astype(BF16),
            row_norm_back(grad_keys, k_hat, k_inv).astype(BF16),
            grad_values.astype(BF16),
        )
        for m in range(3):
            for r in range(NR):
                dbuf[r, y, m, :, cols] = grads[m][r * half : (r + 1) * half]
    for r in range(NR):
        for i, (_, device) in enumerate(y_peers):
            remote(dbuf.at[r, y], dbuf.at[r, y], ds_.at[r, i], dr.at[r, y], device).start()

    first_part, second_part = 0.0, 0.0
    for m in range(3):
        grad = jnp.concatenate([dbuf[r, y, m].astype(F32) for r in range(NR)], axis=0)
        first_part = first_part + grad * whole[m][HD : HD + 1]
        second_part = second_part + grad * whole[m][0:HD]
    fin[mp] = columns_to_rows(
        jnp.sum(first_part, axis=-1, keepdims=True), jnp.sum(second_part, axis=-1, keepdims=True)
    )[0:2]
    share(fin, mp, near_peers + [partner] + far_peers, st_s.at[3], st_r.at[3])

    goal = [1 - zh, zh]
    apart = width // rows

    def term_block(side, r, tb, wait):
        if wait:
            wait_block(dbuf.at[r, tb], dr.at[r, tb])
        for half_c in range(NC):
            j = goal[side] * NC + half_c
            acc = None
            for m in range(3):
                weights = wall[m, pl.ds(j * apart, apart)].reshape(width, wall.shape[4])
                term = mm_nt(dbuf[r, tb, m], weights)
                acc = term if acc is None else acc + term
            tbuf[half_c, side, r, tb] = acc.astype(BF16)
        remote(
            tbuf.at[1 - c, side, r, tb], tr.at[side, r, tb], tcs.at[side, r, tb], tcr.at[side, r, tb], other_core
        ).start()

    def add_cores(side, r, tb):
        wait_block(tr.at[side, r, tb], tcr.at[side, r, tb])
        sbuf[side, r, tb] = (tbuf[c, side, r, tb].astype(F32) + tr[side, r, tb].astype(F32)).astype(BF16)

        @pl.when(tb != x)
        def _():
            remote(
                sbuf.at[side, r, tb], sr.at[side, r, x], ss.at[side, r, tb], srs.at[side, r, x], dev(tb, y, zh, p, c)
            ).start()

    other_core = dev(x, y, zh, p, 1 - c)
    order = [0, 1, 3, 2] if NY == 4 else list(range(NY))

    def blocks(side, r):
        before = None
        for i in order[1:]:
            tb = at_y[i]
            term_block(side, r, tb, side == 0)
            if before is not None:
                add_cores(side, r, before)
            before = tb
        add_cores(side, r, before)

    own = [(side, r) for side in range(2) for r in range(NR)]
    for side, r in own:
        term_block(side, r, y, False)
    for side, r in own:
        add_cores(side, r, y)

    def gather_x(side, r):
        k = goal[side]
        value = sbuf[side, r, x].astype(F32)
        for i in range(1, NX):
            wait_block(sr.at[side, r, at_x[i]], srs.at[side, r, at_x[i]])
            value = value + sr[side, r, at_x[i]].astype(F32)
        ubuf[side, r] = value.astype(BF16)
        if side == 0:
            remote(ubuf.at[0, r], ur.at[r, zh], us.at[0, r], urs.at[r, zh], dev(y, x, k, p, c)).start()
        else:

            @pl.when(x == y)
            def _():
                pltpu.make_async_copy(ubuf.at[1, r], ur.at[r, zh], urs.at[r, zh]).start()

            @pl.when(x != y)
            def _():
                remote(ubuf.at[1, r], ur.at[r, zh], us.at[1, r], urs.at[r, zh], dev(y, x, k, p, c)).start()

    for r in range(NR):
        blocks(0, r)
    for r in range(NR):
        gather_x(0, r)
        blocks(1, r)
    for r in range(NR):
        gather_x(1, r)
    arrived(st_z, n_z, st_s.at[0])
    arrived(rs, n_mp, st_s.at[1])
    arrived(st_xyc, n_xyc, st_s.at[2])
    arrived(fin, n_mp, st_s.at[3])
    for k in range(ZH):
        here = (x == y) & (zh == k)

        @pl.when(jnp.logical_not(here))
        def _():
            wait_block(xraw.at[0], xs.at[k])

    @pl.when(x != y)
    def _():
        wait_block(mi.at[0], ms.at[1])

    def left_y(i, carry):
        for j in range(ZH * NC):
            wait_block(token_rows(1, j, 0), cs.at[i, j])
        for m in range(4):
            wait_block(psend.at[m, 0], ps.at[m, i])
        for r in range(NR):
            wait_block(dbuf.at[r, 0], ds_.at[r, i])
        return carry

    lax.fori_loop(0, NY - 1, left_y, 0)

    def left_near(i, carry):
        for k in range(ZH):
            wait_block(token_rows(0, 0, 0), n3s.at[k, i])
        return carry

    lax.fori_loop(0, NX * NC - 1, left_near, 0)

    @pl.when(x == y)
    def _():
        for i in range(n_mp - 1):
            wait_block(gx.at[0], gs.at[i])

    def left_blocks(tb, carry):
        for side in range(2):
            for r in range(NR):
                wait_block(tr.at[side, r, tb], tcs.at[side, r, tb])

        @pl.when(tb != x)
        def _():
            for side in range(2):
                for r in range(NR):
                    wait_block(sbuf.at[side, r, tb], ss.at[side, r, tb])

        return carry

    lax.fori_loop(0, NY, left_blocks, 0)

    def left_weights(i, carry):
        m, s = lax.div(i, ZL), lax.rem(i, ZL)
        for h in range(NH):

            @pl.when((p < ZL - 1) & (s <= p))
            def _():
                wait_block(wall.at[m, s, h], ws.at[0, m, s, h])

            @pl.when((p > 0) & (s >= p))
            def _():
                wait_block(wall.at[m, s, h], ws.at[1, m, s, h])

        return carry

    lax.fori_loop(0, 4 * ZL, left_weights, 0)

    arrived(fin, n_mp, st_r.at[3])
    sums = jnp.sum(fin[...], axis=0) * (1.0 / n_feat)
    first, second = rows_to_columns(sums[0:1], sums[1:2])
    for r in range(NR):
        part = slice(r * half, (r + 1) * half)
        share_sum = 0.0
        for k in range(ZH):
            wait_block(ur.at[r, k], urs.at[r, k])
            share_sum = share_sum + ur[r, k].astype(F32)
        upstream = share_sum * gain[...].astype(F32).reshape(1, -1)
        out[part] = ((upstream - first[part] - normed[part] * second[part]) * invc[part, 0:1]).astype(BF16)

    for side in range(2):
        for r in range(NR):

            @pl.when((side == 0) | (x != y))
            def _():
                wait_block(ubuf.at[side, r], us.at[side, r])


def per_device(tokens, norm_gain, attn_weights, stored_grads, cotangent):
    width = tokens.shape[1]
    _, rows, columns = attn_weights.shape
    n_mp = NX * ZH * NC
    nj = ZH * NC
    dma = pltpu.SemaphoreType.DMA
    vmem = pl.BlockSpec(memory_space=pltpu.VMEM)
    return pl.pallas_call(
        kernel,
        out_shape=jax.ShapeDtypeStruct((HD, width), BF16),
        in_specs=[pl.BlockSpec(memory_space=pltpu.HBM)] * 5,
        out_specs=vmem,
        scratch_shapes=[
            pltpu.VMEM(tokens.shape, BF16),
            pltpu.VMEM((width,), BF16),
            pltpu.VMEM(attn_weights.shape, BF16),
            pltpu.VMEM(attn_weights.shape, BF16),
            pltpu.VMEM((ZH * ZL, 1, HD), F32),
            pltpu.VMEM((NX * NY * NC, 1, HD), F32),
            pltpu.VMEM((n_mp, 2, HD), F32),
            pltpu.VMEM((ZH * NC + 1, 1, width), F32),
            pltpu.VMEM((n_mp, 2, HD), F32),
            pltpu.VMEM((2, 2, HD), F32),
            pltpu.VMEM((ZH, HD, width), BF16),
            pltpu.VMEM((HD, width), F32),
            pltpu.VMEM((HD, HD), F32),
            pltpu.VMEM((2, nj, NY * HD + EXTRA, width), BF16),
            pltpu.VMEM((4, ZL, NH, rows // NH, columns), BF16),
            pltpu.VMEM((NY, HD + EXTRA, columns), F32),
            pltpu.VMEM((4, HD + EXTRA, columns), F32),
            pltpu.VMEM((4, NY, HD + EXTRA, columns), BF16),
            pltpu.VMEM((4, NY, HD + EXTRA, columns), BF16),
            pltpu.VMEM((NR, NY, 3, HD // NR, columns), BF16),
            pltpu.VMEM((NC, 2, NR, NY, HD // NR, width), BF16),
            pltpu.VMEM((2, NR, NY, HD // NR, width), BF16),
            pltpu.VMEM((2, NR, NY, HD // NR, width), BF16),
            pltpu.VMEM((2, NR, NX, HD // NR, width), BF16),
            pltpu.VMEM((2, NR, HD // NR, width), BF16),
            pltpu.VMEM((NR, ZH, HD // NR, width), BF16),
            dma((4,)),
            dma((4,)),
            dma((4,)),
            dma((n_mp - 1,)),
            dma((1,)),
            dma((2,)),
            dma((ZH,)),
            dma((ZH,)),
            dma((2, nj, NY)),
            dma((NY, nj)),
            dma((ZH, NX * NC)),
            dma((2, 4, ZL, NH)),
            dma((4, ZL, NH)),
            dma((4, NY)),
            dma((4, NY)),
            dma((NR, NY)),
            dma((NR, NY)),
            dma((2, NR, NY)),
            dma((2, NR, NY)),
            dma((2, NR, NY)),
            dma((2, NR, NX)),
            dma((2, NR)),
            dma((NR, ZH)),
        ],
        compiler_params=pltpu.CompilerParams(
            collective_id=0, has_side_effects=True, vmem_limit_bytes=60 * 1024 * 1024
        ),
    )(tokens, norm_gain, attn_weights, stored_grads, cotangent)


def solution(mesh):
    return jax.shard_map(
        per_device,
        mesh=mesh,
        in_specs=(P("dp", "mp"), P("mp"), P(None, "dp", "mp"), P(None, "dp", "mp"), P("dp", None)),
        out_specs=P("dp", "mp"),
        check_vma=False,
    )
```

```python
import jax
import jax.numpy as jnp
from jax import lax
from jax.experimental import pallas as pl
from jax.experimental.pallas import tpu as pltpu
from jax.sharding import PartitionSpec as P

MESH = pl.DeviceIdType.MESH
F32, BF16 = jnp.float32, jnp.bfloat16
HD = 128
NX, NY, ZH, ZL, NC = 4, 4, 2, 8, 2
NH = 2
EXTRA = 16
NR = 2
ascent_radius = 0.15


def mm(a, b):
    return lax.dot_general(a, b, (((1,), (0,)), ((), ())), preferred_element_type=F32)


def mm_nt(a, b):
    return lax.dot_general(a, b, (((1,), (1,)), ((), ())), preferred_element_type=F32)


def mm_tn(a, b):
    return lax.dot_general(a, b, (((0,), (0,)), ((), ())), preferred_element_type=F32)


def row_norm(matrix):
    center = matrix - jnp.mean(matrix, axis=-1, keepdims=True)
    inverse = lax.rsqrt(jnp.mean(center * center, axis=-1, keepdims=True) + 1e-06)
    return center * inverse, inverse


def row_norm_back(upstream, normed, inverse):
    first_mean = jnp.mean(upstream, axis=-1, keepdims=True)
    second_mean = jnp.mean(upstream * normed, axis=-1, keepdims=True)
    return (upstream - first_mean - normed * second_mean) * inverse


def columns_to_rows(first, second):
    lane = lax.broadcasted_iota(jnp.int32, (HD, HD), 1)
    both = jnp.where(lane == 0, first, jnp.where(lane == 1, second, 0.0))
    return both.T[0:8]


def rows_to_columns(first, second):
    sub = lax.broadcasted_iota(jnp.int32, (HD, HD), 0)
    both = jnp.where(sub == 0, first, jnp.where(sub == 1, second, 0.0))
    turned = both.T
    return turned[:, 0:1], turned[:, 1:2]


def kernel(
    tok_hbm, gain_hbm, w_hbm, g_hbm, cot, out,
    tok, gain, w, g,
    st_z, st_xyc, rs, gx, fin, mi, xraw, normed, invc, xc, wall, pf, pown, psend, precv, dbuf, tbuf, tr, sbuf, sr, ubuf, ur,
    ins, st_s, st_r, gs, gr, ms, xs, xw, xr, cs, n3s, ws, wr, ps, pr, ds_, dr, tcs, tcr, ss, srs, us, urs,
):
    n_mp = NX * ZH * NC
    n_z = ZH * ZL
    width = tok.shape[1]
    band = ZH * NC * width
    n_feat = n_mp * width
    rows = w.shape[1]
    dp = lax.axis_index("dp")
    mp = lax.axis_index("mp")
    y, p = lax.div(dp, ZL), lax.rem(dp, ZL)
    x, c = lax.div(mp, ZH * NC), lax.rem(mp, NC)
    zh = lax.rem(lax.div(mp, NC), ZH)
    z = zh * ZL + p
    xcore = x * NC + c
    xyc = y * NX * NC + xcore
    half = HD // NR
    n_xyc = NX * NY * NC

    def dev(x_, y_, zh_, p_, c_):
        return (y_ * ZL + p_, (x_ * ZH + zh_) * NC + c_)

    def dev_z(k):
        return dev(x, y, lax.div(k, ZL), lax.rem(k, ZL), c)

    def dev_y(k):
        return dev(x, k, zh, p, c)

    def remote(src, dst, ssem, rsem, device):
        return pltpu.make_async_remote_copy(
            src_ref=src, dst_ref=dst, send_sem=ssem, recv_sem=rsem, device_id=device, device_id_type=MESH
        )

    def token_rows(sel, j, tb):
        return xc.at[sel, j, pl.ds(pl.multiple_of(tb * HD, HD), HD)]

    def share(buf, mine, peers, ssem, rsem):
        for device in peers:
            remote(buf.at[mine], buf.at[mine], ssem, rsem, device).start()

    def arrived(buf, n, sem):
        part = buf.at[pl.ds(0, n - 1)]
        pltpu.make_async_copy(part, part, sem).wait()

    loads = [
        pltpu.make_async_copy(src, dst, ins.at[i])
        for i, (src, dst) in enumerate(((w_hbm, w), (g_hbm, g), (tok_hbm, tok), (gain_hbm, gain)))
    ]
    for load in loads:
        load.start()

    barrier = pltpu.get_barrier_semaphore()

    def greet(device):
        pl.semaphore_signal(barrier, inc=1, device_id=device, device_id_type=MESH)

    z_peers = []
    for i in range(1, n_z):
        k = lax.rem(z + i, n_z)
        z_peers.append((k, dev_z(k)))
    at_x = [lax.rem(x + i, NX) for i in range(NX)]
    at_y = [lax.rem(y + i, NY) for i in range(NY)]
    at_c = [c, 1 - c]
    at_z = [zh, 1 - zh]
    plane_peers = [
        dev(at_x[i], at_y[j], zh, p, at_c[q]) for j in range(NY) for i in range(NX) for q in range(NC) if i + j + q
    ]
    near_peers = [dev(at_x[i], y, zh, p, at_c[q]) for i in range(NX) for q in range(NC) if i + q]
    far_peers = [dev(at_x[i], y, 1 - zh, p, at_c[q]) for i in range(NX) for q in range(NC) if i + q]
    partner = dev(x, y, 1 - zh, p, c)
    y_peers = [(at_y[i], dev_y(at_y[i])) for i in range(1, NY)]
    for _, device in z_peers:
        greet(device)
    for device in far_peers + plane_peers:
        greet(device)

    @pl.when(x != y)
    def _():
        greet(dev(y, x, 1 - zh, p, c))

    loads[0].wait()
    loads[1].wait()
    lane = lax.broadcasted_iota(jnp.int32, (1, HD), 1)
    row = jnp.zeros((1, HD), F32)
    for m in range(4):
        for base, ref in ((0, w), (4, g)):
            values = ref[m].astype(F32)
            sums = jnp.sum(values * values, axis=0, keepdims=True)
            row = jnp.where(lane == base + m, jnp.sum(sums, axis=1, keepdims=True), row)
    st_z[z] = row
    loads[2].wait()
    loads[3].wait()
    part = tok[...].astype(F32)
    part_mean = jnp.sum(part, axis=-1, keepdims=True) * (1.0 / width)
    part_square = jnp.sum(jnp.square(part - part_mean), axis=-1, keepdims=True)
    rs[mp] = columns_to_rows(part_mean, part_square)[0:2]
    gx[ZH * NC] = gain[...].astype(F32).reshape(1, -1)
    for j in range(ZH * NC):
        xc[1, j, NY * HD :] = jnp.zeros((EXTRA, width), BF16)

    pl.semaphore_wait(
        barrier, (n_z - 1) + (n_xyc - 1) + (ZH - 1) * (NX * NC - 1) + jnp.where(x != y, ZH - 1, 0)
    )

    share(st_z, z, [d for _, d in z_peers], st_s.at[0], st_r.at[0])
    share(rs, mp, near_peers + [partner] + far_peers, st_s.at[1], st_r.at[1])
    arrived(st_z, n_z, st_r.at[0])
    st_xyc[xyc] = jnp.sum(st_z[...], axis=0)
    share(st_xyc, xyc, plane_peers, st_s.at[2], st_r.at[2])

    for k in at_z[::-1]:
        here = (x == y) & (zh == k)

        @pl.when(here)
        def _():
            pltpu.make_async_copy(tok, xraw.at[zh], xw.at[zh]).start()

        @pl.when(jnp.logical_not(here))
        def _():
            remote(tok, xraw.at[zh], xs.at[k], xw.at[zh], dev(y, x, k, p, c)).start()

    arrived(rs, n_mp, st_r.at[1])
    means = rs[:, 0:1, :]
    mean = jnp.sum(means, axis=0) * (1.0 / n_mp)
    square = jnp.sum(rs[:, 1:2, :], axis=0) + width * jnp.sum(jnp.square(means - mean[None]), axis=0)
    inverse = lax.rsqrt(square * (1.0 / n_feat) + 1e-06)
    mean_col, inv_col = rows_to_columns(mean, inverse)
    normed[...] = (tok[...].astype(F32) - mean_col) * inv_col
    invc[...] = jnp.broadcast_to(inv_col, (HD, HD))
    mi[0] = jnp.concatenate([mean, inverse], axis=0)

    @pl.when(x == y)
    def _():
        pltpu.make_async_copy(mi.at[0], mi.at[1], ms.at[0]).start()

    @pl.when(x != y)
    def _():
        remote(mi.at[0], mi.at[1], ms.at[1], ms.at[0], dev(y, x, zh, p, c)).start()

    arrived(st_xyc, n_xyc, st_r.at[2])
    total = jnp.sum(st_xyc[...], axis=0)
    piece = rows // NH
    for m in range(4):
        ratio = (
            ascent_radius * jnp.sqrt(total[:, m : m + 1]) / (jnp.sqrt(total[:, 4 + m : 5 + m]) + 1e-12)
        )
        shifted = (w[m].astype(F32) + ratio * g[m].astype(F32)).astype(BF16)
        for h in range(NH):
            wall[m, p, h] = shifted[h * piece : (h + 1) * piece]

    pairs = ((3, 0), (1, 2))

    def send_weight(way, m, s, h):
        @pl.when(p < ZL - 1 if way == 0 else p > 0)
        def _():
            block = wall.at[m, s, h]
            remote(
                block, block, ws.at[way, m, s, h], wr.at[m, s, h], dev(x, y, zh, p + 1 - 2 * way, c)
            ).start()

    def send_own(ph):
        for m in pairs[ph]:
            for h in range(NH):
                send_weight(0, m, p, h)
                send_weight(1, m, p, h)

    send_own(0)

    mp_peers = near_peers + [partner] + far_peers

    @pl.when(x == y)
    def _():
        slot = zh * NC + c
        pltpu.make_async_copy(gx.at[ZH * NC], gx.at[slot], gr.at[0]).start()
        for i, device in enumerate(mp_peers):
            remote(gx.at[ZH * NC], gx.at[slot], gs.at[i], gr.at[0], device).start()

    for j in range(ZH * NC):
        pltpu.make_async_copy(
            cot.at[:, pl.ds(pl.multiple_of(y * band + j * width, HD), width)], token_rows(1, j, y), xr.at[1, j, y]
        ).start()

    for i, (k, device) in enumerate(y_peers):
        for j in range(ZH * NC):
            remote(
                cot.at[:, pl.ds(pl.multiple_of(k * band + j * width, HD), width)],
                token_rows(1, j, y),
                cs.at[i, j],
                xr.at[1, j, y],
                device,
            ).start()

    def wait_block(ref, sem):
        pltpu.make_async_copy(ref, ref, sem).wait()

    def send_tokens():
        wait_block(mi.at[1], ms.at[0])
        arrived(gx, ZH * NC + 1, gr.at[0])
        for j in range(ZH * NC):
            xc[0, j, NY * HD :] = jnp.broadcast_to(gx[j], (EXTRA, width)).astype(BF16)
        mean_there, inv_there = rows_to_columns(mi[1, 0:1], mi[1, 1:2])
        for k in range(ZH):
            j = k * NC + c
            block = token_rows(0, j, x)
            wait_block(xraw.at[k], xw.at[k])
            hat = (xraw[k].astype(F32) - mean_there) * inv_there
            block[...] = (hat * gx[j]).astype(BF16)
            for i, device in enumerate(near_peers):
                remote(block, block, n3s.at[k, i], xr.at[0, j, x], device).start()

    def multiply(m, sel, fresh):
        if fresh:

            def wait_one(i, carry):
                j, tb = lax.div(i, NY), lax.rem(i, NY)

                @pl.when((sel == 1) | (lax.rem(j, NC) != c) | (tb != x))
                def _():
                    wait_block(token_rows(sel, j, tb), xr.at[sel, j, tb])

                return carry

            lax.fori_loop(0, ZH * NC * NY, wait_one, 0)

        columns = wall.shape[4]
        weights = wall[m].reshape(ZL * rows, columns)
        acc = None
        for j in range(ZH * NC):
            term = mm(xc[sel, j], weights[j * width : (j + 1) * width])
            acc = term if acc is None else acc + term
        for k in range(NY):
            pf[k, 0:HD] = acc[k * HD : (k + 1) * HD]
            pf[k, HD:] = acc[NY * HD :]
        pown[m] = pf[y]
        psend[m] = pf[...].astype(BF16)
        for i, (k, device) in enumerate(y_peers):
            remote(psend.at[m, k], precv.at[m, y], ps.at[m, i], pr.at[m, y], device).start()

    def phase(ph, middle):
        def hop(t, carry):
            from_low = p - t
            from_high = p + t
            for m in pairs[ph]:
                for h in range(NH):

                    @pl.when(from_low >= 0)
                    def _():
                        wait_block(wall.at[m, from_low, h], wr.at[m, from_low, h])
                        send_weight(0, m, from_low, h)

                    @pl.when(from_high < ZL)
                    def _():
                        wait_block(wall.at[m, from_high, h], wr.at[m, from_high, h])
                        send_weight(1, m, from_high, h)

            return carry

        cut = max(ZL - 2, 2)
        lax.fori_loop(1, cut, hop, 0)
        middle()
        lax.fori_loop(cut, ZL, hop, 0)

    def middle_first():
        send_own(1)
        send_tokens()

    def middle_second():
        multiply(3, 1, True)
        multiply(0, 0, True)

    phase(0, middle_first)
    phase(1, middle_second)
    multiply(1, 0, False)
    multiply(2, 0, False)

    def projected(m):
        value = pown[m]
        for i in range(1, NY):
            k = lax.rem(y + i, NY)
            wait_block(precv.at[m, k], pr.at[m, k])
            value = value + precv[m, k].astype(F32)
        return value

    grad_attn_all = projected(3)[0:HD].astype(BF16)
    whole = [projected(m) for m in range(3)]
    query_all, key_all = whole[0][0:HD], whole[1][0:HD]
    value_all = whole[2][0:HD].astype(BF16)
    score_scale = HD ** (-0.5)
    for h in range(wall.shape[4] // HD):
        cols = slice(h * HD, (h + 1) * HD)
        q_hat, q_inv = row_norm(query_all[:, cols])
        k_hat, k_inv = row_norm(key_all[:, cols])
        queries, key_rows = q_hat.astype(BF16), k_hat.astype(BF16)
        value_rows, grad_attn = value_all[:, cols], grad_attn_all[:, cols]
        exps = jnp.exp(mm_nt(queries, key_rows) * score_scale)
        probs = exps / jnp.sum(exps, axis=-1, keepdims=True)
        grad_values = mm_tn(probs.astype(BF16), grad_attn)
        grad_probs = mm_nt(grad_attn, value_rows)
        inner = jnp.sum(probs * grad_probs, axis=-1, keepdims=True)
        grad_scores = (probs * (grad_probs - inner) * score_scale).astype(BF16)
        grad_query = mm(grad_scores, key_rows)
        grad_keys = mm_tn(grad_scores, queries)
        grads = (
            row_norm_back(grad_query, q_hat, q_inv).astype(BF16),
            row_norm_back(grad_keys, k_hat, k_inv).astype(BF16),
            grad_values.astype(BF16),
        )
        for m in range(3):
            for r in range(NR):
                dbuf[r, y, m, :, cols] = grads[m][r * half : (r + 1) * half]
    for r in range(NR):
        for i, (_, device) in enumerate(y_peers):
            remote(dbuf.at[r, y], dbuf.at[r, y], ds_.at[r, i], dr.at[r, y], device).start()

    first_part, second_part = 0.0, 0.0
    for m in range(3):
        grad = jnp.concatenate([dbuf[r, y, m].astype(F32) for r in range(NR)], axis=0)
        first_part = first_part + grad * whole[m][HD : HD + 1]
        second_part = second_part + grad * whole[m][0:HD]
    fin[mp] = columns_to_rows(
        jnp.sum(first_part, axis=-1, keepdims=True), jnp.sum(second_part, axis=-1, keepdims=True)
    )[0:2]
    share(fin, mp, near_peers + [partner] + far_peers, st_s.at[3], st_r.at[3])

    goal = [1 - zh, zh]
    apart = width // rows

    def term_block(side, r, tb, wait):
        if wait:
            wait_block(dbuf.at[r, tb], dr.at[r, tb])
        for half_c in range(NC):
            j = goal[side] * NC + half_c
            acc = None
            for m in range(3):
                weights = wall[m, pl.ds(j * apart, apart)].reshape(width, wall.shape[4])
                term = mm_nt(dbuf[r, tb, m], weights)
                acc = term if acc is None else acc + term
            tbuf[half_c, side, r, tb] = acc.astype(BF16)
        remote(
            tbuf.at[1 - c, side, r, tb], tr.at[side, r, tb], tcs.at[side, r, tb], tcr.at[side, r, tb], other_core
        ).start()

    def add_cores(side, r, tb):
        wait_block(tr.at[side, r, tb], tcr.at[side, r, tb])
        sbuf[side, r, tb] = (tbuf[c, side, r, tb].astype(F32) + tr[side, r, tb].astype(F32)).astype(BF16)

        @pl.when(tb != x)
        def _():
            remote(
                sbuf.at[side, r, tb], sr.at[side, r, x], ss.at[side, r, tb], srs.at[side, r, x], dev(tb, y, zh, p, c)
            ).start()

    other_core = dev(x, y, zh, p, 1 - c)
    order = [0, 1, 3, 2] if NY == 4 else list(range(NY))

    def blocks(side, r):
        before = None
        for i in order[1:]:
            tb = at_y[i]
            term_block(side, r, tb, side == 0)
            if before is not None:
                add_cores(side, r, before)
            before = tb
        add_cores(side, r, before)

    own = [(side, r) for side in range(2) for r in range(NR)]
    for side, r in own:
        term_block(side, r, y, False)
    for side, r in own:
        add_cores(side, r, y)

    def gather_x(side, r):
        k = goal[side]
        value = sbuf[side, r, x].astype(F32)
        for i in range(1, NX):
            wait_block(sr.at[side, r, at_x[i]], srs.at[side, r, at_x[i]])
            value = value + sr[side, r, at_x[i]].astype(F32)
        ubuf[side, r] = value.astype(BF16)
        if side == 0:
            remote(ubuf.at[0, r], ur.at[r, zh], us.at[0, r], urs.at[r, zh], dev(y, x, k, p, c)).start()
        else:

            @pl.when(x == y)
            def _():
                pltpu.make_async_copy(ubuf.at[1, r], ur.at[r, zh], urs.at[r, zh]).start()

            @pl.when(x != y)
            def _():
                remote(ubuf.at[1, r], ur.at[r, zh], us.at[1, r], urs.at[r, zh], dev(y, x, k, p, c)).start()

    for r in range(NR - 1):
        blocks(0, r)
        gather_x(0, r)
    blocks(0, NR - 1)
    for r in range(NR - 1):
        blocks(1, r)
    gather_x(0, NR - 1)
    blocks(1, NR - 1)
    for r in range(NR):
        gather_x(1, r)
    arrived(st_z, n_z, st_s.at[0])
    arrived(rs, n_mp, st_s.at[1])
    arrived(st_xyc, n_xyc, st_s.at[2])
    arrived(fin, n_mp, st_s.at[3])
    for k in range(ZH):
        here = (x == y) & (zh == k)

        @pl.when(jnp.logical_not(here))
        def _():
            wait_block(xraw.at[0], xs.at[k])

    @pl.when(x != y)
    def _():
        wait_block(mi.at[0], ms.at[1])

    def left_y(i, carry):
        for j in range(ZH * NC):
            wait_block(token_rows(1, j, 0), cs.at[i, j])
        for m in range(4):
            wait_block(psend.at[m, 0], ps.at[m, i])
        for r in range(NR):
            wait_block(dbuf.at[r, 0], ds_.at[r, i])
        return carry

    lax.fori_loop(0, NY - 1, left_y, 0)

    def left_near(i, carry):
        for k in range(ZH):
            wait_block(token_rows(0, 0, 0), n3s.at[k, i])
        return carry

    lax.fori_loop(0, NX * NC - 1, left_near, 0)

    @pl.when(x == y)
    def _():
        for i in range(n_mp - 1):
            wait_block(gx.at[0], gs.at[i])

    def left_blocks(tb, carry):
        for side in range(2):
            for r in range(NR):
                wait_block(tr.at[side, r, tb], tcs.at[side, r, tb])

        @pl.when(tb != x)
        def _():
            for side in range(2):
                for r in range(NR):
                    wait_block(sbuf.at[side, r, tb], ss.at[side, r, tb])

        return carry

    lax.fori_loop(0, NY, left_blocks, 0)

    def left_weights(i, carry):
        m, s = lax.div(i, ZL), lax.rem(i, ZL)
        for h in range(NH):

            @pl.when((p < ZL - 1) & (s <= p))
            def _():
                wait_block(wall.at[m, s, h], ws.at[0, m, s, h])

            @pl.when((p > 0) & (s >= p))
            def _():
                wait_block(wall.at[m, s, h], ws.at[1, m, s, h])

        return carry

    lax.fori_loop(0, 4 * ZL, left_weights, 0)

    arrived(fin, n_mp, st_r.at[3])
    sums = jnp.sum(fin[...], axis=0) * (1.0 / n_feat)
    first, second = rows_to_columns(sums[0:1], sums[1:2])
    for r in range(NR):
        part = slice(r * half, (r + 1) * half)
        share_sum = 0.0
        for k in range(ZH):
            wait_block(ur.at[r, k], urs.at[r, k])
            share_sum = share_sum + ur[r, k].astype(F32)
        upstream = share_sum * gain[...].astype(F32).reshape(1, -1)
        out[part] = ((upstream - first[part] - normed[part] * second[part]) * invc[part, 0:1]).astype(BF16)

    for side in range(2):
        for r in range(NR):

            @pl.when((side == 0) | (x != y))
            def _():
                wait_block(ubuf.at[side, r], us.at[side, r])


def per_device(tokens, norm_gain, attn_weights, stored_grads, cotangent):
    width = tokens.shape[1]
    _, rows, columns = attn_weights.shape
    n_mp = NX * ZH * NC
    nj = ZH * NC
    dma = pltpu.SemaphoreType.DMA
    vmem = pl.BlockSpec(memory_space=pltpu.VMEM)
    return pl.pallas_call(
        kernel,
        out_shape=jax.ShapeDtypeStruct((HD, width), BF16),
        in_specs=[pl.BlockSpec(memory_space=pltpu.HBM)] * 5,
        out_specs=vmem,
        scratch_shapes=[
            pltpu.VMEM(tokens.shape, BF16),
            pltpu.VMEM((width,), BF16),
            pltpu.VMEM(attn_weights.shape, BF16),
            pltpu.VMEM(attn_weights.shape, BF16),
            pltpu.VMEM((ZH * ZL, 1, HD), F32),
            pltpu.VMEM((NX * NY * NC, 1, HD), F32),
            pltpu.VMEM((n_mp, 2, HD), F32),
            pltpu.VMEM((ZH * NC + 1, 1, width), F32),
            pltpu.VMEM((n_mp, 2, HD), F32),
            pltpu.VMEM((2, 2, HD), F32),
            pltpu.VMEM((ZH, HD, width), BF16),
            pltpu.VMEM((HD, width), F32),
            pltpu.VMEM((HD, HD), F32),
            pltpu.VMEM((2, nj, NY * HD + EXTRA, width), BF16),
            pltpu.VMEM((4, ZL, NH, rows // NH, columns), BF16),
            pltpu.VMEM((NY, HD + EXTRA, columns), F32),
            pltpu.VMEM((4, HD + EXTRA, columns), F32),
            pltpu.VMEM((4, NY, HD + EXTRA, columns), BF16),
            pltpu.VMEM((4, NY, HD + EXTRA, columns), BF16),
            pltpu.VMEM((NR, NY, 3, HD // NR, columns), BF16),
            pltpu.VMEM((NC, 2, NR, NY, HD // NR, width), BF16),
            pltpu.VMEM((2, NR, NY, HD // NR, width), BF16),
            pltpu.VMEM((2, NR, NY, HD // NR, width), BF16),
            pltpu.VMEM((2, NR, NX, HD // NR, width), BF16),
            pltpu.VMEM((2, NR, HD // NR, width), BF16),
            pltpu.VMEM((NR, ZH, HD // NR, width), BF16),
            dma((4,)),
            dma((4,)),
            dma((4,)),
            dma((n_mp - 1,)),
            dma((1,)),
            dma((2,)),
            dma((ZH,)),
            dma((ZH,)),
            dma((2, nj, NY)),
            dma((NY, nj)),
            dma((ZH, NX * NC)),
            dma((2, 4, ZL, NH)),
            dma((4, ZL, NH)),
            dma((4, NY)),
            dma((4, NY)),
            dma((NR, NY)),
            dma((NR, NY)),
            dma((2, NR, NY)),
            dma((2, NR, NY)),
            dma((2, NR, NY)),
            dma((2, NR, NX)),
            dma((2, NR)),
            dma((NR, ZH)),
        ],
        compiler_params=pltpu.CompilerParams(
            collective_id=0, has_side_effects=True, vmem_limit_bytes=60 * 1024 * 1024
        ),
    )(tokens, norm_gain, attn_weights, stored_grads, cotangent)


def solution(mesh):
    return jax.shard_map(
        per_device,
        mesh=mesh,
        in_specs=(P("dp", "mp"), P("mp"), P(None, "dp", "mp"), P(None, "dp", "mp"), P("dp", None)),
        out_specs=P("dp", "mp"),
        check_vma=False,
    )
```

```python
import jax
import jax.numpy as jnp
from jax import lax
from jax.experimental import pallas as pl
from jax.experimental.pallas import tpu as pltpu
from jax.sharding import PartitionSpec as P

MESH = pl.DeviceIdType.MESH
F32, BF16 = jnp.float32, jnp.bfloat16
HD = 128
NX, NY, ZH, ZL, NC = 4, 4, 2, 8, 2
NH = 2
EXTRA = 16
NR = 2
ascent_radius = 0.15


def mm(a, b):
    return lax.dot_general(a, b, (((1,), (0,)), ((), ())), preferred_element_type=F32)


def mm_nt(a, b):
    return lax.dot_general(a, b, (((1,), (1,)), ((), ())), preferred_element_type=F32)


def mm_tn(a, b):
    return lax.dot_general(a, b, (((0,), (0,)), ((), ())), preferred_element_type=F32)


def row_norm(matrix):
    center = matrix - jnp.mean(matrix, axis=-1, keepdims=True)
    inverse = lax.rsqrt(jnp.mean(center * center, axis=-1, keepdims=True) + 1e-06)
    return center * inverse, inverse


def row_norm_back(upstream, normed, inverse):
    first_mean = jnp.mean(upstream, axis=-1, keepdims=True)
    second_mean = jnp.mean(upstream * normed, axis=-1, keepdims=True)
    return (upstream - first_mean - normed * second_mean) * inverse


def columns_to_rows(first, second):
    lane = lax.broadcasted_iota(jnp.int32, (HD, HD), 1)
    both = jnp.where(lane == 0, first, jnp.where(lane == 1, second, 0.0))
    return both.T[0:8]


def rows_to_columns(first, second):
    sub = lax.broadcasted_iota(jnp.int32, (HD, HD), 0)
    both = jnp.where(sub == 0, first, jnp.where(sub == 1, second, 0.0))
    turned = both.T
    return turned[:, 0:1], turned[:, 1:2]


def kernel(
    tok_hbm, gain_hbm, w_hbm, g_hbm, cot, out,
    tok, gain, w, g,
    st_z, st_xyc, rs, gx, fin, mi, xraw, normed, invc, xc, wall, pf, pown, psend, precv, dbuf, tbuf, tr, sbuf, sr, ubuf, ur,
    ins, st_s, st_r, gs, gr, ms, xs, xw, xr, cs, n3s, ws, wr, ps, pr, ds_, dr, tcs, tcr, ss, srs, us, urs,
):
    n_mp = NX * ZH * NC
    n_z = ZH * ZL
    width = tok.shape[1]
    band = ZH * NC * width
    n_feat = n_mp * width
    rows = w.shape[1]
    dp = lax.axis_index("dp")
    mp = lax.axis_index("mp")
    y, p = lax.div(dp, ZL), lax.rem(dp, ZL)
    x, c = lax.div(mp, ZH * NC), lax.rem(mp, NC)
    zh = lax.rem(lax.div(mp, NC), ZH)
    z = zh * ZL + p
    xcore = x * NC + c
    xyc = y * NX * NC + xcore
    half = HD // NR
    n_xyc = NX * NY * NC

    def dev(x_, y_, zh_, p_, c_):
        return (y_ * ZL + p_, (x_ * ZH + zh_) * NC + c_)

    def dev_z(k):
        return dev(x, y, lax.div(k, ZL), lax.rem(k, ZL), c)

    def dev_y(k):
        return dev(x, k, zh, p, c)

    def remote(src, dst, ssem, rsem, device):
        return pltpu.make_async_remote_copy(
            src_ref=src, dst_ref=dst, send_sem=ssem, recv_sem=rsem, device_id=device, device_id_type=MESH
        )

    def token_rows(sel, j, tb):
        return xc.at[sel, j, pl.ds(pl.multiple_of(tb * HD, HD), HD)]

    def share(buf, mine, peers, ssem, rsem):
        for device in peers:
            remote(buf.at[mine], buf.at[mine], ssem, rsem, device).start()

    def arrived(buf, n, sem):
        part = buf.at[pl.ds(0, n - 1)]
        pltpu.make_async_copy(part, part, sem).wait()

    loads = [
        pltpu.make_async_copy(src, dst, ins.at[i])
        for i, (src, dst) in enumerate(((w_hbm, w), (g_hbm, g), (tok_hbm, tok), (gain_hbm, gain)))
    ]
    for load in loads:
        load.start()

    barrier = pltpu.get_barrier_semaphore()

    def greet(device):
        pl.semaphore_signal(barrier, inc=1, device_id=device, device_id_type=MESH)

    z_peers = []
    for i in range(1, n_z):
        k = lax.rem(z + i, n_z)
        z_peers.append((k, dev_z(k)))
    at_x = [lax.rem(x + i, NX) for i in range(NX)]
    at_y = [lax.rem(y + i, NY) for i in range(NY)]
    at_c = [c, 1 - c]
    at_z = [zh, 1 - zh]
    plane_peers = [
        dev(at_x[i], at_y[j], zh, p, at_c[q]) for j in range(NY) for i in range(NX) for q in range(NC) if i + j + q
    ]
    near_peers = [dev(at_x[i], y, zh, p, at_c[q]) for i in range(NX) for q in range(NC) if i + q]
    far_peers = [dev(at_x[i], y, 1 - zh, p, at_c[q]) for i in range(NX) for q in range(NC) if i + q]
    partner = dev(x, y, 1 - zh, p, c)
    y_peers = [(at_y[i], dev_y(at_y[i])) for i in range(1, NY)]
    for _, device in z_peers:
        greet(device)
    for device in far_peers + plane_peers:
        greet(device)

    @pl.when(x != y)
    def _():
        greet(dev(y, x, 1 - zh, p, c))

    loads[0].wait()
    loads[1].wait()
    lane = lax.broadcasted_iota(jnp.int32, (1, HD), 1)
    row = jnp.zeros((1, HD), F32)
    for m in range(4):
        for base, ref in ((0, w), (4, g)):
            values = ref[m].astype(F32)
            sums = jnp.sum(values * values, axis=0, keepdims=True)
            row = jnp.where(lane == base + m, jnp.sum(sums, axis=1, keepdims=True), row)
    st_z[z] = row
    loads[2].wait()
    loads[3].wait()
    part = tok[...].astype(F32)
    part_mean = jnp.sum(part, axis=-1, keepdims=True) * (1.0 / width)
    part_square = jnp.sum(jnp.square(part - part_mean), axis=-1, keepdims=True)
    rs[mp] = columns_to_rows(part_mean, part_square)[0:2]
    gx[ZH * NC] = gain[...].astype(F32).reshape(1, -1)
    for j in range(ZH * NC):
        xc[1, j, NY * HD :] = jnp.zeros((EXTRA, width), BF16)

    pl.semaphore_wait(
        barrier, (n_z - 1) + (n_xyc - 1) + (ZH - 1) * (NX * NC - 1) + jnp.where(x != y, ZH - 1, 0)
    )

    share(st_z, z, [d for _, d in z_peers], st_s.at[0], st_r.at[0])
    share(rs, mp, near_peers + [partner] + far_peers, st_s.at[1], st_r.at[1])
    arrived(st_z, n_z, st_r.at[0])
    st_xyc[xyc] = jnp.sum(st_z[...], axis=0)
    share(st_xyc, xyc, plane_peers, st_s.at[2], st_r.at[2])

    for k in at_z[::-1]:
        here = (x == y) & (zh == k)

        @pl.when(here)
        def _():
            pltpu.make_async_copy(tok, xraw.at[zh], xw.at[zh]).start()

        @pl.when(jnp.logical_not(here))
        def _():
            remote(tok, xraw.at[zh], xs.at[k], xw.at[zh], dev(y, x, k, p, c)).start()

    arrived(rs, n_mp, st_r.at[1])
    means = rs[:, 0:1, :]
    mean = jnp.sum(means, axis=0) * (1.0 / n_mp)
    square = jnp.sum(rs[:, 1:2, :], axis=0) + width * jnp.sum(jnp.square(means - mean[None]), axis=0)
    inverse = lax.rsqrt(square * (1.0 / n_feat) + 1e-06)
    mean_col, inv_col = rows_to_columns(mean, inverse)
    normed[...] = (tok[...].astype(F32) - mean_col) * inv_col
    invc[...] = jnp.broadcast_to(inv_col, (HD, HD))
    mi[0] = jnp.concatenate([mean, inverse], axis=0)

    @pl.when(x == y)
    def _():
        pltpu.make_async_copy(mi.at[0], mi.at[1], ms.at[0]).start()

    @pl.when(x != y)
    def _():
        remote(mi.at[0], mi.at[1], ms.at[1], ms.at[0], dev(y, x, zh, p, c)).start()

    arrived(st_xyc, n_xyc, st_r.at[2])
    total = jnp.sum(st_xyc[...], axis=0)
    piece = rows // NH
    for m in range(4):
        ratio = (
            ascent_radius * jnp.sqrt(total[:, m : m + 1]) / (jnp.sqrt(total[:, 4 + m : 5 + m]) + 1e-12)
        )
        shifted = (w[m].astype(F32) + ratio * g[m].astype(F32)).astype(BF16)
        for h in range(NH):
            wall[m, p, h] = shifted[h * piece : (h + 1) * piece]

    pairs = ((3, 0), (1, 2))

    def send_weight(way, m, s, h):
        @pl.when(p < ZL - 1 if way == 0 else p > 0)
        def _():
            block = wall.at[m, s, h]
            remote(
                block, block, ws.at[way, m, s, h], wr.at[m, s, h], dev(x, y, zh, p + 1 - 2 * way, c)
            ).start()

    def send_own(ph):
        for m in pairs[ph]:
            for h in range(NH):
                send_weight(0, m, p, h)
                send_weight(1, m, p, h)

    send_own(0)

    mp_peers = near_peers + [partner] + far_peers

    @pl.when(x == y)
    def _():
        slot = zh * NC + c
        pltpu.make_async_copy(gx.at[ZH * NC], gx.at[slot], gr.at[0]).start()
        for i, device in enumerate(mp_peers):
            remote(gx.at[ZH * NC], gx.at[slot], gs.at[i], gr.at[0], device).start()

    for j in range(ZH * NC):
        pltpu.make_async_copy(
            cot.at[:, pl.ds(pl.multiple_of(y * band + j * width, HD), width)], token_rows(1, j, y), xr.at[1, j, y]
        ).start()

    for i, (k, device) in enumerate(y_peers):
        for j in range(ZH * NC):
            remote(
                cot.at[:, pl.ds(pl.multiple_of(k * band + j * width, HD), width)],
                token_rows(1, j, y),
                cs.at[i, j],
                xr.at[1, j, y],
                device,
            ).start()

    def wait_block(ref, sem):
        pltpu.make_async_copy(ref, ref, sem).wait()

    def send_tokens():
        wait_block(mi.at[1], ms.at[0])
        arrived(gx, ZH * NC + 1, gr.at[0])
        for j in range(ZH * NC):
            xc[0, j, NY * HD :] = jnp.broadcast_to(gx[j], (EXTRA, width)).astype(BF16)
        mean_there, inv_there = rows_to_columns(mi[1, 0:1], mi[1, 1:2])
        for k in range(ZH):
            j = k * NC + c
            block = token_rows(0, j, x)
            wait_block(xraw.at[k], xw.at[k])
            hat = (xraw[k].astype(F32) - mean_there) * inv_there
            block[...] = (hat * gx[j]).astype(BF16)
            for i, device in enumerate(near_peers):
                remote(block, block, n3s.at[k, i], xr.at[0, j, x], device).start()

    def multiply(m, sel, fresh):
        if fresh:

            def wait_one(i, carry):
                j, tb = lax.div(i, NY), lax.rem(i, NY)

                @pl.when((sel == 1) | (lax.rem(j, NC) != c) | (tb != x))
                def _():
                    wait_block(token_rows(sel, j, tb), xr.at[sel, j, tb])

                return carry

            lax.fori_loop(0, ZH * NC * NY, wait_one, 0)

        columns = wall.shape[4]
        weights = wall[m].reshape(ZL * rows, columns)
        acc = None
        for j in range(ZH * NC):
            term = mm(xc[sel, j], weights[j * width : (j + 1) * width])
            acc = term if acc is None else acc + term
        for k in range(NY):
            pf[k, 0:HD] = acc[k * HD : (k + 1) * HD]
            pf[k, HD:] = acc[NY * HD :]
        pown[m] = pf[y]
        psend[m] = pf[...].astype(BF16)
        for i, (k, device) in enumerate(y_peers):
            remote(psend.at[m, k], precv.at[m, y], ps.at[m, i], pr.at[m, y], device).start()

    def phase(ph, middle):
        def hop(t, carry):
            from_low = p - t
            from_high = p + t
            for m in pairs[ph]:
                for h in range(NH):

                    @pl.when(from_low >= 0)
                    def _():
                        wait_block(wall.at[m, from_low, h], wr.at[m, from_low, h])
                        send_weight(0, m, from_low, h)

                    @pl.when(from_high < ZL)
                    def _():
                        wait_block(wall.at[m, from_high, h], wr.at[m, from_high, h])
                        send_weight(1, m, from_high, h)

            return carry

        cut = max(ZL - 2, 2)
        lax.fori_loop(1, cut, hop, 0)
        middle()
        lax.fori_loop(cut, ZL, hop, 0)

    def middle_first():
        send_own(1)
        send_tokens()

    def middle_second():
        multiply(3, 1, True)
        multiply(0, 0, True)

    phase(0, middle_first)
    phase(1, middle_second)
    multiply(1, 0, False)
    multiply(2, 0, False)

    def projected(m):
        value = pown[m]
        for i in range(1, NY):
            k = lax.rem(y + i, NY)
            wait_block(precv.at[m, k], pr.at[m, k])
            value = value + precv[m, k].astype(F32)
        return value

    grad_attn_all = projected(3)[0:HD].astype(BF16)
    whole = [projected(m) for m in range(3)]
    query_all, key_all = whole[0][0:HD], whole[1][0:HD]
    value_all = whole[2][0:HD].astype(BF16)
    score_scale = HD ** (-0.5)
    for h in range(wall.shape[4] // HD):
        cols = slice(h * HD, (h + 1) * HD)
        q_hat, q_inv = row_norm(query_all[:, cols])
        k_hat, k_inv = row_norm(key_all[:, cols])
        queries, key_rows = q_hat.astype(BF16), k_hat.astype(BF16)
        value_rows, grad_attn = value_all[:, cols], grad_attn_all[:, cols]
        exps = jnp.exp(mm_nt(queries, key_rows) * score_scale)
        probs = exps / jnp.sum(exps, axis=-1, keepdims=True)
        grad_values = mm_tn(probs.astype(BF16), grad_attn)
        grad_probs = mm_nt(grad_attn, value_rows)
        inner = jnp.sum(probs * grad_probs, axis=-1, keepdims=True)
        grad_scores = (probs * (grad_probs - inner) * score_scale).astype(BF16)
        grad_query = mm(grad_scores, key_rows)
        grad_keys = mm_tn(grad_scores, queries)
        grads = (
            row_norm_back(grad_query, q_hat, q_inv).astype(BF16),
            row_norm_back(grad_keys, k_hat, k_inv).astype(BF16),
            grad_values.astype(BF16),
        )
        for m in range(3):
            for r in range(NR):
                dbuf[r, y, m, :, cols] = grads[m][r * half : (r + 1) * half]
    for r in range(NR):
        for i, (_, device) in enumerate(y_peers):
            remote(dbuf.at[r, y], dbuf.at[r, y], ds_.at[r, i], dr.at[r, y], device).start()

    first_part, second_part = 0.0, 0.0
    for m in range(3):
        grad = jnp.concatenate([dbuf[r, y, m].astype(F32) for r in range(NR)], axis=0)
        first_part = first_part + grad * whole[m][HD : HD + 1]
        second_part = second_part + grad * whole[m][0:HD]
    fin[mp] = columns_to_rows(
        jnp.sum(first_part, axis=-1, keepdims=True), jnp.sum(second_part, axis=-1, keepdims=True)
    )[0:2]
    share(fin, mp, near_peers + [partner] + far_peers, st_s.at[3], st_r.at[3])

    goal = [1 - zh, zh]
    apart = width // rows

    def term_block(side, r, tb, wait):
        if wait:
            wait_block(dbuf.at[r, tb], dr.at[r, tb])
        for half_c in range(NC):
            j = goal[side] * NC + half_c
            acc = None
            for m in range(3):
                weights = wall[m, pl.ds(j * apart, apart)].reshape(width, wall.shape[4])
                term = mm_nt(dbuf[r, tb, m], weights)
                acc = term if acc is None else acc + term
            tbuf[half_c, side, r, tb] = acc.astype(BF16)
        remote(
            tbuf.at[1 - c, side, r, tb], tr.at[side, r, tb], tcs.at[side, r, tb], tcr.at[side, r, tb], other_core
        ).start()

    def add_cores(side, r, tb):
        wait_block(tr.at[side, r, tb], tcr.at[side, r, tb])
        sbuf[side, r, tb] = (tbuf[c, side, r, tb].astype(F32) + tr[side, r, tb].astype(F32)).astype(BF16)

        @pl.when(tb != x)
        def _():
            remote(
                sbuf.at[side, r, tb], sr.at[side, r, x], ss.at[side, r, tb], srs.at[side, r, x], dev(tb, y, zh, p, c)
            ).start()

    other_core = dev(x, y, zh, p, 1 - c)
    order = [0, 1, 3, 2] if NY == 4 else list(range(NY))

    def blocks(side, r):
        before = None
        for i in order[1:]:
            tb = at_y[i]
            term_block(side, r, tb, side == 0)
            if before is not None:
                add_cores(side, r, before)
            before = tb
        add_cores(side, r, before)

    own = [(side, r) for side in range(2) for r in range(NR)]
    for side, r in own:
        term_block(side, r, y, False)
    for side, r in own:
        add_cores(side, r, y)

    def gather_x(side, r):
        k = goal[side]
        value = sbuf[side, r, x].astype(F32)
        for i in range(1, NX):
            wait_block(sr.at[side, r, at_x[i]], srs.at[side, r, at_x[i]])
            value = value + sr[side, r, at_x[i]].astype(F32)
        ubuf[side, r] = value.astype(BF16)
        if side == 0:
            remote(ubuf.at[0, r], ur.at[r, zh], us.at[0, r], urs.at[r, zh], dev(y, x, k, p, c)).start()
        else:

            @pl.when(x == y)
            def _():
                pltpu.make_async_copy(ubuf.at[1, r], ur.at[r, zh], urs.at[r, zh]).start()

            @pl.when(x != y)
            def _():
                remote(ubuf.at[1, r], ur.at[r, zh], us.at[1, r], urs.at[r, zh], dev(y, x, k, p, c)).start()

    for r in range(NR):
        blocks(0, r)
    for r in range(NR):
        gather_x(0, r)
    for r in range(NR):
        blocks(1, r)
    for r in range(NR):
        gather_x(1, r)
    arrived(st_z, n_z, st_s.at[0])
    arrived(rs, n_mp, st_s.at[1])
    arrived(st_xyc, n_xyc, st_s.at[2])
    arrived(fin, n_mp, st_s.at[3])
    for k in range(ZH):
        here = (x == y) & (zh == k)

        @pl.when(jnp.logical_not(here))
        def _():
            wait_block(xraw.at[0], xs.at[k])

    @pl.when(x != y)
    def _():
        wait_block(mi.at[0], ms.at[1])

    def left_y(i, carry):
        for j in range(ZH * NC):
            wait_block(token_rows(1, j, 0), cs.at[i, j])
        for m in range(4):
            wait_block(psend.at[m, 0], ps.at[m, i])
        for r in range(NR):
            wait_block(dbuf.at[r, 0], ds_.at[r, i])
        return carry

    lax.fori_loop(0, NY - 1, left_y, 0)

    def left_near(i, carry):
        for k in range(ZH):
            wait_block(token_rows(0, 0, 0), n3s.at[k, i])
        return carry

    lax.fori_loop(0, NX * NC - 1, left_near, 0)

    @pl.when(x == y)
    def _():
        for i in range(n_mp - 1):
            wait_block(gx.at[0], gs.at[i])

    def left_blocks(tb, carry):
        for side in range(2):
            for r in range(NR):
                wait_block(tr.at[side, r, tb], tcs.at[side, r, tb])

        @pl.when(tb != x)
        def _():
            for side in range(2):
                for r in range(NR):
                    wait_block(sbuf.at[side, r, tb], ss.at[side, r, tb])

        return carry

    lax.fori_loop(0, NY, left_blocks, 0)

    def left_weights(i, carry):
        m, s = lax.div(i, ZL), lax.rem(i, ZL)
        for h in range(NH):

            @pl.when((p < ZL - 1) & (s <= p))
            def _():
                wait_block(wall.at[m, s, h], ws.at[0, m, s, h])

            @pl.when((p > 0) & (s >= p))
            def _():
                wait_block(wall.at[m, s, h], ws.at[1, m, s, h])

        return carry

    lax.fori_loop(0, 4 * ZL, left_weights, 0)

    arrived(fin, n_mp, st_r.at[3])
    sums = jnp.sum(fin[...], axis=0) * (1.0 / n_feat)
    first, second = rows_to_columns(sums[0:1], sums[1:2])
    for r in range(NR):
        part = slice(r * half, (r + 1) * half)
        share_sum = 0.0
        for k in range(ZH):
            wait_block(ur.at[r, k], urs.at[r, k])
            share_sum = share_sum + ur[r, k].astype(F32)
        upstream = share_sum * gain[...].astype(F32).reshape(1, -1)
        out[part] = ((upstream - first[part] - normed[part] * second[part]) * invc[part, 0:1]).astype(BF16)

    for side in range(2):
        for r in range(NR):

            @pl.when((side == 0) | (x != y))
            def _():
                wait_block(ubuf.at[side, r], us.at[side, r])


def per_device(tokens, norm_gain, attn_weights, stored_grads, cotangent):
    width = tokens.shape[1]
    _, rows, columns = attn_weights.shape
    n_mp = NX * ZH * NC
    nj = ZH * NC
    dma = pltpu.SemaphoreType.DMA
    vmem = pl.BlockSpec(memory_space=pltpu.VMEM)
    return pl.pallas_call(
        kernel,
        out_shape=jax.ShapeDtypeStruct((HD, width), BF16),
        in_specs=[pl.BlockSpec(memory_space=pltpu.HBM)] * 5,
        out_specs=vmem,
        scratch_shapes=[
            pltpu.VMEM(tokens.shape, BF16),
            pltpu.VMEM((width,), BF16),
            pltpu.VMEM(attn_weights.shape, BF16),
            pltpu.VMEM(attn_weights.shape, BF16),
            pltpu.VMEM((ZH * ZL, 1, HD), F32),
            pltpu.VMEM((NX * NY * NC, 1, HD), F32),
            pltpu.VMEM((n_mp, 2, HD), F32),
            pltpu.VMEM((ZH * NC + 1, 1, width), F32),
            pltpu.VMEM((n_mp, 2, HD), F32),
            pltpu.VMEM((2, 2, HD), F32),
            pltpu.VMEM((ZH, HD, width), BF16),
            pltpu.VMEM((HD, width), F32),
            pltpu.VMEM((HD, HD), F32),
            pltpu.VMEM((2, nj, NY * HD + EXTRA, width), BF16),
            pltpu.VMEM((4, ZL, NH, rows // NH, columns), BF16),
            pltpu.VMEM((NY, HD + EXTRA, columns), F32),
            pltpu.VMEM((4, HD + EXTRA, columns), F32),
            pltpu.VMEM((4, NY, HD + EXTRA, columns), BF16),
            pltpu.VMEM((4, NY, HD + EXTRA, columns), BF16),
            pltpu.VMEM((NR, NY, 3, HD // NR, columns), BF16),
            pltpu.VMEM((NC, 2, NR, NY, HD // NR, width), BF16),
            pltpu.VMEM((2, NR, NY, HD // NR, width), BF16),
            pltpu.VMEM((2, NR, NY, HD // NR, width), BF16),
            pltpu.VMEM((2, NR, NX, HD // NR, width), BF16),
            pltpu.VMEM((2, NR, HD // NR, width), BF16),
            pltpu.VMEM((NR, ZH, HD // NR, width), BF16),
            dma((4,)),
            dma((4,)),
            dma((4,)),
            dma((n_mp - 1,)),
            dma((1,)),
            dma((2,)),
            dma((ZH,)),
            dma((ZH,)),
            dma((2, nj, NY)),
            dma((NY, nj)),
            dma((ZH, NX * NC)),
            dma((2, 4, ZL, NH)),
            dma((4, ZL, NH)),
            dma((4, NY)),
            dma((4, NY)),
            dma((NR, NY)),
            dma((NR, NY)),
            dma((2, NR, NY)),
            dma((2, NR, NY)),
            dma((2, NR, NY)),
            dma((2, NR, NX)),
            dma((2, NR)),
            dma((NR, ZH)),
        ],
        compiler_params=pltpu.CompilerParams(
            collective_id=0, has_side_effects=True, vmem_limit_bytes=60 * 1024 * 1024
        ),
    )(tokens, norm_gain, attn_weights, stored_grads, cotangent)


def solution(mesh):
    return jax.shard_map(
        per_device,
        mesh=mesh,
        in_specs=(P("dp", "mp"), P("mp"), P(None, "dp", "mp"), P(None, "dp", "mp"), P("dp", None)),
        out_specs=P("dp", "mp"),
        check_vma=False,
    )
```
